128 devices in a mesh: dp: 32 (over x, z, core), row: 2 (over y_lo), col: 2 (over y_hi).
Axes of the slice: x: 4, y: 4 (y_hi: 2, y_lo: 2; y = y_hi * 2 + y_lo), z: 4, core: 2. Of those that a mesh axis runs over, the one named last changes fastest.
Arguments:
- activations: bfloat16 [16384, 768], P(('dp', 'row'), 'col'), may hold values from -6 to 6
- timesteps: int32 [64], P(('dp', 'col')), may hold values from 0 to 999
- class_labels: int32 [64], P(('dp', 'col')), may hold values from 0 to 1000
- time_table: bfloat16 [1000, 768], P(None, 'row'), may hold values from -4 to 4
- class_table: bfloat16 [1001, 768], P(None, 'row'), may hold values from -4 to 4
- modulation: bfloat16 [768, 6, 768], P('row', None, 'col'), may hold values from -0.21875 to 0.21875
- modulation_bias: bfloat16 [6, 768], P(None, 'col'), may hold values from -3 to 3
- attention: bfloat16 [768, 3, 768], P('col', None, 'row'), may hold values from -0.21875 to 0.21875
- attention_bias: bfloat16 [2, 768], P(None, 'row'), may hold values from -2 to 2
- projection: bfloat16 [768, 768], P('row', 'col'), may hold values from -0.875 to 0.875
- projection_bias: bfloat16 [768], P('col'), may hold values from -2 to 2
- expansion: bfloat16 [768, 3072], P('col', 'row'), may hold values from -0.21875 to 0.21875
- widening_bias: bfloat16 [3072], P('row'), may hold values from -2 to 2
- reduction: bfloat16 [3072, 768], P('row', 'col'), may hold values from -0.109375 to 0.109375
- narrowing_bias: bfloat16 [768], P('col'), may hold values from -2 to 2
- cotangent: bfloat16 [16384, 768], P(('dp', 'row'), 'col'), may hold values from -6 to 6
Outputs:
- result: bfloat16 [16384, 768], P(('dp', 'row'), 'col')
- activations_grad: float32 [16384, 768], P(('dp', 'row'), 'col')
- time_grad: float32 [1000, 768], P(None, 'row')
- class_grad: float32 [1001, 768], P(None, 'row')
- modulation_grad: float32 [768, 6, 768], P('row', None, 'col')
- modulation_bias_grad: float32 [6, 768], P(None, 'col')
- attention_grad: float32 [768, 3, 768], P('col', None, 'row')
- attention_bias_grad: float32 [2, 768], P(None, 'row')
- projection_grad: float32 [768, 768], P('row', 'col')
- projection_bias_grad: float32 [768], P('col')
- expansion_grad: float32 [768, 3072], P('col', 'row')
- expansion_bias_grad: float32 [3072], P('row')
- reduction_grad: float32 [3072, 768], P('row', 'col')
- reduction_bias_grad: float32 [768], P('col')
The draws below stay inside these ranges and needn't reach their ends.
Inputs may be any that keep to these rules, and one draw needn't show every extreme that they name: `timesteps`: row of time_table used by each latent. `class_labels`: row of class_table used by each latent.
All inputs are finite; a program needn't handle non-finite values.
Results may differ from the reference program's by a relative error of at most 0.02.
Values may be sent and summed in bfloat16 or wider, within the bound.
A program may use at most 128 MiB of HBM per device.

```python
import math
import jax
import jax.numpy as jnp
from jax import lax

D = 768
HEADS = 12
HEAD_DIM = 64
FF = 3072
STEPS = 1000
CLASSES = 1001
SEQ = 256
LATENTS = 64
TOKENS = 16384


def set_ends(entries, key, least, largest):
    dims = entries.shape
    index_at = [jax.random.randint(jax.random.fold_in(key, axis), (), 0, dims[axis]) for axis in range(len(dims))]
    entries = entries.at[tuple(index_at)].set(least)
    longest = dims.index(max(dims))
    index_at[longest] = (index_at[longest] + 1) % dims[longest]
    return entries.at[tuple(index_at)].set(largest)


def levels(rng, extent, pieces, smallest, largest):
    factor_of = 1.0
    for dim, parts in pieces:
        draws = jax.random.uniform(jax.random.fold_in(jax.random.fold_in(rng, 6), dim), (parts,), jnp.float32, smallest / len(pieces), largest / len(pieces))
        factor_of = factor_of * jnp.repeat(jnp.exp(draws), extent[dim] // parts).reshape((-1,) + (1,) * (len(extent) - 1 - dim))
    return factor_of


def centred(key, dims, scale, bound, pieces=(), kind=jnp.bfloat16):
    drawn = jax.random.normal(key, dims, jnp.float32) * scale
    if len(pieces) > 0:
        drawn = levels(key, dims, pieces, -0.22, 0.18) * drawn
    return jnp.clip(drawn, min=-bound, max=bound).astype(kind)


def setup_inputs(seed: int = 0) -> dict:
    arg_keys = jax.random.split(jax.random.key(seed), 17)
    return {
        "activations": centred(arg_keys[0], (TOKENS, D), 1.0, 6.0, ((0, 64), (1, 2))),
        "timesteps": set_ends(jax.random.randint(arg_keys[1], (LATENTS,), 0, STEPS), jax.random.fold_in(arg_keys[1], 1), 0, STEPS - 1).astype(jnp.int32),
        "class_labels": set_ends(jax.random.randint(arg_keys[2], (LATENTS,), 0, CLASSES), jax.random.fold_in(arg_keys[2], 1), 0, CLASSES - 1).astype(jnp.int32),
        "time_table": centred(arg_keys[3], (STEPS, D), 0.7, 4.0, ((1, 2),)),
        "class_table": centred(arg_keys[4], (CLASSES, D), 0.7, 4.0, ((1, 2),)),
        "modulation": centred(arg_keys[5], (D, 6, D), D ** -0.5, 0.21875, ((0, 2), (2, 2))),
        "modulation_bias": centred(arg_keys[6], (6, D), 0.4, 3.0, ((1, 2),)),
        "attention": centred(arg_keys[7], (D, 3, D), D ** -0.5, 0.21875, ((0, 2), (2, 2))),
        "attention_bias": centred(arg_keys[8], (2, D), 0.3, 2.0, ((1, 2),)),
        "projection": centred(arg_keys[9], (D, D), (D // 16) ** -0.5, 0.875, ((0, 2), (1, 2))),
        "projection_bias": centred(arg_keys[10], (D,), 0.3, 2.0, ((0, 2),)),
        "expansion": centred(arg_keys[11], (D, FF), D ** -0.5, 0.21875, ((0, 2), (1, 2))),
        "widening_bias": centred(arg_keys[12], (FF,), 0.3, 2.0, ((0, 2),)),
        "reduction": centred(arg_keys[13], (FF, D), FF ** -0.5, 0.109375, ((0, 2), (1, 2))),
        "narrowing_bias": centred(arg_keys[14], (D,), 0.3, 2.0, ((0, 2),)),
        "cotangent": centred(arg_keys[15], (TOKENS, D), 1.0, 6.0, ((0, 64), (1, 2))),
    }


exact_precision_flag = lax.Precision.HIGHEST

@jax.custom_vjp
def low(v):
    return lax.optimization_barrier(v.astype(jnp.bfloat16)).astype(jnp.float32)

@jax.custom_vjp
def reduced_precision_backward(v):
    return v

def low_keep(v):
    return (low(v), None)

def low_pass(kept, grad):
    return (grad,)

def back_keep(v):
    return (v, None)

def back_low(kept, grad):
    return (low(grad),)
low.defvjp(low_keep, low_pass)
reduced_precision_backward.defvjp(back_keep, back_low)

def layer_norm(values):
    average = lax.optimization_barrier(jnp.mean(values, axis=-1, keepdims=True))
    square = lax.optimization_barrier(jnp.mean(values * values, axis=-1, keepdims=True))
    return (values - average) * lax.rsqrt(square - average * average + 1e-06)

@jax.checkpoint
def attend(query_heads, key_heads, value_heads):
    score_scale = HEAD_DIM ** (-0.5)
    scores = reduced_precision_backward(jnp.einsum('lqhd,lkhd->lhqk', query_heads, key_heads, precision=exact_precision_flag) * score_scale)
    highest = lax.optimization_barrier(jnp.max(scores, axis=-1, keepdims=True))
    exponent = jnp.exp(scores - highest)
    softmax_weights = exponent / lax.optimization_barrier(jnp.sum(exponent, axis=-1, keepdims=True))
    mixture = jnp.einsum('lhqk,lkhd->lqhd', low(softmax_weights), value_heads, precision=exact_precision_flag)
    return mixture.reshape(mixture.shape[0], SEQ, HEADS * HEAD_DIM)

def block_forward(inputs, step_index, label_index, time_table, class_table, modulation, modulation_bias, attention, attention_bias, projection, projection_bias, expansion, widening_bias, reduction, narrowing_bias):
    condition = jnp.take(time_table, step_index, axis=0) + jnp.take(class_table, label_index, axis=0)
    silu_cond = low(jax.nn.silu(condition))
    modvals = reduced_precision_backward(jnp.einsum('ld,dke->lke', silu_cond, modulation, precision=exact_precision_flag) + modulation_bias)
    shift_first = modvals[:, 0][:, None, :]
    scale_first = modvals[:, 1][:, None, :]
    gate_first = modvals[:, 2][:, None, :]
    shift_second = modvals[:, 3][:, None, :]
    scale_second = modvals[:, 4][:, None, :]
    gate_second = modvals[:, 5][:, None, :]
    hidden_first = low(layer_norm(inputs) * (1.0 + scale_first) + shift_first)
    triple_bias = jnp.stack([attention_bias[0], jnp.zeros_like(attention_bias[0]), attention_bias[1]])
    triple = reduced_precision_backward(jnp.einsum('lsd,dke->lske', hidden_first, attention, precision=exact_precision_flag) + triple_bias)
    latents = inputs.shape[0]
    query_heads = low(triple[:, :, 0]).reshape(latents, SEQ, HEADS, HEAD_DIM)
    key_heads = low(triple[:, :, 1]).reshape(latents, SEQ, HEADS, HEAD_DIM)
    value_heads = low(triple[:, :, 2]).reshape(latents, SEQ, HEADS, HEAD_DIM)
    attended = reduced_precision_backward(low(attend(query_heads, key_heads, value_heads)))
    branch_first = reduced_precision_backward(jnp.einsum('lsd,de->lse', attended, projection, precision=exact_precision_flag) + projection_bias)
    residual_mid = inputs + gate_first * branch_first
    hidden_after_feedforward = low(layer_norm(residual_mid) * (1.0 + scale_second) + shift_second)
    expanded_hidden_rows = reduced_precision_backward(jnp.einsum('ikn,nb->ikb', hidden_after_feedforward, expansion, precision=exact_precision_flag) + widening_bias)
    gelu_activated_rows = low(jax.nn.gelu(expanded_hidden_rows, approximate=True))
    feedforward_branch_output = reduced_precision_backward(jnp.einsum('mxk,ki->mxi', gelu_activated_rows, reduction, precision=exact_precision_flag) + narrowing_bias)
    return residual_mid + gate_second * feedforward_branch_output

def reference(activations, timesteps, class_labels, time_table, class_table, modulation, modulation_bias, attention, attention_bias, projection, projection_bias, expansion, widening_bias, reduction, narrowing_bias, cotangent):
    latents = timesteps.shape[0]
    block_size = math.gcd(latents, 16)
    block_count = latents // block_size
    inputs = activations.astype(jnp.float32).reshape(block_count, block_size, SEQ, D)
    step_index = timesteps.astype(jnp.int32).reshape(block_count, block_size)
    label_index = class_labels.astype(jnp.int32).reshape(block_count, block_size)
    params = tuple((weight.astype(jnp.float32) for weight in (time_table, class_table, modulation, modulation_bias, attention, attention_bias, projection, projection_bias, expansion, widening_bias, reduction, narrowing_bias)))

    def forward(block_inputs, *weights):

        def per_block(packed):
            return jax.checkpoint(block_forward)(packed[0], packed[1], packed[2], *weights)
        return lax.map(per_block, (block_inputs, step_index, label_index))
    finished, pullback = jax.vjp(forward, inputs, *params)
    gradients = pullback(cotangent.astype(jnp.float32).reshape(finished.shape))
    result = finished.reshape(latents * SEQ, D).astype(jnp.bfloat16)
    return (result, gradients[0].reshape(latents * SEQ, D), gradients[1], gradients[2], gradients[3], gradients[4], gradients[5], gradients[6], gradients[7], gradients[8], gradients[9], gradients[10], gradients[11], gradients[12])
```

```python
import math

import jax
import jax.numpy as jnp
from jax import lax
from jax.experimental import pallas as pl
from jax.experimental.pallas import tpu as pltpu
from jax.sharding import PartitionSpec as P

D = 768
HALF = 384
SEQ = 256
HEAD_DIM = 64
STEPS = 1000
CLASSES = 1001
SEG = 1536
EPSILON = 1e-06
ROWS = 32
SEMS = 128
F32 = jnp.float32
BF16 = jnp.bfloat16
MESH = pl.DeviceIdType.MESH


def dot(u, v):
    return lax.dot_general(u, v, (((1,), (0,)), ((), ())), preferred_element_type=F32)


def dot_nt(u, v):
    return lax.dot_general(u, v, (((1,), (1,)), ((), ())), preferred_element_type=F32)


def dot_tn(u, v):
    return lax.dot_general(u, v, (((0,), (0,)), ((), ())), preferred_element_type=F32)


def xor(u, v):
    return u + v - 2 * u * v


class Place:
    def __init__(self, n):
        self.n = n
        self.dp = lax.axis_index("dp")
        self.r = lax.axis_index("row")
        self.c = lax.axis_index("col")
        self.k = lax.rem(self.dp, 2)
        chip = lax.div(self.dp, 2)
        z = lax.rem(chip, n)
        x = lax.div(chip, n)
        self.major = x * (1 - self.k) + z * self.k
        self.minor = z * (1 - self.k) + x * self.k
        self.shard = (self.k * n + self.major) * n + self.minor
        self.latent = xor(self.c, self.k * self.r)

    def at(self, dp=None, row=None, col=None):
        return {
            "dp": self.dp if dp is None else dp,
            "row": self.r if row is None else row,
            "col": self.c if col is None else col,
        }

    def plane(self, major, minor):
        x = major * (1 - self.k) + minor * self.k
        z = minor * (1 - self.k) + major * self.k
        return self.at(dp=(x * self.n + z) * 2 + self.k)

    def along_minor(self, step):
        return self.plane(self.major, lax.rem(self.minor + step, self.n))

    def along_major(self, step):
        return self.plane(lax.rem(self.major + step, self.n), self.minor)

    def sibling(self):
        return self.at(dp=self.dp + 1 - 2 * self.k)

    def group(self, step):
        row = xor(self.r, step & 1)
        col = xor(self.c, step >> 1)
        return self.at(row=row, col=col)

    def partner(self):
        return self.at(row=1 - self.r, col=xor(self.c, self.k))

    def column(self):
        return self.at(col=1 - self.c)


class Wires:
    def __init__(self, send_sems, recv_sems):
        self.send_sems, self.recv_sems = send_sems, recv_sems
        self.used = 0
        self.sent = []

    def slot(self):
        self.used += 1
        assert self.used <= SEMS
        return self.used - 1

    def copy(self, slot, src, dst, device):
        return pltpu.make_async_remote_copy(
            src_ref=src,
            dst_ref=dst,
            send_sem=self.send_sems.at[slot],
            recv_sem=self.recv_sems.at[slot],
            device_id=device,
            device_id_type=MESH,
        )

    def send(self, slot, src, dst, device):
        copy = self.copy(slot, src, dst, device)
        copy.start()
        self.sent.append(copy)

    def arrived(self, slot, dst, device):
        self.copy(slot, dst, dst, device).wait_recv()

    def drain(self):
        for copy in self.sent:
            copy.wait_send()


class Gather:
    def __init__(self, place, wires, view):
        self.place, self.wires, self.view = place, wires, view
        self.slots = [wires.slot() for _ in range(2 * (place.n - 1) + 1)]

    def minor(self):
        p, w, n = self.place, self.wires, self.place.n
        mine = self.view(p.shard, 1)
        for step in range(1, n):
            w.send(self.slots[step - 1], mine, mine, p.along_minor(step))

    def major(self):
        p, w, n = self.place, self.wires, self.place.n
        row = (p.k * n + p.major) * n
        for step in range(1, n):
            other = lax.rem(p.minor + n - step, n)
            w.arrived(self.slots[step - 1], self.view(row + other, 1), p.along_minor(step))
        mine = self.view(row, n)
        for step in range(1, n):
            w.send(self.slots[n - 2 + step], mine, mine, p.along_major(step))

    def cores(self):
        p, w, n = self.place, self.wires, self.place.n
        for step in range(1, n):
            other = lax.rem(p.major + n - step, n)
            block = self.view((p.k * n + other) * n, n)
            w.arrived(self.slots[n - 2 + step], block, p.along_major(step))
        mine = self.view(p.k * n * n, n * n)
        w.send(self.slots[-1], mine, mine, p.sibling())

    def finish(self):
        p, w, n = self.place, self.wires, self.place.n
        w.arrived(self.slots[-1], self.view((1 - p.k) * n * n, n * n), p.sibling())


class Reduce:
    def __init__(self, place, wires, seg, grads, from_core, from_major, from_minor, from_col, final):
        self.place, self.wires, self.seg = place, wires, seg
        self.grads, self.final = grads, final
        self.from_core, self.from_major = from_core, from_major
        self.from_minor, self.from_col = from_minor, from_col
        n = place.n
        self.rows = SEG // (2 * n * n)
        self.slots = [wires.slot() for _ in range(2 * n)]
        self.gather = Gather(place, wires, self.final_view)

    def view(self, first, count):
        start = pl.multiple_of(first * self.rows, 16)
        return self.grads.at[self.seg, :, pl.ds(start, count * self.rows)]

    def final_view(self, first, count):
        start = pl.multiple_of(first * self.rows, 16)
        return self.final.at[self.seg, pl.ds(start, count * self.rows)]

    def add(self, first, count, arrivals):
        chunk = 48
        base = first * self.rows

        def step(i, carry):
            at = pl.ds(pl.multiple_of(base + i * chunk, 16), chunk)
            here = pl.ds(pl.multiple_of(i * chunk, 16), chunk)
            total = self.grads[self.seg, :, at].astype(F32)
            for ref in arrivals:
                total = total + ref[:, here].astype(F32)
            self.grads[self.seg, :, at] = total.astype(BF16)
            return carry

        lax.fori_loop(0, count * self.rows // chunk, step, 0)

    def to_core(self):
        p, n = self.place, self.place.n
        self.wires.send(
            self.slots[0],
            self.view((1 - p.k) * n * n, n * n),
            self.from_core.at[self.seg],
            p.sibling(),
        )

    def to_major(self):
        p, w, n = self.place, self.wires, self.place.n
        w.arrived(self.slots[0], self.from_core.at[self.seg], p.sibling())
        self.add(p.k * n * n, n * n, [self.from_core.at[self.seg]])
        for step in range(1, n):
            other = lax.rem(p.major + step, n)
            w.send(
                self.slots[step],
                self.view((p.k * n + other) * n, n),
                self.from_major.at[self.seg, step - 1],
                p.along_major(step),
            )

    def to_minor(self):
        p, w, n = self.place, self.wires, self.place.n
        for step in range(1, n):
            w.arrived(self.slots[step], self.from_major.at[self.seg, step - 1], p.along_major(step))
        row = (p.k * n + p.major) * n
        if n > 1:
            self.add(row, n, [self.from_major.at[self.seg, step - 1] for step in range(1, n)])
        for step in range(1, n):
            other = lax.rem(p.minor + step, n)
            w.send(
                self.slots[n - 1 + step],
                self.view(row + other, 1),
                self.from_minor.at[self.seg, step - 1],
                p.along_minor(step),
            )

    def to_col(self):
        p, w, n = self.place, self.wires, self.place.n
        for step in range(1, n):
            w.arrived(
                self.slots[n - 1 + step], self.from_minor.at[self.seg, step - 1], p.along_minor(step)
            )
        if n > 1:
            self.add(p.shard, 1, [self.from_minor.at[self.seg, step - 1] for step in range(1, n)])
        start = pl.multiple_of(p.shard * self.rows, 16)
        w.send(
            self.slots[-1],
            self.grads.at[self.seg, 1 - p.c, pl.ds(start, self.rows)],
            self.from_col.at[self.seg],
            p.column(),
        )

    def to_gather(self):
        p, w = self.place, self.wires
        w.arrived(self.slots[-1], self.from_col.at[self.seg], p.column())
        start = pl.multiple_of(p.shard * self.rows, 16)
        mine = self.grads[self.seg, p.c, pl.ds(start, self.rows)].astype(F32)
        total = mine + self.from_col[self.seg].astype(F32)
        self.final[self.seg, pl.ds(start, self.rows)] = total.astype(BF16)
        self.gather.minor()


def kernel(
    n,
    x_ref,
    cot_ref,
    modp_ref,
    weights_hbm,
    triple_bias_ref,
    widening_ref,
    result_ref,
    xgrad_ref,
    final_hbm,
    payload_hbm,
    weights,
    x_all,
    cot_all,
    mod_parts,
    mod,
    normed1,
    rstd1,
    hidden1,
    triple,
    probs,
    attended,
    send1,
    recv1,
    branch1,
    normed2,
    rstd2,
    hidden2,
    activated,
    slope,
    grad_b2,
    send2,
    recv2,
    grad_up,
    send3,
    recv3,
    grad_res,
    grad_b1,
    grad_att,
    grad_tri,
    send4,
    recv4,
    res_out,
    res_in,
    xg_out,
    xg_in,
    payload_out,
    payload,
    grads,
    from_core,
    from_major,
    from_minor,
    from_col,
    final,
    send_sems,
    recv_sems,
    local_sems,
):
    place = Place(n)
    wires = Wires(send_sems, recv_sems)
    r, c, k, latent = place.r, place.c, place.k, place.latent

    barrier = pltpu.get_barrier_semaphore()
    others = [place.group(s) for s in (1, 2, 3)] + [place.sibling()]
    for step in range(1, n):
        others += [place.along_minor(step), place.along_major(step)]
    for other in others:
        pl.semaphore_signal(barrier, inc=1, device_id=other, device_id_type=MESH)
    pl.semaphore_wait(barrier, len(others))

    shard_rows = SEG // (2 * n * n)

    def weight_view(seg):
        def view(first, count):
            start = pl.multiple_of(first * shard_rows, 16)
            return weights.at[seg, 1 - c, pl.ds(start, count * shard_rows)]

        return view

    gathers = [Gather(place, wires, weight_view(seg)) for seg in range(3)]
    weight_slots = [wires.slot() for _ in range(3)]
    my_rows = pl.ds(pl.multiple_of(place.shard * shard_rows, 16), shard_rows)

    def weights_out(seg):
        wires.send(
            weight_slots[seg],
            weights_hbm.at[seg, my_rows],
            weights.at[seg, c, my_rows],
            place.column(),
        )

    def weights_minor(seg):
        wires.arrived(weight_slots[seg], weights.at[seg, 1 - c, my_rows], place.column())
        gathers[seg].minor()

    own = [
        pltpu.make_async_copy(weights_hbm.at[seg], weights.at[seg, c], local_sems.at[seg])
        for seg in range(3)
    ]

    weights_out(0)
    own[0].start()
    own[1].start()
    own[2].start()
    mod_slots = [wires.slot() for _ in range(3)]
    for step in (1, 2, 3):
        there = place.group(step)
        its_latent = xor(there["col"], k * there["row"])
        wires.send(
            mod_slots[step - 1], modp_ref.at[its_latent], mod_parts.at[step], there
        )
    _, x_collect, x_sent = spread_halves(place, wires, x_ref, x_all)
    weights_out(1)
    weights_out(2)
    _, cot_collect, cot_sent = spread_halves(place, wires, cot_ref, cot_all)
    weights_minor(0)

    for step in (1, 2, 3):
        wires.arrived(mod_slots[step - 1], mod_parts.at[step], place.group(step))
    mod[c] = modp_ref[latent] + mod_parts[1]
    mod[1 - c] = mod_parts[2] + mod_parts[3]

    def vec(half, row):
        return mod[half, row : row + 1, :]

    def over_rows(body, init=0):
        def step(i, carry):
            return body(pl.ds(pl.multiple_of(i * ROWS, ROWS), ROWS), carry)

        return lax.fori_loop(0, SEQ // ROWS, step, init)

    def norm(values):
        average = (
            jnp.sum(values[0], axis=-1, keepdims=True) + jnp.sum(values[1], axis=-1, keepdims=True)
        ) * (1.0 / D)
        square = (
            jnp.sum(values[0] * values[0], axis=-1, keepdims=True)
            + jnp.sum(values[1] * values[1], axis=-1, keepdims=True)
        ) * (1.0 / D)
        inverse = lax.rsqrt(square - average * average + EPSILON)
        return [(v - average) * inverse for v in values], inverse

    def norm_back(grad, normed, inverse):
        average = (
            jnp.sum(grad[0], axis=-1, keepdims=True) + jnp.sum(grad[1], axis=-1, keepdims=True)
        ) * (1.0 / D)
        crossed = (
            jnp.sum(grad[0] * normed[0], axis=-1, keepdims=True)
            + jnp.sum(grad[1] * normed[1], axis=-1, keepdims=True)
        ) * (1.0 / D)
        return [inverse * (g - average - m * crossed) for g, m in zip(grad, normed)]

    def token_sum(v):
        return jnp.sum(v, axis=0, keepdims=True)

    x_collect()
    gathers[0].major()

    def first_norm(rows, carry):
        normed, inverse = norm([x_all[h, rows].astype(F32) for h in range(2)])
        rstd1[rows] = inverse
        for h in range(2):
            normed1[h, rows] = normed[h]
            hidden1[h, rows] = (normed[h] * (1.0 + vec(h, 1)) + vec(h, 0)).astype(BF16)
        return carry

    over_rows(first_norm)
    gathers[0].cores()
    weights_minor(1)
    weights_minor(2)
    own[0].wait()
    gathers[0].finish()

    def weight(seg, half, block):
        return weights[seg, half, block * HALF : (block + 1) * HALF, :]

    for kind in range(3):
        value = dot(hidden1[0], weight(0, 0, kind)) + dot(hidden1[1], weight(0, 1, kind))
        triple[kind] = (value + triple_bias_ref[kind]).astype(BF16)
    gathers[1].major()

    low_lanes = lax.broadcasted_iota(jnp.int32, (SEQ, 128), 1) < HEAD_DIM

    def one_head(v, head):
        mask = low_lanes if head == 0 else jnp.logical_not(low_lanes)
        return jnp.where(mask, v, jnp.zeros_like(v))

    score_scale = HEAD_DIM ** (-0.5)

    def attend(pair, carry):
        lanes = pl.ds(pl.multiple_of(pair * 128, 128), 128)
        query = triple[0, :, lanes] * BF16(score_scale)
        keys = triple[1, :, lanes]
        values = triple[2, :, lanes]
        mixed = []
        for head in range(2):
            scores = dot_nt(one_head(query, head), keys)
            exponent = jnp.exp(scores - jnp.max(scores, axis=-1, keepdims=True))
            total = jnp.sum(exponent, axis=-1, keepdims=True)
            weights_now = exponent * (1.0 / total)
            probs[2 * pair + head] = weights_now
            mixed.append(dot(weights_now.astype(BF16), values))
        attended[:, lanes] = jnp.where(low_lanes, mixed[0], mixed[1]).astype(BF16)
        return carry

    lax.fori_loop(0, 3, attend, 0)
    gathers[1].cores()
    gathers[2].major()

    def exchange(half, value, out, landing, slots):
        out[half] = value.astype(BF16)
        wires.send(slots[half], out.at[half], landing.at[half], place.partner())

    def exchanged(landing, slots):
        for half in range(2):
            wires.arrived(slots[half], landing.at[half], place.partner())

    slots1, slots2, slots3, slots4 = ([wires.slot() for _ in range(2)] for _ in range(4))
    for half in range(2):
        exchange(half, dot(attended[...], weight(0, half, 3)), send1, recv1, slots1)
    cot_collect()
    zero = jnp.zeros((1, HALF), F32)

    def start_back(rows, carry):
        out = []
        for h in range(2):
            low = (cot_all[h, rows].astype(F32) * vec(h, 5)).astype(BF16)
            grad_b2[h, rows] = low
            out.append(carry[h] + token_sum(low.astype(F32)))
        return tuple(out)

    narrowing_sum = over_rows(start_back, (zero, zero))
    gathers[2].cores()
    exchanged(recv1, slots1)

    def second_norm(rows, carry):
        middle = []
        for h in range(2):
            branch = send1[h, rows].astype(F32) + recv1[h, rows].astype(F32) + vec(h, 6)
            branch1[h, rows] = branch
            middle.append(x_all[h, rows].astype(F32) + vec(h, 2) * branch)
        normed, inverse = norm(middle)
        rstd2[rows] = inverse
        for h in range(2):
            normed2[h, rows] = normed[h]
            hidden2[h, rows] = (normed[h] * (1.0 + vec(h, 4)) + vec(h, 3)).astype(BF16)
        return carry

    over_rows(second_norm)
    own[1].wait()
    gathers[1].finish()
    root = math.sqrt(2.0 / math.pi)
    for block in range(4):
        upper = dot(hidden2[0], weight(1, 0, block)) + dot(hidden2[1], weight(1, 1, block))
        upper = upper + widening_ref[block]
        squared = upper * upper
        bent = jnp.tanh(root * upper * (1.0 + 0.044715 * squared))
        half_up = 0.5 * (1.0 + bent)
        activated[block] = (upper * half_up).astype(BF16)
        slope[block] = half_up + (0.5 * root) * upper * (1.0 - bent * bent) * (
            1.0 + (3.0 * 0.044715) * squared
        )
    own[2].wait()
    gathers[2].finish()
    widening_sum = []
    for block in range(4):
        back = dot_nt(grad_b2[0], weight(2, 0, block)) + dot_nt(grad_b2[1], weight(2, 1, block))
        low = (back * slope[block]).astype(BF16)
        grad_up[block] = low
        widening_sum.append(token_sum(low.astype(F32)))
    for half in range(2):
        value = dot_nt(grad_up[0], weight(1, half, 0))
        for block in range(1, 4):
            value = value + dot_nt(grad_up[block], weight(1, half, block))
        exchange(half, value, send3, recv3, slots3)
    for half in range(2):
        value = dot(activated[0], weight(2, half, 0))
        for block in range(1, 4):
            value = value + dot(activated[block], weight(2, half, block))
        exchange(half, value, send2, recv2, slots2)

    reduces = [
        Reduce(place, wires, seg, grads, from_core, from_major, from_minor, from_col, final)
        for seg in range(3)
    ]

    def keep_grad(seg, half, block, value):
        grads[seg, half, block * HALF : (block + 1) * HALF, :] = value.astype(BF16)

    for block in range(4):
        for half in range(2):
            keep_grad(2, half, block, dot_tn(activated[block], grad_b2[half]))
    reduces[2].to_core()
    for block in range(4):
        for half in range(2):
            keep_grad(1, half, block, dot_tn(hidden2[half], grad_up[block]))
    reduces[1].to_core()

    exchanged(recv3, slots3)

    def second_back(rows, carry):
        shift, scale, gate, bias = (list(part) for part in carry)
        inverse = rstd2[rows]
        normed = [normed2[h, rows] for h in range(2)]
        scaled = []
        for h in range(2):
            grad = send3[h, rows].astype(F32) + recv3[h, rows].astype(F32)
            shift[h] = shift[h] + token_sum(grad)
            scale[h] = scale[h] + token_sum(grad * normed[h])
            scaled.append(grad * (1.0 + vec(h, 4)))
        back = norm_back(scaled, normed, inverse)
        for h in range(2):
            total = cot_all[h, rows].astype(F32) + back[h]
            grad_res[h, rows] = total
            gate[h] = gate[h] + token_sum(total * branch1[h, rows])
            low = (total * vec(h, 2)).astype(BF16)
            grad_b1[h, rows] = low
            bias[h] = bias[h] + token_sum(low.astype(F32))
        return tuple(shift), tuple(scale), tuple(gate), tuple(bias)

    pair_zero = (zero, zero)
    shift2, scale2, gate1, projection_sum = over_rows(second_back, (pair_zero,) * 4)
    grad_att[...] = (
        dot_nt(grad_b1[0], weight(0, 0, 3)) + dot_nt(grad_b1[1], weight(0, 1, 3))
    ).astype(BF16)
    reduces[2].to_major()
    for half in range(2):
        keep_grad(0, half, 3, dot_tn(attended[...], grad_b1[half]))

    def attend_back(pair, carry):
        lanes = pl.ds(pl.multiple_of(pair * 128, 128), 128)
        query = triple[0, :, lanes] * BF16(score_scale)
        keys = triple[1, :, lanes]
        values = triple[2, :, lanes]
        above = grad_att[:, lanes]
        by_query, by_keys, by_values = [], [], []
        for head in range(2):
            weights_now = probs[2 * pair + head]
            grad_probs = dot_nt(one_head(above, head), values)
            by_values.append(dot_tn(weights_now.astype(BF16), above))
            crossed = jnp.sum(grad_probs * weights_now, axis=-1, keepdims=True)
            low = (weights_now * (grad_probs - crossed)).astype(BF16)
            by_query.append(dot(low, keys) * score_scale)
            by_keys.append(dot_tn(low, query))
        for kind, parts in enumerate((by_query, by_keys, by_values)):
            grad_tri[kind, :, lanes] = jnp.where(low_lanes, parts[0], parts[1]).astype(BF16)
        return carry

    lax.fori_loop(0, 3, attend_back, 0)
    for half in range(2):
        value = dot_nt(grad_tri[0], weight(0, half, 0))
        for kind in range(1, 3):
            value = value + dot_nt(grad_tri[kind], weight(0, half, kind))
        exchange(half, value, send4, recv4, slots4)
    reduces[1].to_major()
    for half in range(2):
        for kind in range(3):
            keep_grad(0, half, kind, dot_tn(hidden1[half], grad_tri[kind]))
    reduces[0].to_core()
    reduces[2].to_minor()

    exchanged(recv2, slots2)
    mine = r == latent
    self_col = xor(latent, k * latent)
    out_half = c * (r == latent).astype(jnp.int32) + (1 - self_col) * (r != latent).astype(jnp.int32)
    across = place.at(row=latent, col=1 - self_col)
    back_from = place.at(row=1 - r, col=xor(r, k * (1 - r)))

    def branch_end(rows, carry):
        gate = list(carry)
        for h in range(2):
            branch = send2[h, rows].astype(F32) + recv2[h, rows].astype(F32) + vec(h, 7)
            gate[h] = gate[h] + token_sum(cot_all[h, rows].astype(F32) * branch)
            middle = x_all[h, rows].astype(F32) + vec(h, 2) * branch1[h, rows]
            res_out[h, rows] = (middle + vec(h, 5) * branch).astype(BF16)
        return tuple(gate)

    gate2 = over_rows(branch_end, pair_zero)
    res_slot, xg_slot = wires.slot(), wires.slot()

    @pl.when(jnp.logical_not(mine))
    def _():
        wires.copy(res_slot, res_out.at[out_half], res_in, across).start()

    reduces[1].to_minor()
    reduces[2].to_col()
    exchanged(recv4, slots4)

    def first_back(rows, carry):
        shift, scale = (list(part) for part in carry)
        inverse = rstd1[rows]
        normed = [normed1[h, rows] for h in range(2)]
        scaled = []
        for h in range(2):
            grad = send4[h, rows].astype(F32) + recv4[h, rows].astype(F32)
            shift[h] = shift[h] + token_sum(grad)
            scale[h] = scale[h] + token_sum(grad * normed[h])
            scaled.append(grad * (1.0 + vec(h, 1)))
        back = norm_back(scaled, normed, inverse)
        for h in range(2):
            xg_out[h, rows] = grad_res[h, rows] + back[h]
        return tuple(shift), tuple(scale)

    shift1, scale1 = over_rows(first_back, (pair_zero,) * 2)

    def sums(kind):
        return token_sum(grad_tri[kind].astype(F32))

    shared = [sums(0), sums(2)] + widening_sum + [jnp.zeros((2, HALF), F32)]
    for h in range(2):
        own_rows = [shift1[h], scale1[h], gate1[h], shift2[h], scale2[h], gate2[h]]
        own_rows += [projection_sum[h], narrowing_sum[h]]
        payload_out[h] = jnp.concatenate(own_rows + shared, axis=0).astype(BF16)
    payload_slot = wires.slot()
    spot = 2 * place.shard + latent
    wires.send(payload_slot, payload_out.at[1 - c], payload.at[spot], place.column())
    payload[spot] = payload_out[c]

    @pl.when(jnp.logical_not(mine))
    def _():
        wires.copy(xg_slot, xg_out.at[out_half], xg_in, across).start()

    def payload_view(first, count):
        return payload.at[pl.ds(2 * first, 2 * count)]

    payloads = Gather(place, wires, payload_view)
    reduces[0].to_major()
    wires.arrived(payload_slot, payload.at[2 * place.shard + 1 - latent], place.column())
    payloads.minor()
    reduces[2].to_gather()
    reduces[1].to_col()
    payloads.major()
    reduces[0].to_minor()
    reduces[1].to_gather()
    reduces[2].gather.major()
    payloads.cores()
    reduces[0].to_col()
    reduces[1].gather.major()
    reduces[2].gather.cores()
    reduces[0].to_gather()
    payloads.finish()
    payload_copy = pltpu.make_async_copy(payload, payload_hbm, local_sems.at[3])
    payload_copy.start()
    reduces[1].gather.cores()
    reduces[2].gather.finish()
    outs = [
        pltpu.make_async_copy(final.at[seg], final_hbm.at[seg], local_sems.at[4 + seg])
        for seg in range(3)
    ]
    outs[2].start()
    reduces[0].gather.major()
    reduces[1].gather.finish()
    outs[1].start()

    @pl.when(mine)
    def _():
        result_ref[...] = res_out[out_half]
        xgrad_ref[...] = xg_out[out_half]

    @pl.when(jnp.logical_not(mine))
    def _():
        wires.copy(res_slot, res_out.at[out_half], res_in, across).wait_send()
        wires.copy(res_slot, res_out.at[out_half], res_in, back_from).wait_recv()
        wires.copy(xg_slot, xg_out.at[out_half], xg_in, across).wait_send()
        wires.copy(xg_slot, xg_out.at[out_half], xg_in, back_from).wait_recv()
        result_ref[...] = res_in[...]
        xgrad_ref[...] = xg_in[...]

    reduces[0].gather.cores()
    reduces[0].gather.finish()
    outs[0].start()
    x_sent()
    cot_sent()
    wires.drain()
    payload_copy.wait()
    for out in outs:
        out.wait()


def spread_halves(place, wires, source, landing):
    r, c, k, latent = place.r, place.c, place.k, place.latent
    slots = [wires.slot() for _ in range(2)]

    def copy(row, half):
        return pltpu.make_async_remote_copy(
            src_ref=source,
            dst_ref=landing.at[half],
            send_sem=wires.send_sems.at[slots[row]],
            recv_sem=wires.recv_sems.at[slots[half]],
            device_id=place.at(row=jnp.int32(row), col=xor(r, k * row)),
            device_id_type=MESH,
        )

    def each_target(act):
        for row in range(2):
            away = jnp.logical_or(r != row, c != xor(r, k * row))
            for half in range(2):
                @pl.when(jnp.logical_and(away, c == half))
                def _():
                    act(copy(row, half))

    each_target(lambda made: made.start())

    @pl.when(r == latent)
    def _():
        landing[c] = source[...]

    def collect():
        for half in range(2):
            @pl.when(jnp.logical_or(r != latent, c != half))
            def _():
                copy(0, half).wait_recv()

    def sent():
        each_target(lambda made: made.wait_send())

    return slots, collect, sent


def whole(shape, dtype):
    return pltpu.VMEM(shape, dtype)


def run_block(n, x, cot, modp, weights, triple_bias, widening):
    shards = 2 * n * n
    rows = SEG // shards
    tokens = (2, SEQ, HALF)
    vmem = pl.BlockSpec(memory_space=pltpu.VMEM)
    hbm = pl.BlockSpec(memory_space=pl.ANY)
    peers = max(n - 1, 1)
    scratch = [
        whole((3, 2, SEG, HALF), BF16),
        whole(tokens, BF16),
        whole(tokens, BF16),
        whole((4, 8, HALF), F32),
        whole((2, 8, HALF), F32),
        whole(tokens, F32),
        whole((SEQ, 1), F32),
        whole(tokens, BF16),
        whole((3, SEQ, HALF), BF16),
        whole((6, SEQ, SEQ), F32),
        whole((SEQ, HALF), BF16),
        whole(tokens, BF16),
        whole(tokens, BF16),
        whole(tokens, F32),
        whole(tokens, F32),
        whole((SEQ, 1), F32),
        whole(tokens, BF16),
        whole((4, SEQ, HALF), BF16),
        whole((4, SEQ, HALF), F32),
        whole(tokens, BF16),
        whole(tokens, BF16),
        whole(tokens, BF16),
        whole((4, SEQ, HALF), BF16),
        whole(tokens, BF16),
        whole(tokens, BF16),
        whole(tokens, F32),
        whole(tokens, BF16),
        whole((SEQ, HALF), BF16),
        whole((3, SEQ, HALF), BF16),
        whole(tokens, BF16),
        whole(tokens, BF16),
        whole(tokens, BF16),
        whole((SEQ, HALF), BF16),
        whole(tokens, F32),
        whole((SEQ, HALF), F32),
        whole((2, 16, HALF), BF16),
        whole((2 * shards, 16, HALF), BF16),
        whole((3, 2, SEG, HALF), BF16),
        whole((3, 2, SEG // 2, HALF), BF16),
        whole((3, peers, 2, SEG // (2 * n), HALF), BF16),
        whole((3, peers, 2, rows, HALF), BF16),
        whole((3, rows, HALF), BF16),
        whole((3, SEG, HALF), BF16),
        pltpu.SemaphoreType.DMA((SEMS,)),
        pltpu.SemaphoreType.DMA((SEMS,)),
        pltpu.SemaphoreType.DMA((8,)),
    ]

    def body(*refs):
        kernel(n, *refs)

    return pl.pallas_call(
        body,
        out_shape=(
            jax.ShapeDtypeStruct((SEQ, HALF), BF16),
            jax.ShapeDtypeStruct((SEQ, HALF), F32),
            jax.ShapeDtypeStruct((3, SEG, HALF), BF16),
            jax.ShapeDtypeStruct((2 * shards, 16, HALF), BF16),
        ),
        in_specs=[vmem, vmem, vmem, hbm, vmem, vmem],
        out_specs=(vmem, vmem, hbm, hbm),
        scratch_shapes=scratch,
        compiler_params=pltpu.CompilerParams(
            collective_id=0, has_side_effects=True, vmem_limit_bytes=60 * 1024 * 1024
        ),
        name="block",
    )(x, cot, modp, weights, triple_bias, widening)


def body(
    activations,
    timesteps,
    class_labels,
    time_table,
    class_table,
    modulation,
    modulation_bias,
    attention,
    attention_bias,
    projection,
    projection_bias,
    expansion,
    widening_bias,
    reduction,
    narrowing_bias,
    cotangent,
):
    n = math.isqrt(lax.axis_size("dp") // 2)
    latents = 4 * n * n
    dp, row = lax.axis_index("dp"), lax.axis_index("row")
    core, chip = dp % 2, dp // 2
    z, x = chip % n, chip // n
    shard = (core * n + jnp.where(core == 0, x, z)) * n + jnp.where(core == 0, z, x)

    picks = lax.all_gather(
        jnp.stack([timesteps, class_labels], axis=1), ("dp", "col"), axis=0, tiled=True
    ).reshape(n, n, 2, 2, 2)
    picks = jnp.stack([picks[:, :, 0], jnp.swapaxes(picks[:, :, 1], 0, 1)]).reshape(latents, 2)
    time_onehot = (picks[:, 0:1] == jnp.arange(STEPS, dtype=jnp.int32)[None, :]).astype(BF16)
    class_onehot = (picks[:, 1:2] == jnp.arange(CLASSES, dtype=jnp.int32)[None, :]).astype(BF16)
    condition = jnp.dot(time_onehot, time_table, preferred_element_type=F32) + jnp.dot(
        class_onehot, class_table, preferred_element_type=F32
    )
    silu_cond, silu_pullback = jax.vjp(jax.nn.silu, condition)
    silu_low = silu_cond.astype(BF16)
    modulation_flat = modulation.reshape(HALF, 6 * HALF)
    silu_mine = lax.dynamic_slice_in_dim(silu_low, 2 * shard, 2, axis=0)
    parts = jnp.dot(silu_mine, modulation_flat, preferred_element_type=F32).reshape(2, 6, HALF)
    extra = jnp.concatenate(
        [modulation_bias, projection_bias[None], narrowing_bias[None]], axis=0
    ).astype(F32)
    extra = jnp.where(row == 0, extra, 0.0)
    modp = jnp.concatenate([parts, jnp.zeros((2, 2, HALF), F32)], axis=1) + extra[None]

    weights = jnp.stack(
        [
            jnp.concatenate([jnp.swapaxes(attention, 0, 1).reshape(3 * HALF, HALF), projection]),
            jnp.swapaxes(expansion.reshape(HALF, 4, HALF), 0, 1).reshape(SEG, HALF),
            reduction,
        ]
    )
    zero_bias = jnp.zeros_like(attention_bias[0])
    triple_bias = jnp.stack([attention_bias[0], zero_bias, attention_bias[1]])[:, None].astype(F32)
    widening = widening_bias.reshape(4, 1, HALF).astype(F32)
    result, activations_grad, final, payload = run_block(
        n, activations, cotangent, modp, weights, triple_bias, widening
    )

    grad_modulation = payload[:, 0:6].reshape(latents, 6 * HALF)
    modulation_grad = lax.dot_general(
        silu_low, grad_modulation, (((0,), (0,)), ((), ())), preferred_element_type=F32
    )
    small = jnp.sum(payload, axis=0, dtype=F32)
    grad_silu = lax.psum(
        lax.dot_general(
            grad_modulation,
            modulation_flat,
            (((1,), (1,)), ((), ())),
            preferred_element_type=F32,
        ),
        "col",
    )
    grad_condition = silu_pullback(grad_silu)[0]

    def table_product(onehot):
        return lax.dot_general(
            onehot.astype(F32),
            grad_condition,
            (((0,), (0,)), ((), ())),
            precision=lax.Precision.HIGHEST,
        )

    attention_grad = jnp.swapaxes(final[0, : 3 * HALF].reshape(3, HALF, HALF), 0, 1)
    expansion_grad = jnp.swapaxes(final[1].reshape(4, HALF, HALF), 0, 1).reshape(HALF, SEG)
    return (
        result,
        activations_grad,
        table_product(time_onehot),
        table_product(class_onehot),
        modulation_grad.reshape(HALF, 6, HALF),
        small[0:6],
        attention_grad.astype(F32),
        small[8:10],
        final[0, 3 * HALF :].astype(F32),
        small[6],
        expansion_grad.astype(F32),
        small[10:14].reshape(SEG),
        final[2].astype(F32),
        small[7],
    )


def solution(mesh):
    placed = (
        P(("dp", "row"), "col"),
        P(("dp", "col")),
        P(("dp", "col")),
        P(None, "row"),
        P(None, "row"),
        P("row", None, "col"),
        P(None, "col"),
        P("col", None, "row"),
        P(None, "row"),
        P("row", "col"),
        P("col"),
        P("col", "row"),
        P("row"),
        P("row", "col"),
        P("col"),
        P(("dp", "row"), "col"),
    )
    return jax.shard_map(
        body,
        mesh=mesh,
        in_specs=placed,
        out_specs=(
            P(("dp", "row"), "col"),
            P(("dp", "row"), "col"),
            P(None, "row"),
            P(None, "row"),
            P("row", None, "col"),
            P(None, "col"),
            P("col", None, "row"),
            P(None, "row"),
            P("row", "col"),
            P("col"),
            P("col", "row"),
            P("row"),
            P("row", "col"),
            P("col"),
        ),
        check_vma=False,
    )
```

```python
import math

import jax
import jax.numpy as jnp
from jax import lax
from jax.experimental import pallas as pl
from jax.experimental.pallas import tpu as pltpu
from jax.sharding import PartitionSpec as P

D = 768
HALF = 384
SEQ = 256
HEAD_DIM = 64
STEPS = 1000
CLASSES = 1001
SEG = 1536
EPSILON = 1e-06
ROWS = 32
PART = SEQ // 2
SEMS = 176
F32 = jnp.float32
BF16 = jnp.bfloat16
MESH = pl.DeviceIdType.MESH


def dot(u, v):
    return lax.dot_general(u, v, (((1,), (0,)), ((), ())), preferred_element_type=F32)


def dot_nt(u, v):
    return lax.dot_general(u, v, (((1,), (1,)), ((), ())), preferred_element_type=F32)


def dot_tn(u, v):
    return lax.dot_general(u, v, (((0,), (0,)), ((), ())), preferred_element_type=F32)


def xor(u, v):
    return u + v - 2 * u * v


class Place:
    def __init__(self, n):
        self.n = n
        self.dp = lax.axis_index("dp")
        self.r = lax.axis_index("row")
        self.c = lax.axis_index("col")
        self.k = lax.rem(self.dp, 2)
        chip = lax.div(self.dp, 2)
        z = lax.rem(chip, n)
        x = lax.div(chip, n)
        self.major = x * (1 - self.k) + z * self.k
        self.minor = z * (1 - self.k) + x * self.k
        self.shard = (self.k * n + self.major) * n + self.minor
        self.latent = xor(self.c, self.k * self.r)

    def at(self, dp=None, row=None, col=None):
        return {
            "dp": self.dp if dp is None else dp,
            "row": self.r if row is None else row,
            "col": self.c if col is None else col,
        }

    def plane(self, major, minor):
        x = major * (1 - self.k) + minor * self.k
        z = minor * (1 - self.k) + major * self.k
        return self.at(dp=(x * self.n + z) * 2 + self.k)

    def along_minor(self, step):
        return self.plane(self.major, lax.rem(self.minor + step, self.n))

    def along_major(self, step):
        return self.plane(lax.rem(self.major + step, self.n), self.minor)

    def sibling(self):
        return self.at(dp=self.dp + 1 - 2 * self.k)

    def group(self, step):
        row = xor(self.r, step & 1)
        col = xor(self.c, step >> 1)
        return self.at(row=row, col=col)

    def partner(self):
        return self.at(row=1 - self.r, col=xor(self.c, self.k))

    def column(self):
        return self.at(col=1 - self.c)


class Wires:
    def __init__(self, send_sems, recv_sems):
        self.send_sems, self.recv_sems = send_sems, recv_sems
        self.used = 0
        self.sent = []

    def slot(self):
        self.used += 1
        assert self.used <= SEMS
        return self.used - 1

    def copy(self, slot, src, dst, device):
        return pltpu.make_async_remote_copy(
            src_ref=src,
            dst_ref=dst,
            send_sem=self.send_sems.at[slot],
            recv_sem=self.recv_sems.at[slot],
            device_id=device,
            device_id_type=MESH,
        )

    def send(self, slot, src, dst, device):
        copy = self.copy(slot, src, dst, device)
        copy.start()
        self.sent.append(copy)

    def arrived(self, slot, dst, device):
        self.copy(slot, dst, dst, device).wait_recv()

    def drain(self):
        for copy in self.sent:
            copy.wait_send()


class Gather:
    def __init__(self, place, wires, view):
        self.place, self.wires, self.view = place, wires, view
        self.near = [wires.slot() for _ in range(place.n - 1)]
        self.ring = [wires.slot() for _ in range(4)]
        self.core = [wires.slot() for _ in range(4)]

    def base(self, step, core=None):
        p = self.place
        own = core is None
        k, major = (p.k, p.major) if own else (core, p.minor)
        return (k * p.n + lax.rem(major + step, p.n)) * p.n

    def to_sibling(self, step):
        n = self.place.n
        mine = self.view(self.base(step), n)
        self.wires.send(self.core[step], mine, mine, self.place.sibling())

    def minor(self):
        p, w, n = self.place, self.wires, self.place.n
        mine = self.view(p.shard, 1)
        for step in range(1, n):
            w.send(self.near[step - 1], mine, mine, p.along_minor(step))

    def major(self):
        p, w, n = self.place, self.wires, self.place.n
        row = self.base(0)
        for step in range(1, n):
            other = lax.rem(p.minor + n - step, n)
            w.arrived(self.near[step - 1], self.view(row + other, 1), p.along_minor(step))
        if n > 1:
            mine = self.view(row, n)
            w.send(self.ring[0], mine, mine, p.along_major(1))
            w.send(self.ring[1], mine, mine, p.along_major(3))
        self.to_sibling(0)

    def major_on(self):
        p, w, n = self.place, self.wires, self.place.n
        if n == 1:
            return
        before, after = self.base(3), self.base(1)
        w.arrived(self.ring[0], self.view(before, n), p.along_major(3))
        half = self.view(before, 2)
        w.send(self.ring[2], half, half, p.along_major(1))
        w.arrived(self.ring[1], self.view(after, n), p.along_major(1))
        half = self.view(after + 2, 2)
        w.send(self.ring[3], half, half, p.along_major(3))
        self.to_sibling(3)
        self.to_sibling(1)

    def cores(self):
        p, w, n = self.place, self.wires, self.place.n
        if n == 1:
            return
        far = self.base(2)
        w.arrived(self.ring[2], self.view(far, 2), p.along_major(3))
        w.arrived(self.ring[3], self.view(far + 2, 2), p.along_major(1))
        self.to_sibling(2)

    def finish(self):
        p, w, n = self.place, self.wires, self.place.n
        for step in range(n):
            w.arrived(self.core[step], self.view(self.base(step, 1 - p.k), n), p.sibling())


class Reduce:
    def __init__(self, place, wires, seg, grads, from_core, from_major, from_minor, final):
        self.place, self.wires, self.seg = place, wires, seg
        self.grads, self.final = grads, final
        self.from_core, self.from_major = from_core, from_major
        self.from_minor = from_minor
        n = place.n
        self.rows = SEG // (2 * n * n)
        self.core = [wires.slot() for _ in range(n)]
        self.ring = [wires.slot() for _ in range(6)]
        self.near = [wires.slot() for _ in range(2 * n)]
        self.gather = Gather(place, wires, self.final_view)

    def span(self, first, count):
        return pl.ds(pl.multiple_of(first * self.rows, 16), count * self.rows)

    def view(self, first, count):
        return self.grads.at[self.seg, :, self.span(first, count)]

    def final_view(self, first, count):
        return self.final.at[self.seg, self.span(first, count)]

    def base(self, step):
        p = self.place
        return (p.k * p.n + lax.rem(p.major + step, p.n)) * p.n

    def add(self, first, count, arrivals):
        kind = BF16 if len(arrivals) == 1 else F32
        size = count * self.rows
        base, chunk = first * self.rows, 96

        def step(i, carry):
            at = pl.ds(pl.multiple_of(base + i * chunk, 16), chunk)
            total = self.grads[self.seg, :, at].astype(kind)
            for ref, start in arrivals:
                here = pl.ds(pl.multiple_of(start * self.rows + i * chunk, 16), chunk)
                total = total + ref[:, here].astype(kind)
            self.grads[self.seg, :, at] = total.astype(BF16)
            return carry

        lax.fori_loop(0, size // chunk, step, 0)

    def to_core(self):
        p, n = self.place, self.place.n
        for step in (2, 1, 3, 0) if n > 1 else (0,):
            block = lax.rem(p.minor + step, n)
            self.wires.send(
                self.core[step],
                self.view(((1 - p.k) * n + block) * n, n),
                self.from_core.at[self.seg, :, self.span(block * n, n)],
                p.sibling(),
            )

    def add_core(self, step):
        p, n = self.place, self.place.n
        block = lax.rem(p.major + step, n)
        landed = self.from_core.at[self.seg, :, self.span(block * n, n)]
        self.wires.arrived(self.core[step], landed, p.sibling())
        self.add(self.base(step), n, [(self.from_core.at[self.seg], block * n)])

    def ring_send(self, piece, first, step):
        self.wires.send(
            self.ring[piece],
            self.view(first, 2),
            self.from_major.at[self.seg, piece],
            self.place.along_major(step),
        )

    def ring_arrived(self, piece, step):
        self.wires.arrived(
            self.ring[piece], self.from_major.at[self.seg, piece], self.place.along_major(step)
        )
        return (self.from_major.at[self.seg, piece], 0)

    def to_major(self):
        if self.place.n == 1:
            self.add_core(0)
            return
        far, after, before = self.base(2), self.base(1), self.base(3)
        self.add_core(2)
        self.ring_send(0, far, 1)
        self.ring_send(1, far + 2, 3)
        self.add_core(1)
        self.ring_send(3, after + 2, 1)
        self.add_core(3)
        self.ring_send(4, before, 3)

    def major_on(self):
        if self.place.n == 1:
            return
        after, before = self.base(1), self.base(3)
        self.add(after, 2, [self.ring_arrived(0, 3)])
        self.ring_send(2, after, 1)
        self.add(before + 2, 2, [self.ring_arrived(1, 1)])
        self.ring_send(5, before + 2, 3)
        self.add_core(0)

    def to_minor(self):
        p, w, n = self.place, self.wires, self.place.n
        row = self.base(0)
        if n > 1:
            second = [self.ring_arrived(3, 3)]
            first = [self.ring_arrived(4, 1)]
            first.append(self.ring_arrived(2, 3))
            self.add(row, 2, first)
            second.append(self.ring_arrived(5, 1))
            self.add(row + 2, 2, second)
        for side in (1, 0):
            half = 1 - p.c if side else p.c
            for step in range(1 - side, n):
                there = p.along_minor(step)
                there["col"] = half
                w.send(
                    self.near[side * n + step],
                    self.grads.at[
                        self.seg, half, self.span(row + lax.rem(p.minor + step, n), 1)
                    ],
                    self.from_minor.at[self.seg, side * n + step],
                    there,
                )

    def to_gather(self):
        p, w, n = self.place, self.wires, self.place.n
        total = self.grads[self.seg, p.c, self.span(p.shard, 1)].astype(F32)
        for side in (0, 1):
            for step in range(1 - side, n):
                landed = self.from_minor.at[self.seg, side * n + step]
                w.arrived(self.near[side * n + step], landed, p.along_minor(step))
                total = total + landed[...].astype(F32)
        self.final[self.seg, self.span(p.shard, 1)] = total.astype(BF16)
        self.gather.minor()


def kernel(
    n,
    x_ref,
    cot_ref,
    step_ref,
    label_ref,
    time_hbm,
    class_hbm,
    modulation_hbm,
    attention_hbm,
    projection_hbm,
    expansion_hbm,
    reduction_hbm,
    modulation_bias_ref,
    projection_bias_ref,
    narrowing_ref,
    attention_bias_ref,
    widening_ref,
    result_ref,
    xgrad_ref,
    final_hbm,
    rows_ref,
    silu_ref,
    condition_grad_ref,
    weights,
    tables_time,
    tables_class,
    modulation,
    ids_out,
    ids_in,
    modp,
    spread_rows,
    silu_out,
    silu_in,
    x_all,
    cot_all,
    mod_parts,
    mod,
    normed1,
    rstd1,
    hidden1,
    triple,
    probs,
    attended,
    send1,
    recv1,
    branch1,
    normed2,
    rstd2,
    hidden2,
    activated,
    slope,
    grad_b2,
    send2,
    recv2,
    grad_up,
    send3,
    recv3,
    grad_res,
    grad_b1,
    grad_att,
    grad_tri,
    send4,
    recv4,
    res_out,
    res_in,
    xg_out,
    xg_low,
    xg_in,
    payload_out,
    payload,
    grads,
    from_core,
    from_major,
    from_minor,
    final,
    send_sems,
    recv_sems,
    local_sems,
):
    place = Place(n)
    wires = Wires(send_sems, recv_sems)
    r, c, k, latent = place.r, place.c, place.k, place.latent

    own = [
        [
            pltpu.make_async_copy(
                attention_hbm.at[kind],
                weights.at[0, c, kind * HALF : (kind + 1) * HALF],
                local_sems.at[kind],
            )
            for kind in range(3)
        ]
        + [
            pltpu.make_async_copy(
                projection_hbm, weights.at[0, c, 3 * HALF : 4 * HALF], local_sems.at[3]
            )
        ],
        [
            pltpu.make_async_copy(
                expansion_hbm.at[:, block * HALF : (block + 1) * HALF],
                weights.at[1, c, block * HALF : (block + 1) * HALF],
                local_sems.at[4 + block],
            )
            for block in range(4)
        ],
        [pltpu.make_async_copy(reduction_hbm, weights.at[2, c], local_sems.at[8])],
    ]
    table_loads = [
        pltpu.make_async_copy(time_hbm, tables_time, local_sems.at[9]),
        pltpu.make_async_copy(class_hbm, tables_class, local_sems.at[10]),
    ]
    modulation_load = pltpu.make_async_copy(modulation_hbm, modulation, local_sems.at[11])
    for copy in own[0] + table_loads + [modulation_load] + own[1] + own[2]:
        copy.start()
    row_at = lax.broadcasted_iota(jnp.int32, (8, 128), 0)
    ids_out[...] = jnp.where(row_at == 0, step_ref[0], label_ref[0])

    barrier = pltpu.get_barrier_semaphore()
    others = [place.group(s) for s in (1, 2, 3)] + [place.sibling()]
    for step in range(1, n):
        others += [place.along_minor(step), place.along_major(step)]
        there = place.along_minor(step)
        there["col"] = 1 - c
        others.append(there)
    for other in others:
        pl.semaphore_signal(barrier, inc=1, device_id=other, device_id_type=MESH)
    pl.semaphore_wait(barrier, len(others))

    shard_rows = SEG // (2 * n * n)

    def weight_view(seg):
        def view(first, count):
            start = pl.multiple_of(first * shard_rows, 16)
            return weights.at[seg, 1 - c, pl.ds(start, count * shard_rows)]

        return view

    gathers = [Gather(place, wires, weight_view(seg)) for seg in range(3)]
    weight_slots = [wires.slot() for _ in range(3)]
    my_rows = pl.ds(pl.multiple_of(place.shard * shard_rows, 16), shard_rows)

    def weights_out(seg):
        for copy in own[seg]:
            copy.wait()
        mine = weights.at[seg, c, my_rows]
        wires.send(weight_slots[seg], mine, mine, place.column())

    def weights_minor(seg):
        wires.arrived(weight_slots[seg], weights.at[seg, 1 - c, my_rows], place.column())
        gathers[seg].minor()

    weights_out(0)
    ids_slot = wires.slot()
    wires.send(ids_slot, ids_out, ids_in, place.column())
    x_spread = Spread(place, wires, x_ref, x_all)
    weights_out(1)
    weights_out(2)

    def table_rows(steps, labels, count):
        lanes = lax.broadcasted_iota(jnp.int32, (count, STEPS), 1)
        class_lanes = lax.broadcasted_iota(jnp.int32, (count, CLASSES), 1)
        return dot((lanes == steps).astype(BF16), tables_time[...]) + dot(
            (class_lanes == labels).astype(BF16), tables_class[...]
        )

    weights_minor(0)
    wires.arrived(ids_slot, ids_in, place.column())
    x_spread.forward()
    latent_at = lax.broadcasted_iota(jnp.int32, (16, 1), 0)

    def by_latent(row):
        return jnp.where(
            latent_at == c,
            ids_out[row : row + 1, 0:1],
            jnp.where(latent_at == 1 - c, ids_in[row : row + 1, 0:1], -1),
        )

    for copy in table_loads:
        copy.wait()
    modulation_load.wait()
    group_condition = table_rows(by_latent(0), by_latent(1), 16)
    group_silu = (group_condition / (1.0 + jnp.exp(-group_condition))).astype(BF16)
    first_row = (r == 0).astype(F32)
    modulation_bias = modulation_bias_ref[...].astype(F32)
    for kind in range(6):
        part = dot(group_silu, modulation[kind])
        for lat in range(2):
            modp[lat, kind : kind + 1, :] = (
                part[lat : lat + 1, :] + first_row * modulation_bias[kind : kind + 1, :]
            )
    for lat in range(2):
        modp[lat, 6:7, :] = first_row * projection_bias_ref[...].astype(F32).reshape(1, HALF)
        modp[lat, 7:8, :] = first_row * narrowing_ref[...].astype(F32).reshape(1, HALF)
    mod_slots = [wires.slot() for _ in range(3)]
    for step in (1, 2, 3):
        there = place.group(step)
        its_latent = xor(there["col"], k * there["row"])
        wires.send(mod_slots[step - 1], modp.at[its_latent], mod_parts.at[step], there)

    gathers[0].major()
    for step in (1, 2, 3):
        wires.arrived(mod_slots[step - 1], mod_parts.at[step], place.group(step))
    mod[c] = modp[latent] + mod_parts[1]
    mod[1 - c] = mod_parts[2] + mod_parts[3]

    def vec(half, row):
        return mod[half, row : row + 1, :]

    def over_rows(body, init=0, part=None):
        def step(i, carry):
            return body(pl.ds(pl.multiple_of(i * ROWS, ROWS), ROWS), carry)

        steps = SEQ // ROWS
        first, last = (0, steps) if part is None else (part * steps // 2, (part + 1) * steps // 2)
        return lax.fori_loop(first, last, step, init)

    def part_rows(part):
        return pl.ds(part * PART, PART)

    def norm(values):
        average = (
            jnp.sum(values[0], axis=-1, keepdims=True) + jnp.sum(values[1], axis=-1, keepdims=True)
        ) * (1.0 / D)
        square = (
            jnp.sum(values[0] * values[0], axis=-1, keepdims=True)
            + jnp.sum(values[1] * values[1], axis=-1, keepdims=True)
        ) * (1.0 / D)
        inverse = lax.rsqrt(square - average * average + EPSILON)
        return [(v - average) * inverse for v in values], inverse

    def norm_back(grad, normed, inverse):
        average = (
            jnp.sum(grad[0], axis=-1, keepdims=True) + jnp.sum(grad[1], axis=-1, keepdims=True)
        ) * (1.0 / D)
        crossed = (
            jnp.sum(grad[0] * normed[0], axis=-1, keepdims=True)
            + jnp.sum(grad[1] * normed[1], axis=-1, keepdims=True)
        ) * (1.0 / D)
        return [inverse * (g - average - m * crossed) for g, m in zip(grad, normed)]

    def token_sum(v):
        return jnp.sum(v, axis=0, keepdims=True)

    gathers[0].major_on()
    x_spread.collect()
    cot_spread = Spread(place, wires, cot_ref, cot_all)

    def first_norm(rows, carry):
        normed, inverse = norm([x_all[h, rows].astype(F32) for h in range(2)])
        rstd1[rows] = inverse
        for h in range(2):
            normed1[h, rows] = normed[h]
            hidden1[h, rows] = (normed[h] * (1.0 + vec(h, 1)) + vec(h, 0)).astype(BF16)
        return carry

    weights_minor(1)
    over_rows(first_norm)
    gathers[0].cores()
    weights_minor(2)

    def weight(seg, half, block):
        return weights[seg, half, block * HALF : (block + 1) * HALF, :]

    for kind in range(3):
        slope[kind] = dot(hidden1[c], weight(0, c, kind))
    cot_spread.forward()
    gathers[1].major()
    gathers[0].finish()
    gathers[2].major()
    for kind in range(3):
        value = slope[kind] + dot(hidden1[1 - c], weight(0, 1 - c, kind))
        if kind != 1:
            value = value + attention_bias_ref[kind // 2 : kind // 2 + 1, :].astype(F32)
        triple[kind] = value.astype(BF16)
    gathers[1].major_on()

    low_lanes = lax.broadcasted_iota(jnp.int32, (SEQ, 128), 1) < HEAD_DIM

    def one_head(v, head):
        mask = low_lanes if head == 0 else jnp.logical_not(low_lanes)
        return jnp.where(mask, v, jnp.zeros_like(v))

    score_scale = HEAD_DIM ** (-0.5)

    def attend(pair):
        lanes = pl.ds(pair * 128, 128)
        query = triple[0, :, lanes] * BF16(score_scale)
        keys = triple[1, :, lanes]
        values = triple[2, :, lanes]
        mixed = []
        for head in range(2):
            scores = dot_nt(one_head(query, head), keys)
            exponent = jnp.exp(scores - jnp.max(scores, axis=-1, keepdims=True))
            total = jnp.sum(exponent, axis=-1, keepdims=True)
            weights_now = exponent * (1.0 / total)
            probs[2 * pair + head] = weights_now
            mixed.append(dot(weights_now.astype(BF16), values))
        attended[:, lanes] = jnp.where(low_lanes, mixed[0], mixed[1]).astype(BF16)

    attend(0)
    gathers[2].major_on()
    attend(1)
    gathers[1].cores()
    attend(2)
    gathers[2].cores()

    def exchange(part, out, landing, slots):
        rows = part_rows(part)
        wires.send(slots[part], out.at[:, rows], landing.at[:, rows], place.partner())

    def exchanged(part, landing, slots):
        wires.arrived(slots[part], landing.at[:, part_rows(part)], place.partner())

    slots1, slots2, slots3, slots4 = ([wires.slot() for _ in range(2)] for _ in range(4))
    for part in range(2):
        rows = part_rows(part)
        for half in range(2):
            send1[half, rows] = dot(attended[rows, :], weight(0, half, 3)).astype(BF16)
        exchange(part, send1, recv1, slots1)
    cot_spread.collect()
    zero = jnp.zeros((1, HALF), F32)

    def start_back(rows, carry):
        out = []
        for h in range(2):
            low = (cot_all[h, rows].astype(F32) * vec(h, 5)).astype(BF16)
            grad_b2[h, rows] = low
            out.append(carry[h] + token_sum(low.astype(F32)))
        return tuple(out)

    narrowing_sum = over_rows(start_back, (zero, zero))

    def second_norm(rows, carry):
        middle = []
        for h in range(2):
            branch = send1[h, rows].astype(F32) + recv1[h, rows].astype(F32) + vec(h, 6)
            branch1[h, rows] = branch
            middle.append(x_all[h, rows].astype(F32) + vec(h, 2) * branch)
        normed, inverse = norm(middle)
        rstd2[rows] = inverse
        for h in range(2):
            normed2[h, rows] = normed[h]
            hidden2[h, rows] = (normed[h] * (1.0 + vec(h, 4)) + vec(h, 3)).astype(BF16)
        return carry

    root = math.sqrt(2.0 / math.pi)
    widening_sum = [zero] * 4
    for part in range(2):
        rows = part_rows(part)
        exchanged(part, recv1, slots1)
        over_rows(second_norm, part=part)
        if part == 0:
            gathers[1].finish()
        for block in range(4):
            upper = dot(hidden2[0, rows], weight(1, 0, block)) + dot(
                hidden2[1, rows], weight(1, 1, block)
            )
            bias = widening_ref[block * HALF : (block + 1) * HALF].astype(F32)
            upper = upper + bias.reshape(1, HALF)
            squared = upper * upper
            bent = jnp.tanh(root * upper * (1.0 + 0.044715 * squared))
            half_up = 0.5 * (1.0 + bent)
            activated[block, rows] = (upper * half_up).astype(BF16)
            slope[block, rows] = half_up + (0.5 * root) * upper * (1.0 - bent * bent) * (
                1.0 + (3.0 * 0.044715) * squared
            )
        if part == 0:
            gathers[2].finish()
        for block in range(4):
            back = dot_nt(grad_b2[0, rows], weight(2, 0, block)) + dot_nt(
                grad_b2[1, rows], weight(2, 1, block)
            )
            low = (back * slope[block, rows]).astype(BF16)
            grad_up[block, rows] = low
            widening_sum[block] = widening_sum[block] + token_sum(low.astype(F32))
        for half in range(2):
            value = dot_nt(grad_up[0, rows], weight(1, half, 0))
            for block in range(1, 4):
                value = value + dot_nt(grad_up[block, rows], weight(1, half, block))
            send3[half, rows] = value.astype(BF16)
        exchange(part, send3, recv3, slots3)

    reduces = [
        Reduce(place, wires, seg, grads, from_core, from_major, from_minor, final)
        for seg in range(3)
    ]

    def keep_grad(seg, half, block, value):
        grads[seg, half, block * HALF : (block + 1) * HALF, :] = value.astype(BF16)

    for block in range(4):
        for half in range(2):
            keep_grad(2, half, block, dot_tn(activated[block], grad_b2[half]))
    reduces[2].to_core()
    for block in range(4):
        for half in range(2):
            keep_grad(1, half, block, dot_tn(hidden2[half], grad_up[block]))
    reduces[1].to_core()
    for part in range(2):
        rows = part_rows(part)
        for half in range(2):
            value = dot(activated[0, rows], weight(2, half, 0))
            for block in range(1, 4):
                value = value + dot(activated[block, rows], weight(2, half, block))
            send2[half, rows] = value.astype(BF16)
        exchange(part, send2, recv2, slots2)
    reduces[2].to_major()

    def second_back(rows, carry):
        shift, scale, gate, bias = (list(part) for part in carry)
        inverse = rstd2[rows]
        normed = [normed2[h, rows] for h in range(2)]
        scaled = []
        for h in range(2):
            grad = send3[h, rows].astype(F32) + recv3[h, rows].astype(F32)
            shift[h] = shift[h] + token_sum(grad)
            scale[h] = scale[h] + token_sum(grad * normed[h])
            scaled.append(grad * (1.0 + vec(h, 4)))
        back = norm_back(scaled, normed, inverse)
        for h in range(2):
            total = cot_all[h, rows].astype(F32) + back[h]
            grad_res[h, rows] = total
            gate[h] = gate[h] + token_sum(total * branch1[h, rows])
            low = (total * vec(h, 2)).astype(BF16)
            grad_b1[h, rows] = low
            bias[h] = bias[h] + token_sum(low.astype(F32))
        return tuple(shift), tuple(scale), tuple(gate), tuple(bias)

    pair_zero = (zero, zero)
    sums2 = (pair_zero,) * 4
    for part in range(2):
        rows = part_rows(part)
        exchanged(part, recv3, slots3)
        sums2 = over_rows(second_back, sums2, part)
        grad_att[rows, :] = (
            dot_nt(grad_b1[0, rows], weight(0, 0, 3)) + dot_nt(grad_b1[1, rows], weight(0, 1, 3))
        ).astype(BF16)
    shift2, scale2, gate1, projection_sum = sums2
    for half in range(2):
        keep_grad(0, half, 3, dot_tn(attended[...], grad_b1[half]))

    def attend_back(pair):
        lanes = pl.ds(pair * 128, 128)
        query = triple[0, :, lanes] * BF16(score_scale)
        keys = triple[1, :, lanes]
        values = triple[2, :, lanes]
        above = grad_att[:, lanes]
        by_query, by_keys, by_values = [], [], []
        for head in range(2):
            weights_now = probs[2 * pair + head]
            grad_probs = dot_nt(one_head(above, head), values)
            by_values.append(dot_tn(weights_now.astype(BF16), above))
            crossed = jnp.sum(grad_probs * weights_now, axis=-1, keepdims=True)
            low = (weights_now * (grad_probs - crossed)).astype(BF16)
            by_query.append(dot(low, keys) * score_scale)
            by_keys.append(dot_tn(low, query))
        for kind, parts in enumerate((by_query, by_keys, by_values)):
            grad_tri[kind, :, lanes] = jnp.where(low_lanes, parts[0], parts[1]).astype(BF16)

    reduces[2].major_on()
    attend_back(0)
    reduces[1].to_major()
    exchanged(0, recv2, slots2)
    exchanged(1, recv2, slots2)
    mine = r == latent
    self_col = xor(latent, k * latent)
    out_half = c * (r == latent).astype(jnp.int32) + (1 - self_col) * (r != latent).astype(jnp.int32)
    across = place.at(row=latent, col=1 - self_col)
    back_from = place.at(row=1 - r, col=xor(r, k * (1 - r)))

    def branch_end(rows, carry):
        gate = list(carry)
        for h in range(2):
            branch = send2[h, rows].astype(F32) + recv2[h, rows].astype(F32) + vec(h, 7)
            gate[h] = gate[h] + token_sum(cot_all[h, rows].astype(F32) * branch)
            middle = x_all[h, rows].astype(F32) + vec(h, 2) * branch1[h, rows]
            res_out[h, rows] = (middle + vec(h, 5) * branch).astype(BF16)
        return tuple(gate)

    gate2 = over_rows(branch_end, pair_zero)
    res_slot, xg_slot = wires.slot(), wires.slot()

    @pl.when(jnp.logical_not(mine))
    def _():
        wires.copy(res_slot, res_out.at[out_half], res_in, across).start()

    attend_back(1)
    reduces[2].to_minor()
    attend_back(2)
    reduces[1].major_on()
    for half in range(2):
        for kind in range(3):
            keep_grad(0, half, kind, dot_tn(hidden1[half], grad_tri[kind]))
    reduces[0].to_core()
    for part in range(2):
        rows = part_rows(part)
        for half in range(2):
            value = dot_nt(grad_tri[0, rows], weight(0, half, 0))
            for kind in range(1, 3):
                value = value + dot_nt(grad_tri[kind, rows], weight(0, half, kind))
            send4[half, rows] = value.astype(BF16)
        exchange(part, send4, recv4, slots4)
    reduces[2].to_gather()
    reduces[1].to_minor()
    reduces[0].to_major()
    reduces[2].gather.major()

    def first_back(rows, carry):
        shift, scale = (list(part) for part in carry)
        inverse = rstd1[rows]
        normed = [normed1[h, rows] for h in range(2)]
        scaled = []
        for h in range(2):
            grad = send4[h, rows].astype(F32) + recv4[h, rows].astype(F32)
            shift[h] = shift[h] + token_sum(grad)
            scale[h] = scale[h] + token_sum(grad * normed[h])
            scaled.append(grad * (1.0 + vec(h, 1)))
        back = norm_back(scaled, normed, inverse)
        for h in range(2):
            total = grad_res[h, rows] + back[h]
            xg_out[h, rows] = total
            xg_low[h, rows] = total.astype(BF16)
        return tuple(shift), tuple(scale)

    sums1 = (pair_zero,) * 2
    for part in range(2):
        exchanged(part, recv4, slots4)
        sums1 = over_rows(first_back, sums1, part)
    shift1, scale1 = sums1

    def sums(kind):
        return token_sum(grad_tri[kind].astype(F32))

    shared = [sums(0), sums(2)] + widening_sum
    digit = lax.broadcasted_iota(jnp.int32, (1, HALF), 1) < 128
    for row in range(2):
        picked = jnp.where(latent == c, ids_out[row : row + 1, 0:1], ids_in[row : row + 1, 0:1])
        high = lax.shift_right_logical(picked, 5)
        shared.append(jnp.where(digit, high, picked - 32 * high).astype(F32))
    for h in range(2):
        own_rows = [shift1[h], scale1[h], gate1[h], shift2[h], scale2[h], gate2[h]]
        own_rows += [projection_sum[h], narrowing_sum[h]]
        payload_out[h] = jnp.concatenate(own_rows + shared, axis=0).astype(BF16)
    payload_slot = wires.slot()
    spot = 2 * place.shard + latent
    wires.send(payload_slot, payload_out.at[1 - c], payload.at[spot], place.column())
    payload[spot] = payload_out[c]

    @pl.when(jnp.logical_not(mine))
    def _():
        wires.copy(xg_slot, xg_low.at[out_half], xg_in, across).start()

    def payload_view(first, count):
        return payload.at[pl.ds(2 * first, 2 * count)]

    payloads = Gather(place, wires, payload_view)
    reduces[0].major_on()
    wires.arrived(payload_slot, payload.at[2 * place.shard + 1 - latent], place.column())
    payloads.minor()
    reduces[1].to_gather()
    reduces[2].gather.major_on()
    payloads.major()
    reduces[0].to_minor()
    payloads.major_on()
    reduces[1].gather.major()
    reduces[2].gather.cores()
    payloads.cores()
    reduces[1].gather.major_on()
    reduces[0].to_gather()
    payloads.finish()

    count = 4 * n * n
    for lat in range(count):
        for part in range(3):
            spread_rows[part, pl.ds(16 * lat, 16), :] = payload[
                lat, :, part * 128 : (part + 1) * 128
            ].astype(F32)
    for kind in range(16):
        for part in range(3):
            rows_ref[kind, :, part * 128 : (part + 1) * 128] = spread_rows[
                part, pl.ds(kind, count, stride=16), :
            ].astype(BF16)
    reduces[0].gather.major()
    reduces[1].gather.cores()
    value = dot_nt(rows_ref[0], modulation[0])
    for kind in range(1, 6):
        value = value + dot_nt(rows_ref[kind], modulation[kind])
    silu_out[...] = value
    silu_slot = wires.slot()
    wires.send(silu_slot, silu_out, silu_in, place.column())

    reduces[0].gather.major_on()
    reduces[2].gather.finish()
    outs = [
        pltpu.make_async_copy(final.at[seg], final_hbm.at[seg], local_sems.at[12 + seg])
        for seg in range(3)
    ]
    outs[2].start()

    def decode(kind):
        both = rows_ref[kind].astype(F32)
        return (32.0 * both[:, 0:1] + both[:, 128:129]).astype(jnp.int32)

    condition = table_rows(decode(14), decode(15), count)
    sigmoid = 1.0 / (1.0 + jnp.exp(-condition))
    silu_ref[...] = (condition * sigmoid).astype(BF16)
    reduces[0].gather.cores()
    reduces[1].gather.finish()
    outs[1].start()
    wires.arrived(silu_slot, silu_in, place.column())
    condition_grad_ref[...] = (silu_out[...] + silu_in[...]) * (
        sigmoid * (1.0 + condition * (1.0 - sigmoid))
    )

    @pl.when(mine)
    def _():
        result_ref[...] = res_out[out_half]
        xgrad_ref[...] = xg_out[out_half]

    @pl.when(jnp.logical_not(mine))
    def _():
        wires.copy(res_slot, res_out.at[out_half], res_in, across).wait_send()
        wires.copy(res_slot, res_out.at[out_half], res_in, back_from).wait_recv()
        wires.copy(xg_slot, xg_low.at[out_half], xg_in, across).wait_send()
        wires.copy(xg_slot, xg_low.at[out_half], xg_in, back_from).wait_recv()
        result_ref[...] = res_in[...]
        xgrad_ref[...] = xg_in[...].astype(F32)

    reduces[0].gather.finish()
    outs[0].start()
    x_spread.sent()
    cot_spread.sent()
    wires.drain()
    for out in outs:
        out.wait()


class Spread:
    def __init__(self, place, wires, source, landing):
        self.place, self.wires, self.landing = place, wires, landing
        r, c, k, latent = place.r, place.c, place.k, place.latent
        self.mine = r == latent
        self.far = 1 - xor(latent, k * latent)
        self.first, _, self.last = [wires.slot() for _ in range(3)]
        self.out = self.copy(
            source, c, self.first, self.first + c, place.at(row=1 - r, col=xor(r, k * (1 - r)))
        )
        self.forwarded = self.copy(
            landing.at[self.far], self.far, self.last, self.last, place.partner()
        )
        self.out.start()

        @pl.when(self.mine)
        def _():
            landing[c] = source[...]

    def copy(self, source, half, send_slot, recv_slot, there):
        return pltpu.make_async_remote_copy(
            src_ref=source,
            dst_ref=self.landing.at[half],
            send_sem=self.wires.send_sems.at[send_slot],
            recv_sem=self.wires.recv_sems.at[recv_slot],
            device_id=there,
            device_id_type=MESH,
        )

    def arrived(self, half, slot):
        self.copy(self.landing.at[half], half, self.last, slot, self.place.partner()).wait_recv()

    def forward(self):
        @pl.when(jnp.logical_not(self.mine))
        def _():
            self.arrived(self.far, self.first + self.far)
            self.forwarded.start()

    def collect(self):
        @pl.when(self.mine)
        def _():
            self.arrived(self.far, self.last)

        @pl.when(jnp.logical_not(self.mine))
        def _():
            self.arrived(1 - self.far, self.first + 1 - self.far)

    def sent(self):
        self.out.wait_send()

        @pl.when(jnp.logical_not(self.mine))
        def _():
            self.forwarded.wait_send()


def whole(shape, dtype):
    return pltpu.VMEM(shape, dtype)


def run_block(n, *operands):
    shards = 2 * n * n
    rows = SEG // shards
    tokens = (2, SEQ, HALF)
    vmem = pl.BlockSpec(memory_space=pltpu.VMEM)
    hbm = pl.BlockSpec(memory_space=pl.ANY)
    smem = pl.BlockSpec(memory_space=pltpu.SMEM)
    scratch = [
        whole((3, 2, SEG, HALF), BF16),
        whole((STEPS, HALF), BF16),
        whole((CLASSES, HALF), BF16),
        whole((6, HALF, HALF), BF16),
        whole((8, 128), jnp.int32),
        whole((8, 128), jnp.int32),
        whole((2, 8, HALF), F32),
        whole((3, 32 * shards, 128), F32),
        whole((2 * shards, HALF), F32),
        whole((2 * shards, HALF), F32),
        whole(tokens, BF16),
        whole(tokens, BF16),
        whole((4, 8, HALF), F32),
        whole((2, 8, HALF), F32),
        whole(tokens, F32),
        whole((SEQ, 1), F32),
        whole(tokens, BF16),
        whole((3, SEQ, HALF), BF16),
        whole((6, SEQ, SEQ), F32),
        whole((SEQ, HALF), BF16),
        whole(tokens, BF16),
        whole(tokens, BF16),
        whole(tokens, F32),
        whole(tokens, F32),
        whole((SEQ, 1), F32),
        whole(tokens, BF16),
        whole((4, SEQ, HALF), BF16),
        whole((4, SEQ, HALF), F32),
        whole(tokens, BF16),
        whole(tokens, BF16),
        whole(tokens, BF16),
        whole((4, SEQ, HALF), BF16),
        whole(tokens, BF16),
        whole(tokens, BF16),
        whole(tokens, F32),
        whole(tokens, BF16),
        whole((SEQ, HALF), BF16),
        whole((3, SEQ, HALF), BF16),
        whole(tokens, BF16),
        whole(tokens, BF16),
        whole(tokens, BF16),
        whole((SEQ, HALF), BF16),
        whole(tokens, F32),
        whole(tokens, BF16),
        whole((SEQ, HALF), BF16),
        whole((2, 16, HALF), BF16),
        whole((2 * shards, 16, HALF), BF16),
        whole((3, 2, SEG, HALF), BF16),
        whole((3, 2, SEG // 2, HALF), BF16),
        whole((3, 6, 2, 2 * rows, HALF), BF16),
        whole((3, 2 * n, rows, HALF), BF16),
        whole((3, SEG, HALF), BF16),
        pltpu.SemaphoreType.DMA((SEMS,)),
        pltpu.SemaphoreType.DMA((SEMS,)),
        pltpu.SemaphoreType.DMA((16,)),
    ]

    def body(*refs):
        kernel(n, *refs)

    return pl.pallas_call(
        body,
        out_shape=(
            jax.ShapeDtypeStruct((SEQ, HALF), BF16),
            jax.ShapeDtypeStruct((SEQ, HALF), F32),
            jax.ShapeDtypeStruct((3, SEG, HALF), BF16),
            jax.ShapeDtypeStruct((16, 2 * shards, HALF), BF16),
            jax.ShapeDtypeStruct((2 * shards, HALF), BF16),
            jax.ShapeDtypeStruct((2 * shards, HALF), F32),
        ),
        in_specs=[vmem, vmem, smem, smem] + [hbm] * 7 + [vmem] * 5,
        out_specs=(vmem, vmem, hbm, vmem, vmem, vmem),
        scratch_shapes=scratch,
        compiler_params=pltpu.CompilerParams(
            collective_id=0, has_side_effects=True, vmem_limit_bytes=60 * 1024 * 1024
        ),
        name="block",
    )(*operands)


def finish_kernel(
    result_in,
    xgrad_in,
    final_hbm,
    rows_ref,
    silu_ref,
    condition_grad_ref,
    result_ref,
    xgrad_ref,
    time_hbm,
    class_hbm,
    modulation_hbm,
    modulation_bias_ref,
    attention_hbm,
    attention_bias_ref,
    projection_hbm,
    projection_bias_ref,
    expansion_hbm,
    widening_ref,
    reduction_hbm,
    narrowing_ref,
    final,
    time_grad,
    class_grad,
    modulation_grad,
    wide,
    sems,
):
    loads = [pltpu.make_async_copy(final_hbm.at[seg], final.at[seg], sems.at[seg]) for seg in range(3)]
    for seg in (2, 1, 0):
        loads[seg].start()
    stores = []

    def store(source, target):
        copy = pltpu.make_async_copy(source, target, sems.at[3 + len(stores)])
        copy.start()
        stores.append(copy)

    result_ref[...] = result_in[...]
    xgrad_ref[...] = xgrad_in[...]
    silu = silu_ref[...]
    for kind in range(6):
        modulation_grad[kind] = dot_tn(silu, rows_ref[kind])
        store(modulation_grad.at[kind], modulation_hbm.at[kind])

    def widen(seg, block):
        at = pl.ds(block * HALF, HALF)
        wide[seg, at] = final[seg, at].astype(F32)
        return wide.at[seg, at]

    loads[2].wait()
    for block in range(4):
        store(widen(2, block), reduction_hbm.at[pl.ds(block * HALF, HALF)])
    loads[1].wait()
    for block in range(4):
        store(widen(1, block), expansion_hbm.at[:, pl.ds(block * HALF, HALF)])
    loads[0].wait()
    for block in range(3):
        store(widen(0, block), attention_hbm.at[block])
    store(widen(0, 3), projection_hbm)

    count = silu.shape[0]
    grad = condition_grad_ref[...]
    high = grad.astype(BF16)
    rest = grad - high.astype(F32)
    middle = rest.astype(BF16)
    low = (rest - middle.astype(F32)).astype(BF16)

    def scatter(kind, size):
        both = rows_ref[kind].astype(F32)
        picked = (32.0 * both[:, 0:1] + both[:, 128:129]).astype(jnp.int32)
        onehot = (lax.broadcasted_iota(jnp.int32, (count, 1024), 1) == picked).astype(BF16)
        return (dot_tn(onehot, high) + dot_tn(onehot, middle) + dot_tn(onehot, low))[:size]

    time_grad[...] = scatter(14, STEPS)
    store(time_grad, time_hbm)
    class_grad[...] = scatter(15, CLASSES)
    store(class_grad, class_hbm)

    def total(kind):
        return jnp.sum(rows_ref[kind].astype(F32), axis=0, keepdims=True)

    for kind in range(6):
        modulation_bias_ref[kind : kind + 1, :] = total(kind)
    projection_bias_ref[...] = total(6).reshape(HALF)
    narrowing_ref[...] = total(7).reshape(HALF)
    for kind in range(2):
        attention_bias_ref[kind : kind + 1, :] = total(8 + kind)
    for block in range(4):
        widening_ref[block * HALF : (block + 1) * HALF] = total(10 + block).reshape(HALF)
    for copy in stores:
        copy.wait()


def finish(result, xgrad, final, rows, silu, condition_grad):
    vmem = pl.BlockSpec(memory_space=pltpu.VMEM)
    hbm = pl.BlockSpec(memory_space=pl.ANY)
    shapes = [
        ((SEQ, HALF), vmem),
        ((SEQ, HALF), vmem),
        ((STEPS, HALF), hbm),
        ((CLASSES, HALF), hbm),
        ((6, HALF, HALF), hbm),
        ((6, HALF), vmem),
        ((3, HALF, HALF), hbm),
        ((2, HALF), vmem),
        ((HALF, HALF), hbm),
        ((HALF,), vmem),
        ((HALF, SEG), hbm),
        ((SEG,), vmem),
        ((SEG, HALF), hbm),
        ((HALF,), vmem),
    ]
    return pl.pallas_call(
        finish_kernel,
        out_shape=tuple(
            jax.ShapeDtypeStruct(shape, BF16 if i == 0 else F32)
            for i, (shape, _) in enumerate(shapes)
        ),
        in_specs=[vmem, vmem, hbm, vmem, vmem, vmem],
        out_specs=tuple(spec for _, spec in shapes),
        scratch_shapes=[
            whole((3, SEG, HALF), BF16),
            whole((STEPS, HALF), F32),
            whole((CLASSES, HALF), F32),
            whole((6, HALF, HALF), F32),
            whole((3, SEG, HALF), F32),
            pltpu.SemaphoreType.DMA((24,)),
        ],
        compiler_params=pltpu.CompilerParams(vmem_limit_bytes=60 * 1024 * 1024),
        name="finish",
    )(result, xgrad, final, rows, silu, condition_grad)


def body(
    activations,
    timesteps,
    class_labels,
    time_table,
    class_table,
    modulation,
    modulation_bias,
    attention,
    attention_bias,
    projection,
    projection_bias,
    expansion,
    widening_bias,
    reduction,
    narrowing_bias,
    cotangent,
):
    n = math.isqrt(lax.axis_size("dp") // 2)
    result, activations_grad, final, rows, silu, condition_grad = run_block(
        n,
        activations,
        cotangent,
        timesteps,
        class_labels,
        time_table,
        class_table,
        jnp.swapaxes(modulation, 0, 1),
        jnp.swapaxes(attention, 0, 1),
        projection,
        expansion,
        reduction,
        modulation_bias,
        projection_bias,
        narrowing_bias,
        attention_bias,
        widening_bias,
    )
    (
        result,
        activations_grad,
        time_grad,
        class_grad,
        modulation_grad,
        modulation_bias_grad,
        attention_grad,
        attention_bias_grad,
        projection_grad,
        projection_bias_grad,
        expansion_grad,
        expansion_bias_grad,
        reduction_grad,
        reduction_bias_grad,
    ) = finish(result, activations_grad, final, rows, silu, condition_grad)
    return (
        result,
        activations_grad,
        time_grad,
        class_grad,
        jnp.swapaxes(modulation_grad, 0, 1),
        modulation_bias_grad,
        jnp.swapaxes(attention_grad, 0, 1),
        attention_bias_grad,
        projection_grad,
        projection_bias_grad,
        expansion_grad,
        expansion_bias_grad,
        reduction_grad,
        reduction_bias_grad,
    )


def solution(mesh):
    placed = (
        P(("dp", "row"), "col"),
        P(("dp", "col")),
        P(("dp", "col")),
        P(None, "row"),
        P(None, "row"),
        P("row", None, "col"),
        P(None, "col"),
        P("col", None, "row"),
        P(None, "row"),
        P("row", "col"),
        P("col"),
        P("col", "row"),
        P("row"),
        P("row", "col"),
        P("col"),
        P(("dp", "row"), "col"),
    )
    return jax.shard_map(
        body,
        mesh=mesh,
        in_specs=placed,
        out_specs=(
            P(("dp", "row"), "col"),
            P(("dp", "row"), "col"),
            P(None, "row"),
            P(None, "row"),
            P("row", None, "col"),
            P(None, "col"),
            P("col", None, "row"),
            P(None, "row"),
            P("row", "col"),
            P("col"),
            P("col", "row"),
            P("row"),
            P("row", "col"),
            P("col"),
        ),
        check_vma=False,
    )
```

```python
import math

import jax
import jax.numpy as jnp
from jax import lax
from jax.experimental import pallas as pl
from jax.experimental.pallas import tpu as pltpu
from jax.sharding import PartitionSpec as P

D = 768
HALF = 384
SEQ = 256
HEAD_DIM = 64
STEPS = 1000
CLASSES = 1001
SEG = 1536
EPSILON = 1e-06
ROWS = 32
PART = SEQ // 2
SEMS = 176
F32 = jnp.float32
BF16 = jnp.bfloat16
MESH = pl.DeviceIdType.MESH


def dot(u, v):
    return lax.dot_general(u, v, (((1,), (0,)), ((), ())), preferred_element_type=F32)


def dot_nt(u, v):
    return lax.dot_general(u, v, (((1,), (1,)), ((), ())), preferred_element_type=F32)


def dot_tn(u, v):
    return lax.dot_general(u, v, (((0,), (0,)), ((), ())), preferred_element_type=F32)


def xor(u, v):
    return u + v - 2 * u * v


class Place:
    def __init__(self, n):
        self.n = n
        self.dp = lax.axis_index("dp")
        self.r = lax.axis_index("row")
        self.c = lax.axis_index("col")
        self.k = lax.rem(self.dp, 2)
        chip = lax.div(self.dp, 2)
        z = lax.rem(chip, n)
        x = lax.div(chip, n)
        self.major = x * (1 - self.k) + z * self.k
        self.minor = z * (1 - self.k) + x * self.k
        self.shard = (self.k * n + self.major) * n + self.minor
        self.latent = xor(self.c, self.k * self.r)

    def at(self, dp=None, row=None, col=None):
        return {
            "dp": self.dp if dp is None else dp,
            "row": self.r if row is None else row,
            "col": self.c if col is None else col,
        }

    def plane(self, major, minor):
        x = major * (1 - self.k) + minor * self.k
        z = minor * (1 - self.k) + major * self.k
        return self.at(dp=(x * self.n + z) * 2 + self.k)

    def along_minor(self, step):
        return self.plane(self.major, lax.rem(self.minor + step, self.n))

    def along_major(self, step):
        return self.plane(lax.rem(self.major + step, self.n), self.minor)

    def sibling(self):
        return self.at(dp=self.dp + 1 - 2 * self.k)

    def group(self, step):
        row = xor(self.r, step & 1)
        col = xor(self.c, step >> 1)
        return self.at(row=row, col=col)

    def partner(self):
        return self.at(row=1 - self.r, col=xor(self.c, self.k))

    def column(self):
        return self.at(col=1 - self.c)


class Wires:
    def __init__(self, send_sems, recv_sems):
        self.send_sems, self.recv_sems = send_sems, recv_sems
        self.used = 0
        self.sent = []

    def slot(self):
        self.used += 1
        assert self.used <= SEMS
        return self.used - 1

    def copy(self, slot, src, dst, device):
        return pltpu.make_async_remote_copy(
            src_ref=src,
            dst_ref=dst,
            send_sem=self.send_sems.at[slot],
            recv_sem=self.recv_sems.at[slot],
            device_id=device,
            device_id_type=MESH,
        )

    def send(self, slot, src, dst, device):
        copy = self.copy(slot, src, dst, device)
        copy.start()
        self.sent.append(copy)

    def arrived(self, slot, dst, device):
        self.copy(slot, dst, dst, device).wait_recv()

    def drain(self):
        for copy in self.sent:
            copy.wait_send()


class Gather:
    def __init__(self, place, wires, view):
        self.place, self.wires, self.view = place, wires, view
        self.near = [wires.slot() for _ in range(place.n - 1)]
        self.ring = [wires.slot() for _ in range(4)]
        self.core = [wires.slot() for _ in range(4)]

    def base(self, step, core=None):
        p = self.place
        own = core is None
        k, major = (p.k, p.major) if own else (core, p.minor)
        return (k * p.n + lax.rem(major + step, p.n)) * p.n

    def to_sibling(self, step):
        n = self.place.n
        mine = self.view(self.base(step), n)
        self.wires.send(self.core[step], mine, mine, self.place.sibling())

    def minor(self):
        p, w, n = self.place, self.wires, self.place.n
        mine = self.view(p.shard, 1)
        for step in range(1, n):
            w.send(self.near[step - 1], mine, mine, p.along_minor(step))

    def major(self):
        p, w, n = self.place, self.wires, self.place.n
        row = self.base(0)
        for step in range(1, n):
            other = lax.rem(p.minor + n - step, n)
            w.arrived(self.near[step - 1], self.view(row + other, 1), p.along_minor(step))
        if n > 1:
            mine = self.view(row, n)
            w.send(self.ring[0], mine, mine, p.along_major(1))
            w.send(self.ring[1], mine, mine, p.along_major(3))
        self.to_sibling(0)

    def major_on(self):
        p, w, n = self.place, self.wires, self.place.n
        if n == 1:
            return
        before, after = self.base(3), self.base(1)
        w.arrived(self.ring[0], self.view(before, n), p.along_major(3))
        half = self.view(before, 2)
        w.send(self.ring[2], half, half, p.along_major(1))
        w.arrived(self.ring[1], self.view(after, n), p.along_major(1))
        half = self.view(after + 2, 2)
        w.send(self.ring[3], half, half, p.along_major(3))
        self.to_sibling(3)
        self.to_sibling(1)

    def cores(self):
        p, w, n = self.place, self.wires, self.place.n
        if n == 1:
            return
        far = self.base(2)
        w.arrived(self.ring[2], self.view(far, 2), p.along_major(3))
        w.arrived(self.ring[3], self.view(far + 2, 2), p.along_major(1))
        self.to_sibling(2)

    def finish(self):
        p, w, n = self.place, self.wires, self.place.n
        for step in range(n):
            w.arrived(self.core[step], self.view(self.base(step, 1 - p.k), n), p.sibling())


class Reduce:
    def __init__(self, place, wires, seg, grads, from_core, from_major, from_minor, final):
        self.place, self.wires, self.seg = place, wires, seg
        self.grads, self.final = grads, final
        self.from_core, self.from_major = from_core, from_major
        self.from_minor = from_minor
        n = place.n
        self.rows = SEG // (2 * n * n)
        self.core = [wires.slot() for _ in range(n)]
        self.ring = [wires.slot() for _ in range(6)]
        self.near = [wires.slot() for _ in range(2 * n)]
        self.gather = Gather(place, wires, self.final_view)

    def span(self, first, count):
        return pl.ds(pl.multiple_of(first * self.rows, 16), count * self.rows)

    def view(self, first, count):
        return self.grads.at[self.seg, :, self.span(first, count)]

    def final_view(self, first, count):
        return self.final.at[self.seg, self.span(first, count)]

    def base(self, step):
        p = self.place
        return (p.k * p.n + lax.rem(p.major + step, p.n)) * p.n

    def add(self, first, count, arrivals):
        kind = BF16 if len(arrivals) == 1 else F32
        size = count * self.rows
        base, chunk = first * self.rows, 96

        def step(i, carry):
            at = pl.ds(pl.multiple_of(base + i * chunk, 16), chunk)
            total = self.grads[self.seg, :, at].astype(kind)
            for ref, start in arrivals:
                here = pl.ds(pl.multiple_of(start * self.rows + i * chunk, 16), chunk)
                total = total + ref[:, here].astype(kind)
            self.grads[self.seg, :, at] = total.astype(BF16)
            return carry

        lax.fori_loop(0, size // chunk, step, 0)

    def to_core(self):
        p, n = self.place, self.place.n
        for step in (2, 1, 3, 0) if n > 1 else (0,):
            block = lax.rem(p.minor + step, n)
            self.wires.send(
                self.core[step],
                self.view(((1 - p.k) * n + block) * n, n),
                self.from_core.at[self.seg, :, self.span(block * n, n)],
                p.sibling(),
            )

    def add_core(self, step):
        p, n = self.place, self.place.n
        block = lax.rem(p.major + step, n)
        landed = self.from_core.at[self.seg, :, self.span(block * n, n)]
        self.wires.arrived(self.core[step], landed, p.sibling())
        self.add(self.base(step), n, [(self.from_core.at[self.seg], block * n)])

    def ring_send(self, piece, first, step):
        self.wires.send(
            self.ring[piece],
            self.view(first, 2),
            self.from_major.at[self.seg, piece],
            self.place.along_major(step),
        )

    def ring_arrived(self, piece, step):
        self.wires.arrived(
            self.ring[piece], self.from_major.at[self.seg, piece], self.place.along_major(step)
        )
        return (self.from_major.at[self.seg, piece], 0)

    def to_major(self):
        if self.place.n == 1:
            self.add_core(0)
            return
        far, after, before = self.base(2), self.base(1), self.base(3)
        self.add_core(2)
        self.ring_send(0, far, 1)
        self.ring_send(1, far + 2, 3)
        self.add_core(1)
        self.ring_send(3, after + 2, 1)
        self.add_core(3)
        self.ring_send(4, before, 3)

    def major_on(self):
        if self.place.n == 1:
            return
        after, before = self.base(1), self.base(3)
        self.add(after, 2, [self.ring_arrived(0, 3)])
        self.ring_send(2, after, 1)
        self.add(before + 2, 2, [self.ring_arrived(1, 1)])
        self.ring_send(5, before + 2, 3)
        self.add_core(0)

    def to_minor(self):
        p, w, n = self.place, self.wires, self.place.n
        row = self.base(0)
        if n > 1:
            second = [self.ring_arrived(3, 3)]
            first = [self.ring_arrived(4, 1)]
            first.append(self.ring_arrived(2, 3))
            self.add(row, 2, first)
            second.append(self.ring_arrived(5, 1))
            self.add(row + 2, 2, second)
        for side in (1, 0):
            half = 1 - p.c if side else p.c
            for step in range(1 - side, n):
                there = p.along_minor(step)
                there["col"] = half
                w.send(
                    self.near[side * n + step],
                    self.grads.at[
                        self.seg, half, self.span(row + lax.rem(p.minor + step, n), 1)
                    ],
                    self.from_minor.at[self.seg, side * n + step],
                    there,
                )

    def to_gather(self):
        p, w, n = self.place, self.wires, self.place.n
        total = self.grads[self.seg, p.c, self.span(p.shard, 1)].astype(F32)
        for side in (0, 1):
            for step in range(1 - side, n):
                landed = self.from_minor.at[self.seg, side * n + step]
                w.arrived(self.near[side * n + step], landed, p.along_minor(step))
                total = total + landed[...].astype(F32)
        self.final[self.seg, self.span(p.shard, 1)] = total.astype(BF16)
        self.gather.minor()


def kernel(
    n,
    x_ref,
    cot_ref,
    step_ref,
    label_ref,
    time_hbm,
    class_hbm,
    modulation_hbm,
    attention_hbm,
    projection_hbm,
    expansion_hbm,
    reduction_hbm,
    modulation_bias_ref,
    projection_bias_ref,
    narrowing_ref,
    attention_bias_ref,
    widening_ref,
    result_ref,
    xgrad_ref,
    final_hbm,
    rows_ref,
    silu_ref,
    condition_grad_ref,
    weights,
    tables_time,
    tables_class,
    modulation,
    ids_out,
    ids_in,
    modp,
    spread_rows,
    silu_out,
    silu_in,
    x_all,
    cot_all,
    mod_parts,
    mod,
    normed1,
    rstd1,
    hidden1,
    triple,
    probs,
    attended,
    send1,
    recv1,
    branch1,
    normed2,
    rstd2,
    hidden2,
    activated,
    slope,
    grad_b2,
    send2,
    recv2,
    grad_up,
    send3,
    recv3,
    grad_res,
    grad_b1,
    grad_att,
    grad_tri,
    send4,
    recv4,
    res_out,
    res_in,
    xg_out,
    xg_low,
    xg_in,
    payload_out,
    payload,
    grads,
    from_core,
    from_major,
    from_minor,
    final,
    send_sems,
    recv_sems,
    local_sems,
):
    place = Place(n)
    wires = Wires(send_sems, recv_sems)
    r, c, k, latent = place.r, place.c, place.k, place.latent

    own = [
        [
            pltpu.make_async_copy(
                attention_hbm.at[kind],
                weights.at[0, c, kind * HALF : (kind + 1) * HALF],
                local_sems.at[kind],
            )
            for kind in range(3)
        ]
        + [
            pltpu.make_async_copy(
                projection_hbm, weights.at[0, c, 3 * HALF : 4 * HALF], local_sems.at[3]
            )
        ],
        [
            pltpu.make_async_copy(
                expansion_hbm.at[:, block * HALF : (block + 1) * HALF],
                weights.at[1, c, block * HALF : (block + 1) * HALF],
                local_sems.at[4 + block],
            )
            for block in range(4)
        ],
        [pltpu.make_async_copy(reduction_hbm, weights.at[2, c], local_sems.at[8])],
    ]
    table_loads = [
        pltpu.make_async_copy(time_hbm, tables_time, local_sems.at[9]),
        pltpu.make_async_copy(class_hbm, tables_class, local_sems.at[10]),
    ]
    modulation_load = pltpu.make_async_copy(modulation_hbm, modulation, local_sems.at[11])
    for copy in own[0] + table_loads + [modulation_load] + own[1] + own[2]:
        copy.start()
    row_at = lax.broadcasted_iota(jnp.int32, (8, 128), 0)
    ids_out[...] = jnp.where(row_at == 0, step_ref[0], label_ref[0])

    barrier = pltpu.get_barrier_semaphore()
    others = [place.group(s) for s in (1, 2, 3)] + [place.sibling()]
    for step in range(1, n):
        others += [place.along_minor(step), place.along_major(step)]
        there = place.along_minor(step)
        there["col"] = 1 - c
        others.append(there)
    for other in others:
        pl.semaphore_signal(barrier, inc=1, device_id=other, device_id_type=MESH)
    pl.semaphore_wait(barrier, len(others))

    shard_rows = SEG // (2 * n * n)

    def weight_view(seg):
        def view(first, count):
            start = pl.multiple_of(first * shard_rows, 16)
            return weights.at[seg, 1 - c, pl.ds(start, count * shard_rows)]

        return view

    gathers = [Gather(place, wires, weight_view(seg)) for seg in range(3)]
    weight_slots = [wires.slot() for _ in range(3)]
    my_rows = pl.ds(pl.multiple_of(place.shard * shard_rows, 16), shard_rows)

    def weights_out(seg):
        for copy in own[seg]:
            copy.wait()
        mine = weights.at[seg, c, my_rows]
        wires.send(weight_slots[seg], mine, mine, place.column())

    def weights_minor(seg):
        wires.arrived(weight_slots[seg], weights.at[seg, 1 - c, my_rows], place.column())
        gathers[seg].minor()

    weights_out(0)
    ids_slot = wires.slot()
    wires.send(ids_slot, ids_out, ids_in, place.column())
    x_spread = Spread(place, wires, x_ref, x_all)
    weights_out(1)
    weights_out(2)

    def table_rows(steps, labels, count):
        lanes = lax.broadcasted_iota(jnp.int32, (count, STEPS), 1)
        class_lanes = lax.broadcasted_iota(jnp.int32, (count, CLASSES), 1)
        return dot((lanes == steps).astype(BF16), tables_time[...]) + dot(
            (class_lanes == labels).astype(BF16), tables_class[...]
        )

    weights_minor(0)
    wires.arrived(ids_slot, ids_in, place.column())
    x_spread.forward()
    latent_at = lax.broadcasted_iota(jnp.int32, (16, 1), 0)

    def by_latent(row):
        return jnp.where(
            latent_at == c,
            ids_out[row : row + 1, 0:1],
            jnp.where(latent_at == 1 - c, ids_in[row : row + 1, 0:1], -1),
        )

    for copy in table_loads:
        copy.wait()
    modulation_load.wait()
    group_condition = table_rows(by_latent(0), by_latent(1), 16)
    group_silu = (group_condition / (1.0 + jnp.exp(-group_condition))).astype(BF16)
    first_row = (r == 0).astype(F32)
    modulation_bias = modulation_bias_ref[...].astype(F32)
    for kind in range(6):
        part = dot(group_silu, modulation[kind])
        for lat in range(2):
            modp[lat, kind : kind + 1, :] = (
                part[lat : lat + 1, :] + first_row * modulation_bias[kind : kind + 1, :]
            )
    for lat in range(2):
        modp[lat, 6:7, :] = first_row * projection_bias_ref[...].astype(F32).reshape(1, HALF)
        modp[lat, 7:8, :] = first_row * narrowing_ref[...].astype(F32).reshape(1, HALF)
    mod_slots = [wires.slot() for _ in range(3)]
    for step in (1, 2, 3):
        there = place.group(step)
        its_latent = xor(there["col"], k * there["row"])
        wires.send(mod_slots[step - 1], modp.at[its_latent], mod_parts.at[step], there)

    gathers[0].major()
    for step in (1, 2, 3):
        wires.arrived(mod_slots[step - 1], mod_parts.at[step], place.group(step))
    mod[c] = modp[latent] + mod_parts[1]
    mod[1 - c] = mod_parts[2] + mod_parts[3]

    def vec(half, row):
        return mod[half, row : row + 1, :]

    def over_rows(body, init=0, part=None):
        def step(i, carry):
            return body(pl.ds(pl.multiple_of(i * ROWS, ROWS), ROWS), carry)

        steps = SEQ // ROWS
        first, last = (0, steps) if part is None else (part * steps // 2, (part + 1) * steps // 2)
        return lax.fori_loop(first, last, step, init)

    def part_rows(part):
        return pl.ds(part * PART, PART)

    def norm(values):
        average = (
            jnp.sum(values[0], axis=-1, keepdims=True) + jnp.sum(values[1], axis=-1, keepdims=True)
        ) * (1.0 / D)
        square = (
            jnp.sum(values[0] * values[0], axis=-1, keepdims=True)
            + jnp.sum(values[1] * values[1], axis=-1, keepdims=True)
        ) * (1.0 / D)
        inverse = lax.rsqrt(square - average * average + EPSILON)
        return [(v - average) * inverse for v in values], inverse

    def norm_back(grad, normed, inverse):
        average = (
            jnp.sum(grad[0], axis=-1, keepdims=True) + jnp.sum(grad[1], axis=-1, keepdims=True)
        ) * (1.0 / D)
        crossed = (
            jnp.sum(grad[0] * normed[0], axis=-1, keepdims=True)
            + jnp.sum(grad[1] * normed[1], axis=-1, keepdims=True)
        ) * (1.0 / D)
        return [inverse * (g - average - m * crossed) for g, m in zip(grad, normed)]

    def token_sum(v):
        return jnp.sum(v, axis=0, keepdims=True)

    gathers[0].major_on()
    x_spread.collect()
    cot_spread = Spread(place, wires, cot_ref, cot_all)

    def first_norm(rows, carry):
        normed, inverse = norm([x_all[h, rows].astype(F32) for h in range(2)])
        rstd1[rows] = inverse
        for h in range(2):
            normed1[h, rows] = normed[h]
            hidden1[h, rows] = (normed[h] * (1.0 + vec(h, 1)) + vec(h, 0)).astype(BF16)
        return carry

    weights_minor(1)
    over_rows(first_norm)
    gathers[0].cores()
    weights_minor(2)

    def weight(seg, half, block):
        return weights[seg, half, block * HALF : (block + 1) * HALF, :]

    for kind in range(3):
        slope[kind] = dot(hidden1[c], weight(0, c, kind))
    cot_spread.forward()
    gathers[1].major()
    gathers[0].finish()
    gathers[2].major()
    for kind in range(3):
        value = slope[kind] + dot(hidden1[1 - c], weight(0, 1 - c, kind))
        if kind != 1:
            value = value + attention_bias_ref[kind // 2 : kind // 2 + 1, :].astype(F32)
        triple[kind] = value.astype(BF16)
    gathers[1].major_on()

    low_lanes = lax.broadcasted_iota(jnp.int32, (SEQ, 128), 1) < HEAD_DIM

    def one_head(v, head):
        mask = low_lanes if head == 0 else jnp.logical_not(low_lanes)
        return jnp.where(mask, v, jnp.zeros_like(v))

    score_scale = HEAD_DIM ** (-0.5)

    def attend(pair):
        lanes = pl.ds(pair * 128, 128)
        query = triple[0, :, lanes] * BF16(score_scale)
        keys = triple[1, :, lanes]
        values = triple[2, :, lanes]
        mixed = []
        for head in range(2):
            scores = dot_nt(one_head(query, head), keys)
            exponent = jnp.exp(scores - jnp.max(scores, axis=-1, keepdims=True))
            total = jnp.sum(exponent, axis=-1, keepdims=True)
            weights_now = exponent * (1.0 / total)
            probs[2 * pair + head] = weights_now
            mixed.append(dot(weights_now.astype(BF16), values))
        attended[:, lanes] = jnp.where(low_lanes, mixed[0], mixed[1]).astype(BF16)

    attend(0)
    gathers[2].major_on()
    attend(1)
    gathers[1].cores()
    attend(2)
    gathers[2].cores()

    def exchange(part, out, landing, slots):
        rows = part_rows(part)
        wires.send(slots[part], out.at[:, rows], landing.at[:, rows], place.partner())

    def exchanged(part, landing, slots):
        wires.arrived(slots[part], landing.at[:, part_rows(part)], place.partner())

    slots1, slots2, slots3, slots4 = ([wires.slot() for _ in range(2)] for _ in range(4))
    for part in range(2):
        rows = part_rows(part)
        for half in range(2):
            send1[half, rows] = dot(attended[rows, :], weight(0, half, 3)).astype(BF16)
        exchange(part, send1, recv1, slots1)
    cot_spread.collect()
    zero = jnp.zeros((1, HALF), F32)

    def start_back(rows, carry):
        out = []
        for h in range(2):
            low = (cot_all[h, rows].astype(F32) * vec(h, 5)).astype(BF16)
            grad_b2[h, rows] = low
            out.append(carry[h] + token_sum(low.astype(F32)))
        return tuple(out)

    narrowing_sum = over_rows(start_back, (zero, zero))

    def second_norm(rows, carry):
        middle = []
        for h in range(2):
            branch = send1[h, rows].astype(F32) + recv1[h, rows].astype(F32) + vec(h, 6)
            branch1[h, rows] = branch
            middle.append(x_all[h, rows].astype(F32) + vec(h, 2) * branch)
        normed, inverse = norm(middle)
        rstd2[rows] = inverse
        for h in range(2):
            normed2[h, rows] = normed[h]
            hidden2[h, rows] = (normed[h] * (1.0 + vec(h, 4)) + vec(h, 3)).astype(BF16)
        return carry

    root = math.sqrt(2.0 / math.pi)
    widening_sum = [zero] * 4
    for part in range(2):
        rows = part_rows(part)
        exchanged(part, recv1, slots1)
        over_rows(second_norm, part=part)
        if part == 0:
            gathers[1].finish()
        for block in range(4):
            upper = dot(hidden2[0, rows], weight(1, 0, block)) + dot(
                hidden2[1, rows], weight(1, 1, block)
            )
            bias = widening_ref[block * HALF : (block + 1) * HALF].astype(F32)
            upper = upper + bias.reshape(1, HALF)
            squared = upper * upper
            bent = jnp.tanh(root * upper * (1.0 + 0.044715 * squared))
            half_up = 0.5 * (1.0 + bent)
            activated[block, rows] = (upper * half_up).astype(BF16)
            slope[block, rows] = half_up + (0.5 * root) * upper * (1.0 - bent * bent) * (
                1.0 + (3.0 * 0.044715) * squared
            )
        if part == 0:
            gathers[2].finish()
        for block in range(4):
            back = dot_nt(grad_b2[0, rows], weight(2, 0, block)) + dot_nt(
                grad_b2[1, rows], weight(2, 1, block)
            )
            low = (back * slope[block, rows]).astype(BF16)
            grad_up[block, rows] = low
            widening_sum[block] = widening_sum[block] + token_sum(low.astype(F32))
        for half in range(2):
            value = dot_nt(grad_up[0, rows], weight(1, half, 0))
            for block in range(1, 4):
                value = value + dot_nt(grad_up[block, rows], weight(1, half, block))
            send3[half, rows] = value.astype(BF16)
        exchange(part, send3, recv3, slots3)

    reduces = [
        Reduce(place, wires, seg, grads, from_core, from_major, from_minor, final)
        for seg in range(3)
    ]

    def keep_grad(seg, half, block, value):
        grads[seg, half, block * HALF : (block + 1) * HALF, :] = value.astype(BF16)

    for block in range(4):
        for half in range(2):
            keep_grad(2, half, block, dot_tn(activated[block], grad_b2[half]))
    reduces[2].to_core()
    for block in range(4):
        for half in range(2):
            keep_grad(1, half, block, dot_tn(hidden2[half], grad_up[block]))
    reduces[1].to_core()
    for part in range(2):
        rows = part_rows(part)
        for half in range(2):
            value = dot(activated[0, rows], weight(2, half, 0))
            for block in range(1, 4):
                value = value + dot(activated[block, rows], weight(2, half, block))
            send2[half, rows] = value.astype(BF16)
        exchange(part, send2, recv2, slots2)
    reduces[2].to_major()

    def second_back(rows, carry):
        shift, scale, gate, bias = (list(part) for part in carry)
        inverse = rstd2[rows]
        normed = [normed2[h, rows] for h in range(2)]
        scaled = []
        for h in range(2):
            grad = send3[h, rows].astype(F32) + recv3[h, rows].astype(F32)
            shift[h] = shift[h] + token_sum(grad)
            scale[h] = scale[h] + token_sum(grad * normed[h])
            scaled.append(grad * (1.0 + vec(h, 4)))
        back = norm_back(scaled, normed, inverse)
        for h in range(2):
            total = cot_all[h, rows].astype(F32) + back[h]
            grad_res[h, rows] = total
            gate[h] = gate[h] + token_sum(total * branch1[h, rows])
            low = (total * vec(h, 2)).astype(BF16)
            grad_b1[h, rows] = low
            bias[h] = bias[h] + token_sum(low.astype(F32))
        return tuple(shift), tuple(scale), tuple(gate), tuple(bias)

    pair_zero = (zero, zero)
    sums2 = (pair_zero,) * 4
    for part in range(2):
        rows = part_rows(part)
        exchanged(part, recv3, slots3)
        sums2 = over_rows(second_back, sums2, part)
        grad_att[rows, :] = (
            dot_nt(grad_b1[0, rows], weight(0, 0, 3)) + dot_nt(grad_b1[1, rows], weight(0, 1, 3))
        ).astype(BF16)
    shift2, scale2, gate1, projection_sum = sums2
    for half in range(2):
        keep_grad(0, half, 3, dot_tn(attended[...], grad_b1[half]))

    def attend_back(pair):
        lanes = pl.ds(pair * 128, 128)
        query = triple[0, :, lanes] * BF16(score_scale)
        keys = triple[1, :, lanes]
        values = triple[2, :, lanes]
        above = grad_att[:, lanes]
        by_query, by_keys, by_values = [], [], []
        for head in range(2):
            weights_now = probs[2 * pair + head]
            grad_probs = dot_nt(one_head(above, head), values)
            by_values.append(dot_tn(weights_now.astype(BF16), above))
            crossed = jnp.sum(grad_probs * weights_now, axis=-1, keepdims=True)
            low = (weights_now * (grad_probs - crossed)).astype(BF16)
            by_query.append(dot(low, keys) * score_scale)
            by_keys.append(dot_tn(low, query))
        for kind, parts in enumerate((by_query, by_keys, by_values)):
            grad_tri[kind, :, lanes] = jnp.where(low_lanes, parts[0], parts[1]).astype(BF16)

    reduces[2].major_on()
    attend_back(0)
    reduces[1].to_major()
    exchanged(0, recv2, slots2)
    exchanged(1, recv2, slots2)
    mine = r == latent
    self_col = xor(latent, k * latent)
    out_half = c * (r == latent).astype(jnp.int32) + (1 - self_col) * (r != latent).astype(jnp.int32)
    across = place.at(row=latent, col=1 - self_col)
    back_from = place.at(row=1 - r, col=xor(r, k * (1 - r)))

    def branch_end(rows, carry):
        gate = list(carry)
        for h in range(2):
            branch = send2[h, rows].astype(F32) + recv2[h, rows].astype(F32) + vec(h, 7)
            gate[h] = gate[h] + token_sum(cot_all[h, rows].astype(F32) * branch)
            middle = x_all[h, rows].astype(F32) + vec(h, 2) * branch1[h, rows]
            res_out[h, rows] = (middle + vec(h, 5) * branch).astype(BF16)
        return tuple(gate)

    gate2 = over_rows(branch_end, pair_zero)
    res_slot, xg_slot = wires.slot(), wires.slot()

    @pl.when(jnp.logical_not(mine))
    def _():
        wires.copy(res_slot, res_out.at[out_half], res_in, across).start()

    attend_back(1)
    reduces[2].to_minor()
    attend_back(2)
    reduces[1].major_on()
    for half in range(2):
        for kind in range(3):
            keep_grad(0, half, kind, dot_tn(hidden1[half], grad_tri[kind]))
    reduces[0].to_core()
    for part in range(2):
        rows = part_rows(part)
        for half in range(2):
            value = dot_nt(grad_tri[0, rows], weight(0, half, 0))
            for kind in range(1, 3):
                value = value + dot_nt(grad_tri[kind, rows], weight(0, half, kind))
            send4[half, rows] = value.astype(BF16)
        exchange(part, send4, recv4, slots4)
    reduces[2].to_gather()
    reduces[1].to_minor()
    reduces[0].to_major()
    reduces[2].gather.major()

    def first_back(rows, carry):
        shift, scale = (list(part) for part in carry)
        inverse = rstd1[rows]
        normed = [normed1[h, rows] for h in range(2)]
        scaled = []
        for h in range(2):
            grad = send4[h, rows].astype(F32) + recv4[h, rows].astype(F32)
            shift[h] = shift[h] + token_sum(grad)
            scale[h] = scale[h] + token_sum(grad * normed[h])
            scaled.append(grad * (1.0 + vec(h, 1)))
        back = norm_back(scaled, normed, inverse)
        for h in range(2):
            total = grad_res[h, rows] + back[h]
            xg_out[h, rows] = total
            xg_low[h, rows] = total.astype(BF16)
        return tuple(shift), tuple(scale)

    sums1 = (pair_zero,) * 2
    for part in range(2):
        exchanged(part, recv4, slots4)
        sums1 = over_rows(first_back, sums1, part)
        if part == 0:
            reduces[0].major_on()
    shift1, scale1 = sums1

    def sums(kind):
        return token_sum(grad_tri[kind].astype(F32))

    shared = [sums(0), sums(2)] + widening_sum
    digit = lax.broadcasted_iota(jnp.int32, (1, HALF), 1) < 128
    for row in range(2):
        picked = jnp.where(latent == c, ids_out[row : row + 1, 0:1], ids_in[row : row + 1, 0:1])
        high = lax.shift_right_logical(picked, 5)
        shared.append(jnp.where(digit, high, picked - 32 * high).astype(F32))
    for h in range(2):
        own_rows = [shift1[h], scale1[h], gate1[h], shift2[h], scale2[h], gate2[h]]
        own_rows += [projection_sum[h], narrowing_sum[h]]
        payload_out[h] = jnp.concatenate(own_rows + shared, axis=0).astype(BF16)
    payload_slot = wires.slot()
    spot = 2 * place.shard + latent
    wires.send(payload_slot, payload_out.at[1 - c], payload.at[spot], place.column())
    payload[spot] = payload_out[c]

    def payload_view(first, count):
        return payload.at[pl.ds(2 * first, 2 * count)]

    payloads = Gather(place, wires, payload_view)
    reduces[0].to_minor()
    wires.arrived(payload_slot, payload.at[2 * place.shard + 1 - latent], place.column())
    payloads.minor()

    @pl.when(jnp.logical_not(mine))
    def _():
        wires.copy(xg_slot, xg_low.at[out_half], xg_in, across).start()

    reduces[1].to_gather()
    reduces[2].gather.major_on()
    payloads.major()
    reduces[0].to_gather()
    payloads.major_on()
    reduces[1].gather.major()
    reduces[2].gather.cores()
    reduces[0].gather.major()
    payloads.cores()
    reduces[1].gather.major_on()
    reduces[0].gather.major_on()
    payloads.finish()

    count = 4 * n * n
    for lat in range(count):
        for part in range(3):
            spread_rows[part, pl.ds(16 * lat, 16), :] = payload[
                lat, :, part * 128 : (part + 1) * 128
            ].astype(F32)
    for kind in range(16):
        for part in range(3):
            rows_ref[kind, :, part * 128 : (part + 1) * 128] = spread_rows[
                part, pl.ds(kind, count, stride=16), :
            ].astype(BF16)
    reduces[1].gather.cores()
    reduces[0].gather.cores()
    value = dot_nt(rows_ref[0], modulation[0])
    for kind in range(1, 6):
        value = value + dot_nt(rows_ref[kind], modulation[kind])
    silu_out[...] = value
    silu_slot = wires.slot()
    wires.send(silu_slot, silu_out, silu_in, place.column())

    reduces[2].gather.finish()
    outs = [
        pltpu.make_async_copy(final.at[seg], final_hbm.at[seg], local_sems.at[12 + seg])
        for seg in range(3)
    ]
    outs[2].start()

    def decode(kind):
        both = rows_ref[kind].astype(F32)
        return (32.0 * both[:, 0:1] + both[:, 128:129]).astype(jnp.int32)

    condition = table_rows(decode(14), decode(15), count)
    sigmoid = 1.0 / (1.0 + jnp.exp(-condition))
    silu_ref[...] = (condition * sigmoid).astype(BF16)
    reduces[1].gather.finish()
    outs[1].start()
    reduces[0].gather.finish()
    outs[0].start()
    wires.arrived(silu_slot, silu_in, place.column())
    condition_grad_ref[...] = (silu_out[...] + silu_in[...]) * (
        sigmoid * (1.0 + condition * (1.0 - sigmoid))
    )

    @pl.when(mine)
    def _():
        result_ref[...] = res_out[out_half]
        xgrad_ref[...] = xg_out[out_half]

    @pl.when(jnp.logical_not(mine))
    def _():
        wires.copy(res_slot, res_out.at[out_half], res_in, across).wait_send()
        wires.copy(res_slot, res_out.at[out_half], res_in, back_from).wait_recv()
        wires.copy(xg_slot, xg_low.at[out_half], xg_in, across).wait_send()
        wires.copy(xg_slot, xg_low.at[out_half], xg_in, back_from).wait_recv()
        result_ref[...] = res_in[...]
        xgrad_ref[...] = xg_in[...].astype(F32)

    x_spread.sent()
    cot_spread.sent()
    wires.drain()
    for out in outs:
        out.wait()


class Spread:
    def __init__(self, place, wires, source, landing):
        self.place, self.wires, self.landing = place, wires, landing
        r, c, k, latent = place.r, place.c, place.k, place.latent
        self.mine = r == latent
        self.far = 1 - xor(latent, k * latent)
        self.first, _, self.last = [wires.slot() for _ in range(3)]
        self.out = self.copy(
            source, c, self.first, self.first + c, place.at(row=1 - r, col=xor(r, k * (1 - r)))
        )
        self.forwarded = self.copy(
            landing.at[self.far], self.far, self.last, self.last, place.partner()
        )
        self.out.start()

        @pl.when(self.mine)
        def _():
            landing[c] = source[...]

    def copy(self, source, half, send_slot, recv_slot, there):
        return pltpu.make_async_remote_copy(
            src_ref=source,
            dst_ref=self.landing.at[half],
            send_sem=self.wires.send_sems.at[send_slot],
            recv_sem=self.wires.recv_sems.at[recv_slot],
            device_id=there,
            device_id_type=MESH,
        )

    def arrived(self, half, slot):
        self.copy(self.landing.at[half], half, self.last, slot, self.place.partner()).wait_recv()

    def forward(self):
        @pl.when(jnp.logical_not(self.mine))
        def _():
            self.arrived(self.far, self.first + self.far)
            self.forwarded.start()

    def collect(self):
        @pl.when(self.mine)
        def _():
            self.arrived(self.far, self.last)

        @pl.when(jnp.logical_not(self.mine))
        def _():
            self.arrived(1 - self.far, self.first + 1 - self.far)

    def sent(self):
        self.out.wait_send()

        @pl.when(jnp.logical_not(self.mine))
        def _():
            self.forwarded.wait_send()


def whole(shape, dtype):
    return pltpu.VMEM(shape, dtype)


def run_block(n, *operands):
    shards = 2 * n * n
    rows = SEG // shards
    tokens = (2, SEQ, HALF)
    vmem = pl.BlockSpec(memory_space=pltpu.VMEM)
    hbm = pl.BlockSpec(memory_space=pl.ANY)
    smem = pl.BlockSpec(memory_space=pltpu.SMEM)
    scratch = [
        whole((3, 2, SEG, HALF), BF16),
        whole((STEPS, HALF), BF16),
        whole((CLASSES, HALF), BF16),
        whole((6, HALF, HALF), BF16),
        whole((8, 128), jnp.int32),
        whole((8, 128), jnp.int32),
        whole((2, 8, HALF), F32),
        whole((3, 32 * shards, 128), F32),
        whole((2 * shards, HALF), F32),
        whole((2 * shards, HALF), F32),
        whole(tokens, BF16),
        whole(tokens, BF16),
        whole((4, 8, HALF), F32),
        whole((2, 8, HALF), F32),
        whole(tokens, F32),
        whole((SEQ, 1), F32),
        whole(tokens, BF16),
        whole((3, SEQ, HALF), BF16),
        whole((6, SEQ, SEQ), F32),
        whole((SEQ, HALF), BF16),
        whole(tokens, BF16),
        whole(tokens, BF16),
        whole(tokens, F32),
        whole(tokens, F32),
        whole((SEQ, 1), F32),
        whole(tokens, BF16),
        whole((4, SEQ, HALF), BF16),
        whole((4, SEQ, HALF), F32),
        whole(tokens, BF16),
        whole(tokens, BF16),
        whole(tokens, BF16),
        whole((4, SEQ, HALF), BF16),
        whole(tokens, BF16),
        whole(tokens, BF16),
        whole(tokens, F32),
        whole(tokens, BF16),
        whole((SEQ, HALF), BF16),
        whole((3, SEQ, HALF), BF16),
        whole(tokens, BF16),
        whole(tokens, BF16),
        whole(tokens, BF16),
        whole((SEQ, HALF), BF16),
        whole(tokens, F32),
        whole(tokens, BF16),
        whole((SEQ, HALF), BF16),
        whole((2, 16, HALF), BF16),
        whole((2 * shards, 16, HALF), BF16),
        whole((3, 2, SEG, HALF), BF16),
        whole((3, 2, SEG // 2, HALF), BF16),
        whole((3, 6, 2, 2 * rows, HALF), BF16),
        whole((3, 2 * n, rows, HALF), BF16),
        whole((3, SEG, HALF), BF16),
        pltpu.SemaphoreType.DMA((SEMS,)),
        pltpu.SemaphoreType.DMA((SEMS,)),
        pltpu.SemaphoreType.DMA((16,)),
    ]

    def body(*refs):
        kernel(n, *refs)

    return pl.pallas_call(
        body,
        out_shape=(
            jax.ShapeDtypeStruct((SEQ, HALF), BF16),
            jax.ShapeDtypeStruct((SEQ, HALF), F32),
            jax.ShapeDtypeStruct((3, SEG, HALF), BF16),
            jax.ShapeDtypeStruct((16, 2 * shards, HALF), BF16),
            jax.ShapeDtypeStruct((2 * shards, HALF), BF16),
            jax.ShapeDtypeStruct((2 * shards, HALF), F32),
        ),
        in_specs=[vmem, vmem, smem, smem] + [hbm] * 7 + [vmem] * 5,
        out_specs=(vmem, vmem, hbm, vmem, vmem, vmem),
        scratch_shapes=scratch,
        compiler_params=pltpu.CompilerParams(
            collective_id=0, has_side_effects=True, vmem_limit_bytes=60 * 1024 * 1024
        ),
        name="block",
    )(*operands)


def finish_kernel(
    result_in,
    xgrad_in,
    final_hbm,
    rows_ref,
    silu_ref,
    condition_grad_ref,
    result_ref,
    xgrad_ref,
    time_hbm,
    class_hbm,
    modulation_hbm,
    modulation_bias_ref,
    attention_hbm,
    attention_bias_ref,
    projection_hbm,
    projection_bias_ref,
    expansion_hbm,
    widening_ref,
    reduction_hbm,
    narrowing_ref,
    final,
    time_grad,
    class_grad,
    modulation_grad,
    wide,
    sems,
):
    loads = [pltpu.make_async_copy(final_hbm.at[seg], final.at[seg], sems.at[seg]) for seg in range(3)]
    for seg in (2, 1, 0):
        loads[seg].start()
    stores = []

    def store(source, target):
        copy = pltpu.make_async_copy(source, target, sems.at[3 + len(stores)])
        copy.start()
        stores.append(copy)

    result_ref[...] = result_in[...]
    xgrad_ref[...] = xgrad_in[...]
    silu = silu_ref[...].T
    for kind in range(6):
        modulation_grad[kind] = dot(silu, rows_ref[kind])
        store(modulation_grad.at[kind], modulation_hbm.at[kind])

    def widen(seg, block):
        at = pl.ds(block * HALF, HALF)
        wide[seg, at] = final[seg, at].astype(F32)
        return wide.at[seg, at]

    loads[2].wait()
    for block in range(4):
        store(widen(2, block), reduction_hbm.at[pl.ds(block * HALF, HALF)])
    loads[1].wait()
    for block in range(4):
        store(widen(1, block), expansion_hbm.at[:, pl.ds(block * HALF, HALF)])
    loads[0].wait()
    for block in range(3):
        store(widen(0, block), attention_hbm.at[block])
    store(widen(0, 3), projection_hbm)

    count = silu_ref.shape[0]
    grad = condition_grad_ref[...]
    high = grad.astype(BF16)
    rest = grad - high.astype(F32)
    middle = rest.astype(BF16)
    low = (rest - middle.astype(F32)).astype(BF16)

    def scatter(kind, size):
        both = rows_ref[kind].astype(F32)
        picked = (32.0 * both[:, 0:1] + both[:, 128:129]).astype(jnp.int32)
        onehot = (lax.broadcasted_iota(jnp.int32, (count, 1024), 1) == picked).astype(BF16)
        onehot = onehot.T
        return (dot(onehot, high) + dot(onehot, middle) + dot(onehot, low))[:size]

    time_grad[...] = scatter(14, STEPS)
    store(time_grad, time_hbm)
    class_grad[...] = scatter(15, CLASSES)
    store(class_grad, class_hbm)

    def total(kind):
        return jnp.sum(rows_ref[kind].astype(F32), axis=0, keepdims=True)

    for kind in range(6):
        modulation_bias_ref[kind : kind + 1, :] = total(kind)
    projection_bias_ref[...] = total(6).reshape(HALF)
    narrowing_ref[...] = total(7).reshape(HALF)
    for kind in range(2):
        attention_bias_ref[kind : kind + 1, :] = total(8 + kind)
    for block in range(4):
        widening_ref[block * HALF : (block + 1) * HALF] = total(10 + block).reshape(HALF)
    for copy in stores:
        copy.wait()


def finish(result, xgrad, final, rows, silu, condition_grad):
    vmem = pl.BlockSpec(memory_space=pltpu.VMEM)
    hbm = pl.BlockSpec(memory_space=pl.ANY)
    shapes = [
        ((SEQ, HALF), vmem),
        ((SEQ, HALF), vmem),
        ((STEPS, HALF), hbm),
        ((CLASSES, HALF), hbm),
        ((6, HALF, HALF), hbm),
        ((6, HALF), vmem),
        ((3, HALF, HALF), hbm),
        ((2, HALF), vmem),
        ((HALF, HALF), hbm),
        ((HALF,), vmem),
        ((HALF, SEG), hbm),
        ((SEG,), vmem),
        ((SEG, HALF), hbm),
        ((HALF,), vmem),
    ]
    return pl.pallas_call(
        finish_kernel,
        out_shape=tuple(
            jax.ShapeDtypeStruct(shape, BF16 if i == 0 else F32)
            for i, (shape, _) in enumerate(shapes)
        ),
        in_specs=[vmem, vmem, hbm, vmem, vmem, vmem],
        out_specs=tuple(spec for _, spec in shapes),
        scratch_shapes=[
            whole((3, SEG, HALF), BF16),
            whole((STEPS, HALF), F32),
            whole((CLASSES, HALF), F32),
            whole((6, HALF, HALF), F32),
            whole((3, SEG, HALF), F32),
            pltpu.SemaphoreType.DMA((24,)),
        ],
        compiler_params=pltpu.CompilerParams(vmem_limit_bytes=60 * 1024 * 1024),
        name="finish",
    )(result, xgrad, final, rows, silu, condition_grad)


def body(
    activations,
    timesteps,
    class_labels,
    time_table,
    class_table,
    modulation,
    modulation_bias,
    attention,
    attention_bias,
    projection,
    projection_bias,
    expansion,
    widening_bias,
    reduction,
    narrowing_bias,
    cotangent,
):
    n = math.isqrt(lax.axis_size("dp") // 2)
    result, activations_grad, final, rows, silu, condition_grad = run_block(
        n,
        activations,
        cotangent,
        timesteps,
        class_labels,
        time_table,
        class_table,
        jnp.swapaxes(modulation, 0, 1),
        jnp.swapaxes(attention, 0, 1),
        projection,
        expansion,
        reduction,
        modulation_bias,
        projection_bias,
        narrowing_bias,
        attention_bias,
        widening_bias,
    )
    (
        result,
        activations_grad,
        time_grad,
        class_grad,
        modulation_grad,
        modulation_bias_grad,
        attention_grad,
        attention_bias_grad,
        projection_grad,
        projection_bias_grad,
        expansion_grad,
        expansion_bias_grad,
        reduction_grad,
        reduction_bias_grad,
    ) = finish(result, activations_grad, final, rows, silu, condition_grad)
    return (
        result,
        activations_grad,
        time_grad,
        class_grad,
        jnp.swapaxes(modulation_grad, 0, 1),
        modulation_bias_grad,
        jnp.swapaxes(attention_grad, 0, 1),
        attention_bias_grad,
        projection_grad,
        projection_bias_grad,
        expansion_grad,
        expansion_bias_grad,
        reduction_grad,
        reduction_bias_grad,
    )


def solution(mesh):
    placed = (
        P(("dp", "row"), "col"),
        P(("dp", "col")),
        P(("dp", "col")),
        P(None, "row"),
        P(None, "row"),
        P("row", None, "col"),
        P(None, "col"),
        P("col", None, "row"),
        P(None, "row"),
        P("row", "col"),
        P("col"),
        P("col", "row"),
        P("row"),
        P("row", "col"),
        P("col"),
        P(("dp", "row"), "col"),
    )
    return jax.shard_map(
        body,
        mesh=mesh,
        in_specs=placed,
        out_specs=(
            P(("dp", "row"), "col"),
            P(("dp", "row"), "col"),
            P(None, "row"),
            P(None, "row"),
            P("row", None, "col"),
            P(None, "col"),
            P("col", None, "row"),
            P(None, "row"),
            P("row", "col"),
            P("col"),
            P("col", "row"),
            P("row"),
            P("row", "col"),
            P("col"),
        ),
        check_vma=False,
    )
```

```python
import math

import jax
import jax.numpy as jnp
from jax import lax
from jax.experimental import pallas as pl
from jax.experimental.pallas import tpu as pltpu
from jax.sharding import PartitionSpec as P

D = 768
HALF = 384
SEQ = 256
HEAD_DIM = 64
STEPS = 1000
CLASSES = 1001
SEG = 1536
EPSILON = 1e-06
ROWS = 32
PART = SEQ // 2
SEMS = 176
F32 = jnp.float32
BF16 = jnp.bfloat16
MESH = pl.DeviceIdType.MESH


def dot(u, v):
    return lax.dot_general(u, v, (((1,), (0,)), ((), ())), preferred_element_type=F32)


def dot_nt(u, v):
    return lax.dot_general(u, v, (((1,), (1,)), ((), ())), preferred_element_type=F32)


def dot_tn(u, v):
    return lax.dot_general(u, v, (((0,), (0,)), ((), ())), preferred_element_type=F32)


def xor(u, v):
    return u + v - 2 * u * v


class Place:
    def __init__(self, n):
        self.n = n
        self.dp = lax.axis_index("dp")
        self.r = lax.axis_index("row")
        self.c = lax.axis_index("col")
        self.k = lax.rem(self.dp, 2)
        chip = lax.div(self.dp, 2)
        z = lax.rem(chip, n)
        x = lax.div(chip, n)
        self.major = x * (1 - self.k) + z * self.k
        self.minor = z * (1 - self.k) + x * self.k
        self.shard = (self.k * n + self.major) * n + self.minor
        self.latent = xor(self.c, self.k * self.r)

    def at(self, dp=None, row=None, col=None):
        return {
            "dp": self.dp if dp is None else dp,
            "row": self.r if row is None else row,
            "col": self.c if col is None else col,
        }

    def plane(self, major, minor):
        x = major * (1 - self.k) + minor * self.k
        z = minor * (1 - self.k) + major * self.k
        return self.at(dp=(x * self.n + z) * 2 + self.k)

    def along_minor(self, step):
        return self.plane(self.major, lax.rem(self.minor + step, self.n))

    def along_major(self, step):
        return self.plane(lax.rem(self.major + step, self.n), self.minor)

    def sibling(self):
        return self.at(dp=self.dp + 1 - 2 * self.k)

    def group(self, step):
        row = xor(self.r, step & 1)
        col = xor(self.c, step >> 1)
        return self.at(row=row, col=col)

    def partner(self):
        return self.at(row=1 - self.r, col=xor(self.c, self.k))

    def column(self):
        return self.at(col=1 - self.c)


class Wires:
    def __init__(self, send_sems, recv_sems):
        self.send_sems, self.recv_sems = send_sems, recv_sems
        self.used = 0
        self.sent = []

    def slot(self):
        self.used += 1
        assert self.used <= SEMS
        return self.used - 1

    def copy(self, slot, src, dst, device):
        return pltpu.make_async_remote_copy(
            src_ref=src,
            dst_ref=dst,
            send_sem=self.send_sems.at[slot],
            recv_sem=self.recv_sems.at[slot],
            device_id=device,
            device_id_type=MESH,
        )

    def send(self, slot, src, dst, device):
        copy = self.copy(slot, src, dst, device)
        copy.start()
        self.sent.append(copy)

    def arrived(self, slot, dst, device):
        self.copy(slot, dst, dst, device).wait_recv()

    def drain(self):
        for copy in self.sent:
            copy.wait_send()


class Gather:
    def __init__(self, place, wires, view):
        self.place, self.wires, self.view = place, wires, view
        self.near = [wires.slot() for _ in range(place.n - 1)]
        self.ring = [wires.slot() for _ in range(4)]
        self.core = [wires.slot() for _ in range(4)]

    def base(self, step, core=None):
        p = self.place
        own = core is None
        k, major = (p.k, p.major) if own else (core, p.minor)
        return (k * p.n + lax.rem(major + step, p.n)) * p.n

    def to_sibling(self, step):
        n = self.place.n
        mine = self.view(self.base(step), n)
        self.wires.send(self.core[step], mine, mine, self.place.sibling())

    def minor(self):
        p, w, n = self.place, self.wires, self.place.n
        mine = self.view(p.shard, 1)
        for step in range(1, n):
            w.send(self.near[step - 1], mine, mine, p.along_minor(step))

    def major(self):
        p, w, n = self.place, self.wires, self.place.n
        row = self.base(0)
        for step in range(1, n):
            other = lax.rem(p.minor + n - step, n)
            w.arrived(self.near[step - 1], self.view(row + other, 1), p.along_minor(step))
        if n > 1:
            mine = self.view(row, n)
            w.send(self.ring[0], mine, mine, p.along_major(1))
            w.send(self.ring[1], mine, mine, p.along_major(3))
        self.to_sibling(0)

    def major_on(self):
        p, w, n = self.place, self.wires, self.place.n
        if n == 1:
            return
        before, after = self.base(3), self.base(1)
        w.arrived(self.ring[0], self.view(before, n), p.along_major(3))
        half = self.view(before, 2)
        w.send(self.ring[2], half, half, p.along_major(1))
        w.arrived(self.ring[1], self.view(after, n), p.along_major(1))
        half = self.view(after + 2, 2)
        w.send(self.ring[3], half, half, p.along_major(3))
        self.to_sibling(3)
        self.to_sibling(1)

    def cores(self):
        p, w, n = self.place, self.wires, self.place.n
        if n == 1:
            return
        far = self.base(2)
        w.arrived(self.ring[2], self.view(far, 2), p.along_major(3))
        w.arrived(self.ring[3], self.view(far + 2, 2), p.along_major(1))
        self.to_sibling(2)

    def finish(self):
        p, w, n = self.place, self.wires, self.place.n
        for step in range(n):
            w.arrived(self.core[step], self.view(self.base(step, 1 - p.k), n), p.sibling())


class Reduce:
    def __init__(self, place, wires, seg, grads, from_core, from_major, from_minor, final):
        self.place, self.wires, self.seg = place, wires, seg
        self.grads, self.final = grads, final
        self.from_core, self.from_major = from_core, from_major
        self.from_minor = from_minor
        n = place.n
        self.rows = SEG // (2 * n * n)
        self.core = [wires.slot() for _ in range(n)]
        self.ring = [wires.slot() for _ in range(6)]
        self.near = [wires.slot() for _ in range(2 * n)]
        self.gather = Gather(place, wires, self.final_view)

    def span(self, first, count):
        return pl.ds(pl.multiple_of(first * self.rows, 16), count * self.rows)

    def view(self, first, count):
        return self.grads.at[self.seg, :, self.span(first, count)]

    def final_view(self, first, count):
        return self.final.at[self.seg, self.span(first, count)]

    def base(self, step):
        p = self.place
        return (p.k * p.n + lax.rem(p.major + step, p.n)) * p.n

    def add(self, first, count, arrivals):
        kind = BF16 if len(arrivals) == 1 else F32
        size = count * self.rows
        base, chunk = first * self.rows, 96

        def step(i, carry):
            at = pl.ds(pl.multiple_of(base + i * chunk, 16), chunk)
            total = self.grads[self.seg, :, at].astype(kind)
            for ref, start in arrivals:
                here = pl.ds(pl.multiple_of(start * self.rows + i * chunk, 16), chunk)
                total = total + ref[:, here].astype(kind)
            self.grads[self.seg, :, at] = total.astype(BF16)
            return carry

        lax.fori_loop(0, size // chunk, step, 0)

    def to_core(self):
        p, n = self.place, self.place.n
        for step in (2, 1, 3, 0) if n > 1 else (0,):
            block = lax.rem(p.minor + step, n)
            self.wires.send(
                self.core[step],
                self.view(((1 - p.k) * n + block) * n, n),
                self.from_core.at[self.seg, :, self.span(block * n, n)],
                p.sibling(),
            )

    def add_core(self, step):
        p, n = self.place, self.place.n
        block = lax.rem(p.major + step, n)
        landed = self.from_core.at[self.seg, :, self.span(block * n, n)]
        self.wires.arrived(self.core[step], landed, p.sibling())
        self.add(self.base(step), n, [(self.from_core.at[self.seg], block * n)])

    def ring_send(self, piece, first, step):
        self.wires.send(
            self.ring[piece],
            self.view(first, 2),
            self.from_major.at[self.seg, piece],
            self.place.along_major(step),
        )

    def ring_arrived(self, piece, step):
        self.wires.arrived(
            self.ring[piece], self.from_major.at[self.seg, piece], self.place.along_major(step)
        )
        return (self.from_major.at[self.seg, piece], 0)

    def to_major(self):
        if self.place.n == 1:
            self.add_core(0)
            return
        far, after, before = self.base(2), self.base(1), self.base(3)
        self.add_core(2)
        self.ring_send(0, far, 1)
        self.ring_send(1, far + 2, 3)
        self.add_core(1)
        self.ring_send(3, after + 2, 1)
        self.add_core(3)
        self.ring_send(4, before, 3)

    def major_on(self):
        if self.place.n == 1:
            return
        after, before = self.base(1), self.base(3)
        self.add(after, 2, [self.ring_arrived(0, 3)])
        self.ring_send(2, after, 1)
        self.add(before + 2, 2, [self.ring_arrived(1, 1)])
        self.ring_send(5, before + 2, 3)
        self.add_core(0)

    def to_minor(self):
        p, w, n = self.place, self.wires, self.place.n
        row = self.base(0)
        if n > 1:
            second = [self.ring_arrived(3, 3)]
            first = [self.ring_arrived(4, 1)]
            first.append(self.ring_arrived(2, 3))
            self.add(row, 2, first)
            second.append(self.ring_arrived(5, 1))
            self.add(row + 2, 2, second)
        for side in (1, 0):
            half = 1 - p.c if side else p.c
            for step in range(1 - side, n):
                there = p.along_minor(step)
                there["col"] = half
                w.send(
                    self.near[side * n + step],
                    self.grads.at[
                        self.seg, half, self.span(row + lax.rem(p.minor + step, n), 1)
                    ],
                    self.from_minor.at[self.seg, side * n + step],
                    there,
                )

    def to_gather(self):
        p, w, n = self.place, self.wires, self.place.n
        total = self.grads[self.seg, p.c, self.span(p.shard, 1)].astype(F32)
        for side in (0, 1):
            for step in range(1 - side, n):
                landed = self.from_minor.at[self.seg, side * n + step]
                w.arrived(self.near[side * n + step], landed, p.along_minor(step))
                total = total + landed[...].astype(F32)
        self.final[self.seg, self.span(p.shard, 1)] = total.astype(BF16)
        self.gather.minor()


def kernel(
    n,
    x_ref,
    cot_ref,
    step_ref,
    label_ref,
    time_hbm,
    class_hbm,
    modulation_hbm,
    attention_hbm,
    projection_hbm,
    expansion_hbm,
    reduction_hbm,
    modulation_bias_ref,
    projection_bias_ref,
    narrowing_ref,
    attention_bias_ref,
    widening_ref,
    result_ref,
    xgrad_ref,
    final_hbm,
    rows_ref,
    silu_ref,
    condition_grad_ref,
    weights,
    tables_time,
    tables_class,
    modulation,
    ids_out,
    ids_in,
    modp,
    spread_rows,
    silu_out,
    silu_in,
    x_all,
    cot_all,
    mod_parts,
    mod,
    normed1,
    rstd1,
    hidden1,
    triple,
    probs,
    attended,
    send1,
    recv1,
    branch1,
    normed2,
    rstd2,
    hidden2,
    activated,
    slope,
    grad_b2,
    send2,
    recv2,
    grad_up,
    send3,
    recv3,
    grad_res,
    grad_b1,
    grad_att,
    grad_tri,
    send4,
    recv4,
    res_out,
    res_in,
    xg_out,
    xg_low,
    xg_in,
    payload_out,
    payload,
    grads,
    from_core,
    from_major,
    from_minor,
    final,
    send_sems,
    recv_sems,
    local_sems,
):
    place = Place(n)
    wires = Wires(send_sems, recv_sems)
    r, c, k, latent = place.r, place.c, place.k, place.latent

    own = [
        [
            pltpu.make_async_copy(
                attention_hbm.at[kind],
                weights.at[0, c, kind * HALF : (kind + 1) * HALF],
                local_sems.at[kind],
            )
            for kind in range(3)
        ]
        + [
            pltpu.make_async_copy(
                projection_hbm, weights.at[0, c, 3 * HALF : 4 * HALF], local_sems.at[3]
            )
        ],
        [
            pltpu.make_async_copy(
                expansion_hbm.at[:, block * HALF : (block + 1) * HALF],
                weights.at[1, c, block * HALF : (block + 1) * HALF],
                local_sems.at[4 + block],
            )
            for block in range(4)
        ],
        [pltpu.make_async_copy(reduction_hbm, weights.at[2, c], local_sems.at[8])],
    ]
    table_loads = [
        pltpu.make_async_copy(time_hbm, tables_time, local_sems.at[9]),
        pltpu.make_async_copy(class_hbm, tables_class, local_sems.at[10]),
    ]
    modulation_load = pltpu.make_async_copy(modulation_hbm, modulation, local_sems.at[11])
    for copy in own[0] + table_loads + [modulation_load] + own[1] + own[2]:
        copy.start()
    row_at = lax.broadcasted_iota(jnp.int32, (8, 128), 0)
    ids_out[...] = jnp.where(row_at == 0, step_ref[0], label_ref[0])

    barrier = pltpu.get_barrier_semaphore()
    others = [place.group(s) for s in (1, 2, 3)] + [place.sibling()]
    for step in range(1, n):
        others += [place.along_minor(step), place.along_major(step)]
        there = place.along_minor(step)
        there["col"] = 1 - c
        others.append(there)
    for other in others:
        pl.semaphore_signal(barrier, inc=1, device_id=other, device_id_type=MESH)
    pl.semaphore_wait(barrier, len(others))

    shard_rows = SEG // (2 * n * n)

    def weight_view(seg):
        def view(first, count):
            start = pl.multiple_of(first * shard_rows, 16)
            return weights.at[seg, 1 - c, pl.ds(start, count * shard_rows)]

        return view

    gathers = [Gather(place, wires, weight_view(seg)) for seg in range(3)]
    weight_slots = [wires.slot() for _ in range(3)]
    my_rows = pl.ds(pl.multiple_of(place.shard * shard_rows, 16), shard_rows)

    def weights_out(seg):
        for copy in own[seg]:
            copy.wait()
        mine = weights.at[seg, c, my_rows]
        wires.send(weight_slots[seg], mine, mine, place.column())

    def weights_minor(seg):
        wires.arrived(weight_slots[seg], weights.at[seg, 1 - c, my_rows], place.column())
        gathers[seg].minor()

    weights_out(0)
    ids_slot = wires.slot()
    wires.send(ids_slot, ids_out, ids_in, place.column())
    x_spread = Spread(place, wires, x_ref, x_all)
    weights_out(1)
    weights_out(2)

    def table_rows(steps, labels, count):
        lanes = lax.broadcasted_iota(jnp.int32, (count, STEPS), 1)
        class_lanes = lax.broadcasted_iota(jnp.int32, (count, CLASSES), 1)
        return dot((lanes == steps).astype(BF16), tables_time[...]) + dot(
            (class_lanes == labels).astype(BF16), tables_class[...]
        )

    weights_minor(0)
    wires.arrived(ids_slot, ids_in, place.column())
    x_spread.forward()
    latent_at = lax.broadcasted_iota(jnp.int32, (16, 1), 0)

    def by_latent(row):
        return jnp.where(
            latent_at == c,
            ids_out[row : row + 1, 0:1],
            jnp.where(latent_at == 1 - c, ids_in[row : row + 1, 0:1], -1),
        )

    for copy in table_loads:
        copy.wait()
    modulation_load.wait()
    group_condition = table_rows(by_latent(0), by_latent(1), 16)
    group_silu = (group_condition / (1.0 + jnp.exp(-group_condition))).astype(BF16)
    first_row = (r == 0).astype(F32)
    modulation_bias = modulation_bias_ref[...].astype(F32)
    for kind in range(6):
        part = dot(group_silu, modulation[kind])
        for lat in range(2):
            modp[lat, kind : kind + 1, :] = (
                part[lat : lat + 1, :] + first_row * modulation_bias[kind : kind + 1, :]
            )
    for lat in range(2):
        modp[lat, 6:7, :] = first_row * projection_bias_ref[...].astype(F32).reshape(1, HALF)
        modp[lat, 7:8, :] = first_row * narrowing_ref[...].astype(F32).reshape(1, HALF)
    mod_slots = [wires.slot() for _ in range(3)]
    for step in (1, 2, 3):
        there = place.group(step)
        its_latent = xor(there["col"], k * there["row"])
        wires.send(mod_slots[step - 1], modp.at[its_latent], mod_parts.at[step], there)

    gathers[0].major()
    for step in (1, 2, 3):
        wires.arrived(mod_slots[step - 1], mod_parts.at[step], place.group(step))
    mod[c] = modp[latent] + mod_parts[1]
    mod[1 - c] = mod_parts[2] + mod_parts[3]

    def vec(half, row):
        return mod[half, row : row + 1, :]

    def over_rows(body, init=0, part=None):
        def step(i, carry):
            return body(pl.ds(pl.multiple_of(i * ROWS, ROWS), ROWS), carry)

        steps = SEQ // ROWS
        first, last = (0, steps) if part is None else (part * steps // 2, (part + 1) * steps // 2)
        return lax.fori_loop(first, last, step, init)

    def part_rows(part):
        return pl.ds(part * PART, PART)

    def norm(values):
        average = (
            jnp.sum(values[0], axis=-1, keepdims=True) + jnp.sum(values[1], axis=-1, keepdims=True)
        ) * (1.0 / D)
        square = (
            jnp.sum(values[0] * values[0], axis=-1, keepdims=True)
            + jnp.sum(values[1] * values[1], axis=-1, keepdims=True)
        ) * (1.0 / D)
        inverse = lax.rsqrt(square - average * average + EPSILON)
        return [(v - average) * inverse for v in values], inverse

    def norm_back(grad, normed, inverse):
        average = (
            jnp.sum(grad[0], axis=-1, keepdims=True) + jnp.sum(grad[1], axis=-1, keepdims=True)
        ) * (1.0 / D)
        crossed = (
            jnp.sum(grad[0] * normed[0], axis=-1, keepdims=True)
            + jnp.sum(grad[1] * normed[1], axis=-1, keepdims=True)
        ) * (1.0 / D)
        return [inverse * (g - average - m * crossed) for g, m in zip(grad, normed)]

    def token_sum(v):
        return jnp.sum(v, axis=0, keepdims=True)

    gathers[0].major_on()
    x_spread.collect()
    cot_spread = Spread(place, wires, cot_ref, cot_all)

    def first_norm(rows, carry):
        normed, inverse = norm([x_all[h, rows].astype(F32) for h in range(2)])
        rstd1[rows] = inverse
        for h in range(2):
            normed1[h, rows] = normed[h]
            hidden1[h, rows] = (normed[h] * (1.0 + vec(h, 1)) + vec(h, 0)).astype(BF16)
        return carry

    weights_minor(1)
    over_rows(first_norm)
    gathers[0].cores()
    weights_minor(2)

    def weight(seg, half, block):
        return weights[seg, half, block * HALF : (block + 1) * HALF, :]

    for kind in range(3):
        slope[kind] = dot(hidden1[c], weight(0, c, kind))
    cot_spread.forward()
    gathers[1].major()
    gathers[0].finish()
    gathers[2].major()
    for kind in range(3):
        value = slope[kind] + dot(hidden1[1 - c], weight(0, 1 - c, kind))
        if kind != 1:
            value = value + attention_bias_ref[kind // 2 : kind // 2 + 1, :].astype(F32)
        triple[kind] = value.astype(BF16)
    gathers[1].major_on()

    low_lanes = lax.broadcasted_iota(jnp.int32, (SEQ, 128), 1) < HEAD_DIM

    def one_head(v, head):
        mask = low_lanes if head == 0 else jnp.logical_not(low_lanes)
        return jnp.where(mask, v, jnp.zeros_like(v))

    score_scale = HEAD_DIM ** (-0.5)

    def attend(pair):
        lanes = pl.ds(pair * 128, 128)
        query = triple[0, :, lanes] * BF16(score_scale)
        keys = triple[1, :, lanes]
        values = triple[2, :, lanes]
        mixed = []
        for head in range(2):
            scores = dot_nt(one_head(query, head), keys)
            exponent = jnp.exp(scores - jnp.max(scores, axis=-1, keepdims=True))
            total = jnp.sum(exponent, axis=-1, keepdims=True)
            weights_now = exponent * (1.0 / total)
            probs[2 * pair + head] = weights_now
            mixed.append(dot(weights_now.astype(BF16), values))
        attended[:, lanes] = jnp.where(low_lanes, mixed[0], mixed[1]).astype(BF16)

    attend(0)
    gathers[2].major_on()
    attend(1)
    gathers[1].cores()
    attend(2)
    gathers[2].cores()

    def exchange(part, out, landing, slots):
        rows = part_rows(part)
        wires.send(slots[part], out.at[:, rows], landing.at[:, rows], place.partner())

    def exchanged(part, landing, slots):
        wires.arrived(slots[part], landing.at[:, part_rows(part)], place.partner())

    slots1, slots2, slots3, slots4 = ([wires.slot() for _ in range(2)] for _ in range(4))
    for part in range(2):
        rows = part_rows(part)
        for half in range(2):
            send1[half, rows] = dot(attended[rows, :], weight(0, half, 3)).astype(BF16)
        exchange(part, send1, recv1, slots1)
    cot_spread.collect()
    zero = jnp.zeros((1, HALF), F32)

    def start_back(rows, carry):
        out = []
        for h in range(2):
            low = (cot_all[h, rows].astype(F32) * vec(h, 5)).astype(BF16)
            grad_b2[h, rows] = low
            out.append(carry[h] + token_sum(low.astype(F32)))
        return tuple(out)

    narrowing_sum = over_rows(start_back, (zero, zero))

    def second_norm(rows, carry):
        middle = []
        for h in range(2):
            branch = send1[h, rows].astype(F32) + recv1[h, rows].astype(F32) + vec(h, 6)
            branch1[h, rows] = branch
            middle.append(x_all[h, rows].astype(F32) + vec(h, 2) * branch)
        normed, inverse = norm(middle)
        rstd2[rows] = inverse
        for h in range(2):
            normed2[h, rows] = normed[h]
            hidden2[h, rows] = (normed[h] * (1.0 + vec(h, 4)) + vec(h, 3)).astype(BF16)
        return carry

    reduces = [
        Reduce(place, wires, seg, grads, from_core, from_major, from_minor, final)
        for seg in range(3)
    ]

    def keep_grad(seg, half, block, value):
        grads[seg, half, block * HALF : (block + 1) * HALF, :] = value.astype(BF16)

    root = math.sqrt(2.0 / math.pi)
    widening_sum = [zero] * 4
    for part in range(2):
        rows = part_rows(part)
        exchanged(part, recv1, slots1)
        over_rows(second_norm, part=part)
        if part == 0:
            gathers[1].finish()
        for block in range(4):
            upper = dot(hidden2[0, rows], weight(1, 0, block)) + dot(
                hidden2[1, rows], weight(1, 1, block)
            )
            bias = widening_ref[block * HALF : (block + 1) * HALF].astype(F32)
            upper = upper + bias.reshape(1, HALF)
            squared = upper * upper
            bent = jnp.tanh(root * upper * (1.0 + 0.044715 * squared))
            half_up = 0.5 * (1.0 + bent)
            activated[block, rows] = (upper * half_up).astype(BF16)
            slope[block, rows] = half_up + (0.5 * root) * upper * (1.0 - bent * bent) * (
                1.0 + (3.0 * 0.044715) * squared
            )
        if part == 0:
            gathers[2].finish()
        else:
            for block in range(4):
                for half in range(2):
                    keep_grad(2, half, block, dot_tn(activated[block], grad_b2[half]))
            reduces[2].to_core()
        for block in range(4):
            back = dot_nt(grad_b2[0, rows], weight(2, 0, block)) + dot_nt(
                grad_b2[1, rows], weight(2, 1, block)
            )
            low = (back * slope[block, rows]).astype(BF16)
            grad_up[block, rows] = low
            widening_sum[block] = widening_sum[block] + token_sum(low.astype(F32))
        for half in range(2):
            value = dot_nt(grad_up[0, rows], weight(1, half, 0))
            for block in range(1, 4):
                value = value + dot_nt(grad_up[block, rows], weight(1, half, block))
            send3[half, rows] = value.astype(BF16)
        exchange(part, send3, recv3, slots3)

    for block in range(4):
        for half in range(2):
            keep_grad(1, half, block, dot_tn(hidden2[half], grad_up[block]))
    reduces[1].to_core()
    reduces[2].to_major()
    for part in range(2):
        rows = part_rows(part)
        for half in range(2):
            value = dot(activated[0, rows], weight(2, half, 0))
            for block in range(1, 4):
                value = value + dot(activated[block, rows], weight(2, half, block))
            send2[half, rows] = value.astype(BF16)
        exchange(part, send2, recv2, slots2)

    def second_back(rows, carry):
        shift, scale, gate, bias = (list(part) for part in carry)
        inverse = rstd2[rows]
        normed = [normed2[h, rows] for h in range(2)]
        scaled = []
        for h in range(2):
            grad = send3[h, rows].astype(F32) + recv3[h, rows].astype(F32)
            shift[h] = shift[h] + token_sum(grad)
            scale[h] = scale[h] + token_sum(grad * normed[h])
            scaled.append(grad * (1.0 + vec(h, 4)))
        back = norm_back(scaled, normed, inverse)
        for h in range(2):
            total = cot_all[h, rows].astype(F32) + back[h]
            grad_res[h, rows] = total
            gate[h] = gate[h] + token_sum(total * branch1[h, rows])
            low = (total * vec(h, 2)).astype(BF16)
            grad_b1[h, rows] = low
            bias[h] = bias[h] + token_sum(low.astype(F32))
        return tuple(shift), tuple(scale), tuple(gate), tuple(bias)

    pair_zero = (zero, zero)
    sums2 = (pair_zero,) * 4
    for part in range(2):
        rows = part_rows(part)
        exchanged(part, recv3, slots3)
        sums2 = over_rows(second_back, sums2, part)
        grad_att[rows, :] = (
            dot_nt(grad_b1[0, rows], weight(0, 0, 3)) + dot_nt(grad_b1[1, rows], weight(0, 1, 3))
        ).astype(BF16)
    shift2, scale2, gate1, projection_sum = sums2
    for half in range(2):
        keep_grad(0, half, 3, dot_tn(attended[...], grad_b1[half]))

    def attend_back(pair):
        lanes = pl.ds(pair * 128, 128)
        query = triple[0, :, lanes] * BF16(score_scale)
        keys = triple[1, :, lanes]
        values = triple[2, :, lanes]
        above = grad_att[:, lanes]
        by_query, by_keys, by_values = [], [], []
        for head in range(2):
            weights_now = probs[2 * pair + head]
            grad_probs = dot_nt(one_head(above, head), values)
            by_values.append(dot_tn(weights_now.astype(BF16), above))
            crossed = jnp.sum(grad_probs * weights_now, axis=-1, keepdims=True)
            low = (weights_now * (grad_probs - crossed)).astype(BF16)
            by_query.append(dot(low, keys) * score_scale)
            by_keys.append(dot_tn(low, query))
        for kind, parts in enumerate((by_query, by_keys, by_values)):
            grad_tri[kind, :, lanes] = jnp.where(low_lanes, parts[0], parts[1]).astype(BF16)

    reduces[2].major_on()
    attend_back(0)
    reduces[1].to_major()
    exchanged(0, recv2, slots2)
    exchanged(1, recv2, slots2)
    mine = r == latent
    self_col = xor(latent, k * latent)
    out_half = c * (r == latent).astype(jnp.int32) + (1 - self_col) * (r != latent).astype(jnp.int32)
    across = place.at(row=latent, col=1 - self_col)
    back_from = place.at(row=1 - r, col=xor(r, k * (1 - r)))

    def branch_end(rows, carry):
        gate = list(carry)
        for h in range(2):
            branch = send2[h, rows].astype(F32) + recv2[h, rows].astype(F32) + vec(h, 7)
            gate[h] = gate[h] + token_sum(cot_all[h, rows].astype(F32) * branch)
            middle = x_all[h, rows].astype(F32) + vec(h, 2) * branch1[h, rows]
            res_out[h, rows] = (middle + vec(h, 5) * branch).astype(BF16)
        return tuple(gate)

    gate2 = over_rows(branch_end, pair_zero)
    res_slot, xg_slot = wires.slot(), wires.slot()

    @pl.when(jnp.logical_not(mine))
    def _():
        wires.copy(res_slot, res_out.at[out_half], res_in, across).start()

    attend_back(1)
    reduces[2].to_minor()
    attend_back(2)
    reduces[1].major_on()
    for half in range(2):
        for kind in range(3):
            keep_grad(0, half, kind, dot_tn(hidden1[half], grad_tri[kind]))
    reduces[0].to_core()
    for part in range(2):
        rows = part_rows(part)
        for half in range(2):
            value = dot_nt(grad_tri[0, rows], weight(0, half, 0))
            for kind in range(1, 3):
                value = value + dot_nt(grad_tri[kind, rows], weight(0, half, kind))
            send4[half, rows] = value.astype(BF16)
        exchange(part, send4, recv4, slots4)
    reduces[2].to_gather()
    reduces[1].to_minor()
    reduces[0].to_major()
    reduces[2].gather.major()

    def first_back(rows, carry):
        shift, scale = (list(part) for part in carry)
        inverse = rstd1[rows]
        normed = [normed1[h, rows] for h in range(2)]
        scaled = []
        for h in range(2):
            grad = send4[h, rows].astype(F32) + recv4[h, rows].astype(F32)
            shift[h] = shift[h] + token_sum(grad)
            scale[h] = scale[h] + token_sum(grad * normed[h])
            scaled.append(grad * (1.0 + vec(h, 1)))
        back = norm_back(scaled, normed, inverse)
        for h in range(2):
            total = grad_res[h, rows] + back[h]
            xg_out[h, rows] = total
            xg_low[h, rows] = total.astype(BF16)
        return tuple(shift), tuple(scale)

    sums1 = (pair_zero,) * 2
    for part in range(2):
        exchanged(part, recv4, slots4)
        sums1 = over_rows(first_back, sums1, part)
        if part == 0:
            reduces[0].major_on()
    shift1, scale1 = sums1

    def sums(kind):
        return token_sum(grad_tri[kind].astype(F32))

    shared = [sums(0), sums(2)] + widening_sum
    digit = lax.broadcasted_iota(jnp.int32, (1, HALF), 1) < 128
    for row in range(2):
        picked = jnp.where(latent == c, ids_out[row : row + 1, 0:1], ids_in[row : row + 1, 0:1])
        high = lax.shift_right_logical(picked, 5)
        shared.append(jnp.where(digit, high, picked - 32 * high).astype(F32))
    for h in range(2):
        own_rows = [shift1[h], scale1[h], gate1[h], shift2[h], scale2[h], gate2[h]]
        own_rows += [projection_sum[h], narrowing_sum[h]]
        payload_out[h] = jnp.concatenate(own_rows + shared, axis=0).astype(BF16)
    payload_slot = wires.slot()
    spot = 2 * place.shard + latent
    wires.send(payload_slot, payload_out.at[1 - c], payload.at[spot], place.column())
    payload[spot] = payload_out[c]

    def payload_view(first, count):
        return payload.at[pl.ds(2 * first, 2 * count)]

    payloads = Gather(place, wires, payload_view)
    reduces[0].to_minor()
    wires.arrived(payload_slot, payload.at[2 * place.shard + 1 - latent], place.column())
    payloads.minor()

    @pl.when(jnp.logical_not(mine))
    def _():
        wires.copy(xg_slot, xg_low.at[out_half], xg_in, across).start()

    reduces[1].to_gather()
    reduces[2].gather.major_on()
    payloads.major()
    reduces[0].to_gather()
    payloads.major_on()
    reduces[1].gather.major()
    reduces[2].gather.cores()
    reduces[0].gather.major()
    payloads.cores()
    reduces[1].gather.major_on()
    reduces[0].gather.major_on()
    payloads.finish()

    count = 4 * n * n
    for lat in range(count):
        for part in range(3):
            spread_rows[part, pl.ds(16 * lat, 16), :] = payload[
                lat, :, part * 128 : (part + 1) * 128
            ].astype(F32)
    for kind in range(16):
        for part in range(3):
            rows_ref[kind, :, part * 128 : (part + 1) * 128] = spread_rows[
                part, pl.ds(kind, count, stride=16), :
            ].astype(BF16)
    reduces[1].gather.cores()
    reduces[0].gather.cores()
    value = dot_nt(rows_ref[0], modulation[0])
    for kind in range(1, 6):
        value = value + dot_nt(rows_ref[kind], modulation[kind])
    silu_out[...] = value
    silu_slot = wires.slot()
    wires.send(silu_slot, silu_out, silu_in, place.column())

    reduces[2].gather.finish()
    outs = [
        pltpu.make_async_copy(final.at[seg], final_hbm.at[seg], local_sems.at[12 + seg])
        for seg in range(3)
    ]
    outs[2].start()

    def decode(kind):
        both = rows_ref[kind].astype(F32)
        return (32.0 * both[:, 0:1] + both[:, 128:129]).astype(jnp.int32)

    condition = table_rows(decode(14), decode(15), count)
    sigmoid = 1.0 / (1.0 + jnp.exp(-condition))
    silu_ref[...] = (condition * sigmoid).astype(BF16)
    reduces[1].gather.finish()
    outs[1].start()
    reduces[0].gather.finish()
    outs[0].start()
    wires.arrived(silu_slot, silu_in, place.column())
    condition_grad_ref[...] = (silu_out[...] + silu_in[...]) * (
        sigmoid * (1.0 + condition * (1.0 - sigmoid))
    )

    @pl.when(mine)
    def _():
        result_ref[...] = res_out[out_half]
        xgrad_ref[...] = xg_out[out_half]

    @pl.when(jnp.logical_not(mine))
    def _():
        wires.copy(res_slot, res_out.at[out_half], res_in, across).wait_send()
        wires.copy(res_slot, res_out.at[out_half], res_in, back_from).wait_recv()
        wires.copy(xg_slot, xg_low.at[out_half], xg_in, across).wait_send()
        wires.copy(xg_slot, xg_low.at[out_half], xg_in, back_from).wait_recv()
        result_ref[...] = res_in[...]
        xgrad_ref[...] = xg_in[...].astype(F32)

    x_spread.sent()
    cot_spread.sent()
    wires.drain()
    for out in outs:
        out.wait()


class Spread:
    def __init__(self, place, wires, source, landing):
        self.place, self.wires, self.landing = place, wires, landing
        r, c, k, latent = place.r, place.c, place.k, place.latent
        self.mine = r == latent
        self.far = 1 - xor(latent, k * latent)
        self.first, _, self.last = [wires.slot() for _ in range(3)]
        self.out = self.copy(
            source, c, self.first, self.first + c, place.at(row=1 - r, col=xor(r, k * (1 - r)))
        )
        self.forwarded = self.copy(
            landing.at[self.far], self.far, self.last, self.last, place.partner()
        )
        self.out.start()

        @pl.when(self.mine)
        def _():
            landing[c] = source[...]

    def copy(self, source, half, send_slot, recv_slot, there):
        return pltpu.make_async_remote_copy(
            src_ref=source,
            dst_ref=self.landing.at[half],
            send_sem=self.wires.send_sems.at[send_slot],
            recv_sem=self.wires.recv_sems.at[recv_slot],
            device_id=there,
            device_id_type=MESH,
        )

    def arrived(self, half, slot):
        self.copy(self.landing.at[half], half, self.last, slot, self.place.partner()).wait_recv()

    def forward(self):
        @pl.when(jnp.logical_not(self.mine))
        def _():
            self.arrived(self.far, self.first + self.far)
            self.forwarded.start()

    def collect(self):
        @pl.when(self.mine)
        def _():
            self.arrived(self.far, self.last)

        @pl.when(jnp.logical_not(self.mine))
        def _():
            self.arrived(1 - self.far, self.first + 1 - self.far)

    def sent(self):
        self.out.wait_send()

        @pl.when(jnp.logical_not(self.mine))
        def _():
            self.forwarded.wait_send()


def whole(shape, dtype):
    return pltpu.VMEM(shape, dtype)


def run_block(n, *operands):
    shards = 2 * n * n
    rows = SEG // shards
    tokens = (2, SEQ, HALF)
    vmem = pl.BlockSpec(memory_space=pltpu.VMEM)
    hbm = pl.BlockSpec(memory_space=pl.ANY)
    smem = pl.BlockSpec(memory_space=pltpu.SMEM)
    scratch = [
        whole((3, 2, SEG, HALF), BF16),
        whole((STEPS, HALF), BF16),
        whole((CLASSES, HALF), BF16),
        whole((6, HALF, HALF), BF16),
        whole((8, 128), jnp.int32),
        whole((8, 128), jnp.int32),
        whole((2, 8, HALF), F32),
        whole((3, 32 * shards, 128), F32),
        whole((2 * shards, HALF), F32),
        whole((2 * shards, HALF), F32),
        whole(tokens, BF16),
        whole(tokens, BF16),
        whole((4, 8, HALF), F32),
        whole((2, 8, HALF), F32),
        whole(tokens, F32),
        whole((SEQ, 1), F32),
        whole(tokens, BF16),
        whole((3, SEQ, HALF), BF16),
        whole((6, SEQ, SEQ), F32),
        whole((SEQ, HALF), BF16),
        whole(tokens, BF16),
        whole(tokens, BF16),
        whole(tokens, F32),
        whole(tokens, F32),
        whole((SEQ, 1), F32),
        whole(tokens, BF16),
        whole((4, SEQ, HALF), BF16),
        whole((4, SEQ, HALF), F32),
        whole(tokens, BF16),
        whole(tokens, BF16),
        whole(tokens, BF16),
        whole((4, SEQ, HALF), BF16),
        whole(tokens, BF16),
        whole(tokens, BF16),
        whole(tokens, F32),
        whole(tokens, BF16),
        whole((SEQ, HALF), BF16),
        whole((3, SEQ, HALF), BF16),
        whole(tokens, BF16),
        whole(tokens, BF16),
        whole(tokens, BF16),
        whole((SEQ, HALF), BF16),
        whole(tokens, F32),
        whole(tokens, BF16),
        whole((SEQ, HALF), BF16),
        whole((2, 16, HALF), BF16),
        whole((2 * shards, 16, HALF), BF16),
        whole((3, 2, SEG, HALF), BF16),
        whole((3, 2, SEG // 2, HALF), BF16),
        whole((3, 6, 2, 2 * rows, HALF), BF16),
        whole((3, 2 * n, rows, HALF), BF16),
        whole((3, SEG, HALF), BF16),
        pltpu.SemaphoreType.DMA((SEMS,)),
        pltpu.SemaphoreType.DMA((SEMS,)),
        pltpu.SemaphoreType.DMA((16,)),
    ]

    def body(*refs):
        kernel(n, *refs)

    return pl.pallas_call(
        body,
        out_shape=(
            jax.ShapeDtypeStruct((SEQ, HALF), BF16),
            jax.ShapeDtypeStruct((SEQ, HALF), F32),
            jax.ShapeDtypeStruct((3, SEG, HALF), BF16),
            jax.ShapeDtypeStruct((16, 2 * shards, HALF), BF16),
            jax.ShapeDtypeStruct((2 * shards, HALF), BF16),
            jax.ShapeDtypeStruct((2 * shards, HALF), F32),
        ),
        in_specs=[vmem, vmem, smem, smem] + [hbm] * 7 + [vmem] * 5,
        out_specs=(vmem, vmem, hbm, vmem, vmem, vmem),
        scratch_shapes=scratch,
        compiler_params=pltpu.CompilerParams(
            collective_id=0, has_side_effects=True, vmem_limit_bytes=60 * 1024 * 1024
        ),
        name="block",
    )(*operands)


def finish_kernel(
    result_in,
    xgrad_in,
    final_hbm,
    rows_ref,
    silu_ref,
    condition_grad_ref,
    result_ref,
    xgrad_ref,
    time_hbm,
    class_hbm,
    modulation_hbm,
    modulation_bias_ref,
    attention_hbm,
    attention_bias_ref,
    projection_hbm,
    projection_bias_ref,
    expansion_hbm,
    widening_ref,
    reduction_hbm,
    narrowing_ref,
    final,
    time_grad,
    class_grad,
    modulation_grad,
    wide,
    sems,
):
    loads = [
        [
            pltpu.make_async_copy(
                final_hbm.at[seg, pl.ds(block * HALF, HALF)],
                final.at[seg, pl.ds(block * HALF, HALF)],
                sems.at[24 + 4 * seg + block],
            )
            for block in range(4)
        ]
        for seg in range(3)
    ]
    for seg in (2, 1, 0):
        for load in loads[seg]:
            load.start()
    stores = []

    def store(source, target):
        copy = pltpu.make_async_copy(source, target, sems.at[3 + len(stores)])
        copy.start()
        stores.append(copy)

    result_ref[...] = result_in[...]
    xgrad_ref[...] = xgrad_in[...]
    silu = silu_ref[...].T
    for kind in range(6):
        modulation_grad[kind] = dot(silu, rows_ref[kind])
        store(modulation_grad.at[kind], modulation_hbm.at[kind])

    def widen(seg, block):
        loads[seg][block].wait()
        at = pl.ds(block * HALF, HALF)
        wide[seg, at] = final[seg, at].astype(F32)
        return wide.at[seg, at]

    for block in range(4):
        store(widen(2, block), reduction_hbm.at[pl.ds(block * HALF, HALF)])
    for block in range(4):
        store(widen(1, block), expansion_hbm.at[:, pl.ds(block * HALF, HALF)])
    for block in range(3):
        store(widen(0, block), attention_hbm.at[block])
    store(widen(0, 3), projection_hbm)

    count = silu_ref.shape[0]
    grad = condition_grad_ref[...]
    high = grad.astype(BF16)
    rest = grad - high.astype(F32)
    middle = rest.astype(BF16)
    low = (rest - middle.astype(F32)).astype(BF16)

    def scatter(kind, size):
        both = rows_ref[kind].astype(F32)
        picked = (32.0 * both[:, 0:1] + both[:, 128:129]).astype(jnp.int32)
        onehot = (lax.broadcasted_iota(jnp.int32, (count, 1024), 1) == picked).astype(BF16)
        onehot = onehot.T
        return (dot(onehot, high) + dot(onehot, middle) + dot(onehot, low))[:size]

    time_grad[...] = scatter(14, STEPS)
    store(time_grad, time_hbm)
    class_grad[...] = scatter(15, CLASSES)
    store(class_grad, class_hbm)

    def total(kind):
        return jnp.sum(rows_ref[kind].astype(F32), axis=0, keepdims=True)

    for kind in range(6):
        modulation_bias_ref[kind : kind + 1, :] = total(kind)
    projection_bias_ref[...] = total(6).reshape(HALF)
    narrowing_ref[...] = total(7).reshape(HALF)
    for kind in range(2):
        attention_bias_ref[kind : kind + 1, :] = total(8 + kind)
    for block in range(4):
        widening_ref[block * HALF : (block + 1) * HALF] = total(10 + block).reshape(HALF)
    for copy in stores:
        copy.wait()


def finish(result, xgrad, final, rows, silu, condition_grad):
    vmem = pl.BlockSpec(memory_space=pltpu.VMEM)
    hbm = pl.BlockSpec(memory_space=pl.ANY)
    shapes = [
        ((SEQ, HALF), vmem),
        ((SEQ, HALF), vmem),
        ((STEPS, HALF), hbm),
        ((CLASSES, HALF), hbm),
        ((6, HALF, HALF), hbm),
        ((6, HALF), vmem),
        ((3, HALF, HALF), hbm),
        ((2, HALF), vmem),
        ((HALF, HALF), hbm),
        ((HALF,), vmem),
        ((HALF, SEG), hbm),
        ((SEG,), vmem),
        ((SEG, HALF), hbm),
        ((HALF,), vmem),
    ]
    return pl.pallas_call(
        finish_kernel,
        out_shape=tuple(
            jax.ShapeDtypeStruct(shape, BF16 if i == 0 else F32)
            for i, (shape, _) in enumerate(shapes)
        ),
        in_specs=[vmem, vmem, hbm, vmem, vmem, vmem],
        out_specs=tuple(spec for _, spec in shapes),
        scratch_shapes=[
            whole((3, SEG, HALF), BF16),
            whole((STEPS, HALF), F32),
            whole((CLASSES, HALF), F32),
            whole((6, HALF, HALF), F32),
            whole((3, SEG, HALF), F32),
            pltpu.SemaphoreType.DMA((40,)),
        ],
        compiler_params=pltpu.CompilerParams(vmem_limit_bytes=60 * 1024 * 1024),
        name="finish",
    )(result, xgrad, final, rows, silu, condition_grad)


def body(
    activations,
    timesteps,
    class_labels,
    time_table,
    class_table,
    modulation,
    modulation_bias,
    attention,
    attention_bias,
    projection,
    projection_bias,
    expansion,
    widening_bias,
    reduction,
    narrowing_bias,
    cotangent,
):
    n = math.isqrt(lax.axis_size("dp") // 2)
    result, activations_grad, final, rows, silu, condition_grad = run_block(
        n,
        activations,
        cotangent,
        timesteps,
        class_labels,
        time_table,
        class_table,
        jnp.swapaxes(modulation, 0, 1),
        jnp.swapaxes(attention, 0, 1),
        projection,
        expansion,
        reduction,
        modulation_bias,
        projection_bias,
        narrowing_bias,
        attention_bias,
        widening_bias,
    )
    (
        result,
        activations_grad,
        time_grad,
        class_grad,
        modulation_grad,
        modulation_bias_grad,
        attention_grad,
        attention_bias_grad,
        projection_grad,
        projection_bias_grad,
        expansion_grad,
        expansion_bias_grad,
        reduction_grad,
        reduction_bias_grad,
    ) = finish(result, activations_grad, final, rows, silu, condition_grad)
    return (
        result,
        activations_grad,
        time_grad,
        class_grad,
        jnp.swapaxes(modulation_grad, 0, 1),
        modulation_bias_grad,
        jnp.swapaxes(attention_grad, 0, 1),
        attention_bias_grad,
        projection_grad,
        projection_bias_grad,
        expansion_grad,
        expansion_bias_grad,
        reduction_grad,
        reduction_bias_grad,
    )


def solution(mesh):
    placed = (
        P(("dp", "row"), "col"),
        P(("dp", "col")),
        P(("dp", "col")),
        P(None, "row"),
        P(None, "row"),
        P("row", None, "col"),
        P(None, "col"),
        P("col", None, "row"),
        P(None, "row"),
        P("row", "col"),
        P("col"),
        P("col", "row"),
        P("row"),
        P("row", "col"),
        P("col"),
        P(("dp", "row"), "col"),
    )
    return jax.shard_map(
        body,
        mesh=mesh,
        in_specs=placed,
        out_specs=(
            P(("dp", "row"), "col"),
            P(("dp", "row"), "col"),
            P(None, "row"),
            P(None, "row"),
            P("row", None, "col"),
            P(None, "col"),
            P("col", None, "row"),
            P(None, "row"),
            P("row", "col"),
            P("col"),
            P("col", "row"),
            P("row"),
            P("row", "col"),
            P("col"),
        ),
        check_vma=False,
    )
```

```python
import math

import jax
import jax.numpy as jnp
from jax import lax
from jax.experimental import pallas as pl
from jax.experimental.pallas import tpu as pltpu
from jax.sharding import PartitionSpec as P

D = 768
HALF = 384
SEQ = 256
HEAD_DIM = 64
STEPS = 1000
CLASSES = 1001
SEG = 1536
EPSILON = 1e-06
ROWS = 32
PART = SEQ // 2
SEMS = 176
F32 = jnp.float32
BF16 = jnp.bfloat16
MESH = pl.DeviceIdType.MESH


def dot(u, v):
    return lax.dot_general(u, v, (((1,), (0,)), ((), ())), preferred_element_type=F32)


def dot_nt(u, v):
    return lax.dot_general(u, v, (((1,), (1,)), ((), ())), preferred_element_type=F32)


def dot_tn(u, v):
    return lax.dot_general(u, v, (((0,), (0,)), ((), ())), preferred_element_type=F32)


def xor(u, v):
    return u + v - 2 * u * v


class Place:
    def __init__(self, n):
        self.n = n
        self.dp = lax.axis_index("dp")
        self.r = lax.axis_index("row")
        self.c = lax.axis_index("col")
        self.k = lax.rem(self.dp, 2)
        chip = lax.div(self.dp, 2)
        z = lax.rem(chip, n)
        x = lax.div(chip, n)
        self.major = x * (1 - self.k) + z * self.k
        self.minor = z * (1 - self.k) + x * self.k
        self.shard = (self.k * n + self.major) * n + self.minor
        self.latent = xor(self.c, self.k * self.r)

    def at(self, dp=None, row=None, col=None):
        return {
            "dp": self.dp if dp is None else dp,
            "row": self.r if row is None else row,
            "col": self.c if col is None else col,
        }

    def plane(self, major, minor):
        x = major * (1 - self.k) + minor * self.k
        z = minor * (1 - self.k) + major * self.k
        return self.at(dp=(x * self.n + z) * 2 + self.k)

    def along_minor(self, step):
        return self.plane(self.major, lax.rem(self.minor + step, self.n))

    def along_major(self, step):
        return self.plane(lax.rem(self.major + step, self.n), self.minor)

    def sibling(self):
        return self.at(dp=self.dp + 1 - 2 * self.k)

    def group(self, step):
        row = xor(self.r, step & 1)
        col = xor(self.c, step >> 1)
        return self.at(row=row, col=col)

    def partner(self):
        return self.at(row=1 - self.r, col=xor(self.c, self.k))

    def column(self):
        return self.at(col=1 - self.c)


class Wires:
    def __init__(self, send_sems, recv_sems):
        self.send_sems, self.recv_sems = send_sems, recv_sems
        self.used = 0
        self.sent = []

    def slot(self):
        self.used += 1
        assert self.used <= SEMS
        return self.used - 1

    def copy(self, slot, src, dst, device):
        return pltpu.make_async_remote_copy(
            src_ref=src,
            dst_ref=dst,
            send_sem=self.send_sems.at[slot],
            recv_sem=self.recv_sems.at[slot],
            device_id=device,
            device_id_type=MESH,
        )

    def send(self, slot, src, dst, device):
        copy = self.copy(slot, src, dst, device)
        copy.start()
        self.sent.append(copy)

    def arrived(self, slot, dst, device):
        self.copy(slot, dst, dst, device).wait_recv()

    def drain(self):
        for copy in self.sent:
            copy.wait_send()


class Gather:
    def __init__(self, place, wires, view):
        self.place, self.wires, self.view = place, wires, view
        self.near = [wires.slot() for _ in range(place.n - 1)]
        self.ring = [wires.slot() for _ in range(4)]
        self.core = [wires.slot() for _ in range(4)]

    def base(self, step, core=None):
        p = self.place
        own = core is None
        k, major = (p.k, p.major) if own else (core, p.minor)
        return (k * p.n + lax.rem(major + step, p.n)) * p.n

    def to_sibling(self, step):
        n = self.place.n
        mine = self.view(self.base(step), n)
        self.wires.send(self.core[step], mine, mine, self.place.sibling())

    def minor(self):
        p, w, n = self.place, self.wires, self.place.n
        mine = self.view(p.shard, 1)
        for step in range(1, n):
            w.send(self.near[step - 1], mine, mine, p.along_minor(step))

    def major(self):
        p, w, n = self.place, self.wires, self.place.n
        row = self.base(0)
        for step in range(1, n):
            other = lax.rem(p.minor + n - step, n)
            w.arrived(self.near[step - 1], self.view(row + other, 1), p.along_minor(step))
        if n > 1:
            mine = self.view(row, n)
            w.send(self.ring[0], mine, mine, p.along_major(1))
            w.send(self.ring[1], mine, mine, p.along_major(3))
        self.to_sibling(0)

    def major_on(self):
        p, w, n = self.place, self.wires, self.place.n
        if n == 1:
            return
        before, after = self.base(3), self.base(1)
        w.arrived(self.ring[0], self.view(before, n), p.along_major(3))
        half = self.view(before, 2)
        w.send(self.ring[2], half, half, p.along_major(1))
        w.arrived(self.ring[1], self.view(after, n), p.along_major(1))
        half = self.view(after + 2, 2)
        w.send(self.ring[3], half, half, p.along_major(3))
        self.to_sibling(3)
        self.to_sibling(1)

    def cores(self):
        p, w, n = self.place, self.wires, self.place.n
        if n == 1:
            return
        far = self.base(2)
        w.arrived(self.ring[2], self.view(far, 2), p.along_major(3))
        w.arrived(self.ring[3], self.view(far + 2, 2), p.along_major(1))
        self.to_sibling(2)

    def finish(self):
        p, w, n = self.place, self.wires, self.place.n
        for step in range(n):
            w.arrived(self.core[step], self.view(self.base(step, 1 - p.k), n), p.sibling())


class Reduce:
    def __init__(self, place, wires, seg, grads, from_core, from_major, from_minor, final):
        self.place, self.wires, self.seg = place, wires, seg
        self.grads, self.final = grads, final
        self.from_core, self.from_major = from_core, from_major
        self.from_minor = from_minor
        n = place.n
        self.rows = SEG // (2 * n * n)
        self.core = [wires.slot() for _ in range(n)]
        self.ring = [wires.slot() for _ in range(6)]
        self.near = [wires.slot() for _ in range(2 * n)]
        self.gather = Gather(place, wires, self.final_view)

    def span(self, first, count):
        return pl.ds(pl.multiple_of(first * self.rows, 16), count * self.rows)

    def view(self, first, count):
        return self.grads.at[self.seg, :, self.span(first, count)]

    def final_view(self, first, count):
        return self.final.at[self.seg, self.span(first, count)]

    def base(self, step):
        p = self.place
        return (p.k * p.n + lax.rem(p.major + step, p.n)) * p.n

    def add(self, first, count, arrivals):
        kind = BF16 if len(arrivals) == 1 else F32
        size = count * self.rows
        base, chunk = first * self.rows, 96

        def step(i, carry):
            at = pl.ds(pl.multiple_of(base + i * chunk, 16), chunk)
            total = self.grads[self.seg, :, at].astype(kind)
            for ref, start in arrivals:
                here = pl.ds(pl.multiple_of(start * self.rows + i * chunk, 16), chunk)
                total = total + ref[:, here].astype(kind)
            self.grads[self.seg, :, at] = total.astype(BF16)
            return carry

        lax.fori_loop(0, size // chunk, step, 0)

    def to_core(self):
        p, n = self.place, self.place.n
        for step in (2, 1, 3, 0) if n > 1 else (0,):
            block = lax.rem(p.minor + step, n)
            self.wires.send(
                self.core[step],
                self.view(((1 - p.k) * n + block) * n, n),
                self.from_core.at[self.seg, :, self.span(block * n, n)],
                p.sibling(),
            )

    def add_core(self, step):
        p, n = self.place, self.place.n
        block = lax.rem(p.major + step, n)
        landed = self.from_core.at[self.seg, :, self.span(block * n, n)]
        self.wires.arrived(self.core[step], landed, p.sibling())
        self.add(self.base(step), n, [(self.from_core.at[self.seg], block * n)])

    def ring_send(self, piece, first, step):
        self.wires.send(
            self.ring[piece],
            self.view(first, 2),
            self.from_major.at[self.seg, piece],
            self.place.along_major(step),
        )

    def ring_arrived(self, piece, step):
        self.wires.arrived(
            self.ring[piece], self.from_major.at[self.seg, piece], self.place.along_major(step)
        )
        return (self.from_major.at[self.seg, piece], 0)

    def to_major(self):
        if self.place.n == 1:
            self.add_core(0)
            return
        far, after, before = self.base(2), self.base(1), self.base(3)
        self.add_core(2)
        self.ring_send(0, far, 1)
        self.ring_send(1, far + 2, 3)
        self.add_core(1)
        self.ring_send(3, after + 2, 1)
        self.add_core(3)
        self.ring_send(4, before, 3)

    def major_on(self):
        if self.place.n == 1:
            return
        after, before = self.base(1), self.base(3)
        self.add(after, 2, [self.ring_arrived(0, 3)])
        self.ring_send(2, after, 1)
        self.add(before + 2, 2, [self.ring_arrived(1, 1)])
        self.ring_send(5, before + 2, 3)
        self.add_core(0)

    def to_minor(self):
        p, w, n = self.place, self.wires, self.place.n
        row = self.base(0)
        if n > 1:
            second = [self.ring_arrived(3, 3)]
            first = [self.ring_arrived(4, 1)]
            first.append(self.ring_arrived(2, 3))
            self.add(row, 2, first)
            second.append(self.ring_arrived(5, 1))
            self.add(row + 2, 2, second)
        for side in (1, 0):
            half = 1 - p.c if side else p.c
            for step in range(1 - side, n):
                there = p.along_minor(step)
                there["col"] = half
                w.send(
                    self.near[side * n + step],
                    self.grads.at[
                        self.seg, half, self.span(row + lax.rem(p.minor + step, n), 1)
                    ],
                    self.from_minor.at[self.seg, side * n + step],
                    there,
                )

    def to_gather(self):
        p, w, n = self.place, self.wires, self.place.n
        total = self.grads[self.seg, p.c, self.span(p.shard, 1)].astype(F32)
        for side in (0, 1):
            for step in range(1 - side, n):
                landed = self.from_minor.at[self.seg, side * n + step]
                w.arrived(self.near[side * n + step], landed, p.along_minor(step))
                total = total + landed[...].astype(F32)
        self.final[self.seg, self.span(p.shard, 1)] = total.astype(BF16)
        self.gather.minor()


def kernel(
    n,
    x_ref,
    cot_ref,
    step_ref,
    label_ref,
    time_hbm,
    class_hbm,
    modulation_hbm,
    attention_hbm,
    projection_hbm,
    expansion_hbm,
    reduction_hbm,
    modulation_bias_ref,
    projection_bias_ref,
    narrowing_ref,
    attention_bias_ref,
    widening_ref,
    result_ref,
    xgrad_ref,
    final_hbm,
    rows_ref,
    silu_ref,
    condition_grad_ref,
    weights,
    tables_time,
    tables_class,
    modulation,
    ids_out,
    ids_in,
    modp,
    spread_rows,
    silu_out,
    silu_in,
    x_all,
    cot_all,
    mod_parts,
    mod,
    normed1,
    rstd1,
    hidden1,
    triple,
    probs,
    attended,
    send1,
    recv1,
    branch1,
    normed2,
    rstd2,
    hidden2,
    activated,
    slope,
    grad_b2,
    send2,
    recv2,
    grad_up,
    send3,
    recv3,
    grad_res,
    grad_b1,
    grad_att,
    grad_tri,
    send4,
    recv4,
    res_out,
    res_in,
    xg_out,
    xg_low,
    xg_in,
    payload_out,
    payload,
    grads,
    from_core,
    from_major,
    from_minor,
    final,
    send_sems,
    recv_sems,
    local_sems,
):
    place = Place(n)
    wires = Wires(send_sems, recv_sems)
    r, c, k, latent = place.r, place.c, place.k, place.latent

    own = [
        [
            pltpu.make_async_copy(
                attention_hbm.at[kind],
                weights.at[0, c, kind * HALF : (kind + 1) * HALF],
                local_sems.at[kind],
            )
            for kind in range(3)
        ]
        + [
            pltpu.make_async_copy(
                projection_hbm, weights.at[0, c, 3 * HALF : 4 * HALF], local_sems.at[3]
            )
        ],
        [
            pltpu.make_async_copy(
                expansion_hbm.at[:, block * HALF : (block + 1) * HALF],
                weights.at[1, c, block * HALF : (block + 1) * HALF],
                local_sems.at[4 + block],
            )
            for block in range(4)
        ],
        [pltpu.make_async_copy(reduction_hbm, weights.at[2, c], local_sems.at[8])],
    ]
    table_loads = [
        pltpu.make_async_copy(time_hbm, tables_time, local_sems.at[9]),
        pltpu.make_async_copy(class_hbm, tables_class, local_sems.at[10]),
    ]
    modulation_load = pltpu.make_async_copy(modulation_hbm, modulation, local_sems.at[11])
    for copy in own[0] + table_loads + [modulation_load] + own[1] + own[2]:
        copy.start()
    row_at = lax.broadcasted_iota(jnp.int32, (8, 128), 0)
    ids_out[...] = jnp.where(row_at == 0, step_ref[0], label_ref[0])

    barrier = pltpu.get_barrier_semaphore()
    others = [place.group(s) for s in (1, 2, 3)] + [place.sibling()]
    for step in range(1, n):
        others += [place.along_minor(step), place.along_major(step)]
        there = place.along_minor(step)
        there["col"] = 1 - c
        others.append(there)
    for other in others:
        pl.semaphore_signal(barrier, inc=1, device_id=other, device_id_type=MESH)
    pl.semaphore_wait(barrier, len(others))

    shard_rows = SEG // (2 * n * n)

    def weight_view(seg):
        def view(first, count):
            start = pl.multiple_of(first * shard_rows, 16)
            return weights.at[seg, 1 - c, pl.ds(start, count * shard_rows)]

        return view

    gathers = [Gather(place, wires, weight_view(seg)) for seg in range(3)]
    weight_slots = [wires.slot() for _ in range(3)]
    my_rows = pl.ds(pl.multiple_of(place.shard * shard_rows, 16), shard_rows)

    def weights_out(seg):
        for copy in own[seg]:
            copy.wait()
        mine = weights.at[seg, c, my_rows]
        wires.send(weight_slots[seg], mine, mine, place.column())

    def weights_minor(seg):
        wires.arrived(weight_slots[seg], weights.at[seg, 1 - c, my_rows], place.column())
        gathers[seg].minor()

    weights_out(0)
    ids_slot = wires.slot()
    wires.send(ids_slot, ids_out, ids_in, place.column())
    x_spread = Spread(place, wires, x_ref, x_all)
    weights_out(1)
    weights_out(2)

    def table_rows(steps, labels, count):
        lanes = lax.broadcasted_iota(jnp.int32, (count, STEPS), 1)
        class_lanes = lax.broadcasted_iota(jnp.int32, (count, CLASSES), 1)
        return dot((lanes == steps).astype(BF16), tables_time[...]) + dot(
            (class_lanes == labels).astype(BF16), tables_class[...]
        )

    weights_minor(0)
    wires.arrived(ids_slot, ids_in, place.column())
    x_spread.forward()
    latent_at = lax.broadcasted_iota(jnp.int32, (16, 1), 0)

    def by_latent(row):
        return jnp.where(
            latent_at == c,
            ids_out[row : row + 1, 0:1],
            jnp.where(latent_at == 1 - c, ids_in[row : row + 1, 0:1], -1),
        )

    for copy in table_loads:
        copy.wait()
    modulation_load.wait()
    group_condition = table_rows(by_latent(0), by_latent(1), 16)
    group_silu = (group_condition / (1.0 + jnp.exp(-group_condition))).astype(BF16)
    first_row = (r == 0).astype(F32)
    modulation_bias = modulation_bias_ref[...].astype(F32)
    for kind in range(6):
        part = dot(group_silu, modulation[kind])
        for lat in range(2):
            modp[lat, kind : kind + 1, :] = (
                part[lat : lat + 1, :] + first_row * modulation_bias[kind : kind + 1, :]
            )
    for lat in range(2):
        modp[lat, 6:7, :] = first_row * projection_bias_ref[...].astype(F32).reshape(1, HALF)
        modp[lat, 7:8, :] = first_row * narrowing_ref[...].astype(F32).reshape(1, HALF)
    mod_slots = [wires.slot() for _ in range(3)]
    for step in (1, 2, 3):
        there = place.group(step)
        its_latent = xor(there["col"], k * there["row"])
        wires.send(mod_slots[step - 1], modp.at[its_latent], mod_parts.at[step], there)

    gathers[0].major()
    weights_minor(1)
    for step in (1, 2, 3):
        wires.arrived(mod_slots[step - 1], mod_parts.at[step], place.group(step))
    mod[c] = modp[latent] + mod_parts[1]
    mod[1 - c] = mod_parts[2] + mod_parts[3]

    def vec(half, row):
        return mod[half, row : row + 1, :]

    def over_rows(body, init=0, part=None):
        def step(i, carry):
            return body(pl.ds(pl.multiple_of(i * ROWS, ROWS), ROWS), carry)

        steps = SEQ // ROWS
        first, last = (0, steps) if part is None else (part * steps // 2, (part + 1) * steps // 2)
        return lax.fori_loop(first, last, step, init)

    def part_rows(part):
        return pl.ds(part * PART, PART)

    def norm(values):
        average = (
            jnp.sum(values[0], axis=-1, keepdims=True) + jnp.sum(values[1], axis=-1, keepdims=True)
        ) * (1.0 / D)
        square = (
            jnp.sum(values[0] * values[0], axis=-1, keepdims=True)
            + jnp.sum(values[1] * values[1], axis=-1, keepdims=True)
        ) * (1.0 / D)
        inverse = lax.rsqrt(square - average * average + EPSILON)
        return [(v - average) * inverse for v in values], inverse

    def norm_back(grad, normed, inverse):
        average = (
            jnp.sum(grad[0], axis=-1, keepdims=True) + jnp.sum(grad[1], axis=-1, keepdims=True)
        ) * (1.0 / D)
        crossed = (
            jnp.sum(grad[0] * normed[0], axis=-1, keepdims=True)
            + jnp.sum(grad[1] * normed[1], axis=-1, keepdims=True)
        ) * (1.0 / D)
        return [inverse * (g - average - m * crossed) for g, m in zip(grad, normed)]

    def token_sum(v):
        return jnp.sum(v, axis=0, keepdims=True)

    gathers[0].major_on()
    x_spread.collect()
    cot_spread = Spread(place, wires, cot_ref, cot_all)

    def first_norm(rows, carry):
        normed, inverse = norm([x_all[h, rows].astype(F32) for h in range(2)])
        rstd1[rows] = inverse
        for h in range(2):
            normed1[h, rows] = normed[h]
            hidden1[h, rows] = (normed[h] * (1.0 + vec(h, 1)) + vec(h, 0)).astype(BF16)
        return carry

    weights_minor(2)
    over_rows(first_norm)
    gathers[0].cores()

    def weight(seg, half, block):
        return weights[seg, half, block * HALF : (block + 1) * HALF, :]

    for kind in range(3):
        slope[kind] = dot(hidden1[c], weight(0, c, kind))
    cot_spread.forward()
    gathers[1].major()
    gathers[0].finish()
    gathers[2].major()
    for kind in range(3):
        value = slope[kind] + dot(hidden1[1 - c], weight(0, 1 - c, kind))
        if kind != 1:
            value = value + attention_bias_ref[kind // 2 : kind // 2 + 1, :].astype(F32)
        triple[kind] = value.astype(BF16)
    gathers[1].major_on()

    low_lanes = lax.broadcasted_iota(jnp.int32, (SEQ, 128), 1) < HEAD_DIM

    def one_head(v, head):
        mask = low_lanes if head == 0 else jnp.logical_not(low_lanes)
        return jnp.where(mask, v, jnp.zeros_like(v))

    score_scale = HEAD_DIM ** (-0.5)

    def attend(pair):
        lanes = pl.ds(pair * 128, 128)
        query = triple[0, :, lanes] * BF16(score_scale)
        keys = triple[1, :, lanes]
        values = triple[2, :, lanes]
        mixed = []
        for head in range(2):
            scores = dot_nt(one_head(query, head), keys)
            exponent = jnp.exp(scores - jnp.max(scores, axis=-1, keepdims=True))
            total = jnp.sum(exponent, axis=-1, keepdims=True)
            weights_now = exponent * (1.0 / total)
            probs[2 * pair + head] = weights_now
            mixed.append(dot(weights_now.astype(BF16), values))
        attended[:, lanes] = jnp.where(low_lanes, mixed[0], mixed[1]).astype(BF16)

    attend(0)
    gathers[2].major_on()
    attend(1)
    gathers[1].cores()
    attend(2)
    gathers[2].cores()

    def exchange(part, out, landing, slots):
        rows = part_rows(part)
        wires.send(slots[part], out.at[:, rows], landing.at[:, rows], place.partner())

    def exchanged(part, landing, slots):
        wires.arrived(slots[part], landing.at[:, part_rows(part)], place.partner())

    slots1, slots2, slots3, slots4 = ([wires.slot() for _ in range(2)] for _ in range(4))
    for part in range(2):
        rows = part_rows(part)
        for half in range(2):
            send1[half, rows] = dot(attended[rows, :], weight(0, half, 3)).astype(BF16)
        exchange(part, send1, recv1, slots1)
    cot_spread.collect()
    zero = jnp.zeros((1, HALF), F32)

    def start_back(rows, carry):
        out = []
        for h in range(2):
            low = (cot_all[h, rows].astype(F32) * vec(h, 5)).astype(BF16)
            grad_b2[h, rows] = low
            out.append(carry[h] + token_sum(low.astype(F32)))
        return tuple(out)

    narrowing_sum = over_rows(start_back, (zero, zero))

    def second_norm(rows, carry):
        middle = []
        for h in range(2):
            branch = send1[h, rows].astype(F32) + recv1[h, rows].astype(F32) + vec(h, 6)
            branch1[h, rows] = branch
            middle.append(x_all[h, rows].astype(F32) + vec(h, 2) * branch)
        normed, inverse = norm(middle)
        rstd2[rows] = inverse
        for h in range(2):
            normed2[h, rows] = normed[h]
            hidden2[h, rows] = (normed[h] * (1.0 + vec(h, 4)) + vec(h, 3)).astype(BF16)
        return carry

    reduces = [
        Reduce(place, wires, seg, grads, from_core, from_major, from_minor, final)
        for seg in range(3)
    ]

    def keep_grad(seg, half, block, value):
        grads[seg, half, block * HALF : (block + 1) * HALF, :] = value.astype(BF16)

    root = math.sqrt(2.0 / math.pi)
    widening_sum = [zero] * 4
    for part in range(2):
        rows = part_rows(part)
        exchanged(part, recv1, slots1)
        over_rows(second_norm, part=part)
        if part == 0:
            gathers[1].finish()
        for block in range(4):
            upper = dot(hidden2[0, rows], weight(1, 0, block)) + dot(
                hidden2[1, rows], weight(1, 1, block)
            )
            bias = widening_ref[block * HALF : (block + 1) * HALF].astype(F32)
            upper = upper + bias.reshape(1, HALF)
            squared = upper * upper
            bent = jnp.tanh(root * upper * (1.0 + 0.044715 * squared))
            half_up = 0.5 * (1.0 + bent)
            activated[block, rows] = (upper * half_up).astype(BF16)
            slope[block, rows] = half_up + (0.5 * root) * upper * (1.0 - bent * bent) * (
                1.0 + (3.0 * 0.044715) * squared
            )
        if part == 0:
            gathers[2].finish()
        else:
            for block in range(4):
                for half in range(2):
                    keep_grad(2, half, block, dot_tn(activated[block], grad_b2[half]))
            reduces[2].to_core()
        for block in range(4):
            back = dot_nt(grad_b2[0, rows], weight(2, 0, block)) + dot_nt(
                grad_b2[1, rows], weight(2, 1, block)
            )
            low = (back * slope[block, rows]).astype(BF16)
            grad_up[block, rows] = low
            widening_sum[block] = widening_sum[block] + token_sum(low.astype(F32))
        for half in range(2):
            value = dot_nt(grad_up[0, rows], weight(1, half, 0))
            for block in range(1, 4):
                value = value + dot_nt(grad_up[block, rows], weight(1, half, block))
            send3[half, rows] = value.astype(BF16)
        exchange(part, send3, recv3, slots3)

    for block in range(4):
        for half in range(2):
            keep_grad(1, half, block, dot_tn(hidden2[half], grad_up[block]))
    reduces[1].to_core()
    reduces[2].to_major()
    for part in range(2):
        rows = part_rows(part)
        for half in range(2):
            value = dot(activated[0, rows], weight(2, half, 0))
            for block in range(1, 4):
                value = value + dot(activated[block, rows], weight(2, half, block))
            send2[half, rows] = value.astype(BF16)
        exchange(part, send2, recv2, slots2)

    def second_back(rows, carry):
        shift, scale, gate, bias = (list(part) for part in carry)
        inverse = rstd2[rows]
        normed = [normed2[h, rows] for h in range(2)]
        scaled = []
        for h in range(2):
            grad = send3[h, rows].astype(F32) + recv3[h, rows].astype(F32)
            shift[h] = shift[h] + token_sum(grad)
            scale[h] = scale[h] + token_sum(grad * normed[h])
            scaled.append(grad * (1.0 + vec(h, 4)))
        back = norm_back(scaled, normed, inverse)
        for h in range(2):
            total = cot_all[h, rows].astype(F32) + back[h]
            grad_res[h, rows] = total
            gate[h] = gate[h] + token_sum(total * branch1[h, rows])
            low = (total * vec(h, 2)).astype(BF16)
            grad_b1[h, rows] = low
            bias[h] = bias[h] + token_sum(low.astype(F32))
        return tuple(shift), tuple(scale), tuple(gate), tuple(bias)

    pair_zero = (zero, zero)
    sums2 = (pair_zero,) * 4
    for part in range(2):
        rows = part_rows(part)
        exchanged(part, recv3, slots3)
        sums2 = over_rows(second_back, sums2, part)
        grad_att[rows, :] = (
            dot_nt(grad_b1[0, rows], weight(0, 0, 3)) + dot_nt(grad_b1[1, rows], weight(0, 1, 3))
        ).astype(BF16)
    shift2, scale2, gate1, projection_sum = sums2
    for half in range(2):
        keep_grad(0, half, 3, dot_tn(attended[...], grad_b1[half]))

    def attend_back(pair):
        lanes = pl.ds(pair * 128, 128)
        query = triple[0, :, lanes] * BF16(score_scale)
        keys = triple[1, :, lanes]
        values = triple[2, :, lanes]
        above = grad_att[:, lanes]
        by_query, by_keys, by_values = [], [], []
        for head in range(2):
            weights_now = probs[2 * pair + head]
            grad_probs = dot_nt(one_head(above, head), values)
            by_values.append(dot_tn(weights_now.astype(BF16), above))
            crossed = jnp.sum(grad_probs * weights_now, axis=-1, keepdims=True)
            low = (weights_now * (grad_probs - crossed)).astype(BF16)
            by_query.append(dot(low, keys) * score_scale)
            by_keys.append(dot_tn(low, query))
        for kind, parts in enumerate((by_query, by_keys, by_values)):
            grad_tri[kind, :, lanes] = jnp.where(low_lanes, parts[0], parts[1]).astype(BF16)

    reduces[2].major_on()
    attend_back(0)
    reduces[1].to_major()
    exchanged(0, recv2, slots2)
    exchanged(1, recv2, slots2)
    mine = r == latent
    self_col = xor(latent, k * latent)
    out_half = c * (r == latent).astype(jnp.int32) + (1 - self_col) * (r != latent).astype(jnp.int32)
    across = place.at(row=latent, col=1 - self_col)
    back_from = place.at(row=1 - r, col=xor(r, k * (1 - r)))

    def branch_end(rows, carry):
        gate = list(carry)
        for h in range(2):
            branch = send2[h, rows].astype(F32) + recv2[h, rows].astype(F32) + vec(h, 7)
            gate[h] = gate[h] + token_sum(cot_all[h, rows].astype(F32) * branch)
            middle = x_all[h, rows].astype(F32) + vec(h, 2) * branch1[h, rows]
            res_out[h, rows] = (middle + vec(h, 5) * branch).astype(BF16)
        return tuple(gate)

    gate2 = over_rows(branch_end, pair_zero)
    res_slot, xg_slot = wires.slot(), wires.slot()

    @pl.when(jnp.logical_not(mine))
    def _():
        wires.copy(res_slot, res_out.at[out_half], res_in, across).start()

    attend_back(1)
    reduces[2].to_minor()
    attend_back(2)
    reduces[1].major_on()
    for half in range(2):
        for kind in range(3):
            keep_grad(0, half, kind, dot_tn(hidden1[half], grad_tri[kind]))
    reduces[0].to_core()
    for part in range(2):
        rows = part_rows(part)
        for half in range(2):
            value = dot_nt(grad_tri[0, rows], weight(0, half, 0))
            for kind in range(1, 3):
                value = value + dot_nt(grad_tri[kind, rows], weight(0, half, kind))
            send4[half, rows] = value.astype(BF16)
        exchange(part, send4, recv4, slots4)
    reduces[2].to_gather()
    reduces[1].to_minor()
    reduces[0].to_major()
    reduces[2].gather.major()

    def first_back(rows, carry):
        shift, scale = (list(part) for part in carry)
        inverse = rstd1[rows]
        normed = [normed1[h, rows] for h in range(2)]
        scaled = []
        for h in range(2):
            grad = send4[h, rows].astype(F32) + recv4[h, rows].astype(F32)
            shift[h] = shift[h] + token_sum(grad)
            scale[h] = scale[h] + token_sum(grad * normed[h])
            scaled.append(grad * (1.0 + vec(h, 1)))
        back = norm_back(scaled, normed, inverse)
        for h in range(2):
            total = grad_res[h, rows] + back[h]
            xg_out[h, rows] = total
            xg_low[h, rows] = total.astype(BF16)
        return tuple(shift), tuple(scale)

    sums1 = (pair_zero,) * 2
    for part in range(2):
        exchanged(part, recv4, slots4)
        sums1 = over_rows(first_back, sums1, part)
        if part == 0:
            reduces[0].major_on()
    shift1, scale1 = sums1

    def sums(kind):
        return token_sum(grad_tri[kind].astype(F32))

    shared = [sums(0), sums(2)] + widening_sum
    digit = lax.broadcasted_iota(jnp.int32, (1, HALF), 1) < 128
    for row in range(2):
        picked = jnp.where(latent == c, ids_out[row : row + 1, 0:1], ids_in[row : row + 1, 0:1])
        high = lax.shift_right_logical(picked, 5)
        shared.append(jnp.where(digit, high, picked - 32 * high).astype(F32))
    for h in range(2):
        own_rows = [shift1[h], scale1[h], gate1[h], shift2[h], scale2[h], gate2[h]]
        own_rows += [projection_sum[h], narrowing_sum[h]]
        payload_out[h] = jnp.concatenate(own_rows + shared, axis=0).astype(BF16)
    payload_slot = wires.slot()
    spot = 2 * place.shard + latent
    wires.send(payload_slot, payload_out.at[1 - c], payload.at[spot], place.column())
    payload[spot] = payload_out[c]

    def payload_view(first, count):
        return payload.at[pl.ds(2 * first, 2 * count)]

    payloads = Gather(place, wires, payload_view)
    reduces[0].to_minor()
    wires.arrived(payload_slot, payload.at[2 * place.shard + 1 - latent], place.column())
    payloads.minor()

    @pl.when(jnp.logical_not(mine))
    def _():
        wires.copy(xg_slot, xg_low.at[out_half], xg_in, across).start()

    reduces[1].to_gather()
    reduces[2].gather.major_on()
    payloads.major()
    reduces[0].to_gather()
    payloads.major_on()
    reduces[1].gather.major()
    reduces[2].gather.cores()
    reduces[0].gather.major()
    payloads.cores()
    reduces[1].gather.major_on()
    reduces[0].gather.major_on()
    payloads.finish()

    count = 4 * n * n
    for lat in range(count):
        for part in range(3):
            spread_rows[part, pl.ds(16 * lat, 16), :] = payload[
                lat, :, part * 128 : (part + 1) * 128
            ].astype(F32)
    for kind in range(16):
        for part in range(3):
            rows_ref[kind, :, part * 128 : (part + 1) * 128] = spread_rows[
                part, pl.ds(kind, count, stride=16), :
            ].astype(BF16)
    reduces[1].gather.cores()
    reduces[0].gather.cores()
    value = dot_nt(rows_ref[0], modulation[0])
    for kind in range(1, 6):
        value = value + dot_nt(rows_ref[kind], modulation[kind])
    silu_out[...] = value
    silu_slot = wires.slot()
    wires.send(silu_slot, silu_out, silu_in, place.column())

    reduces[2].gather.finish()
    outs = [
        pltpu.make_async_copy(final.at[seg], final_hbm.at[seg], local_sems.at[12 + seg])
        for seg in range(3)
    ]
    outs[2].start()

    def decode(kind):
        both = rows_ref[kind].astype(F32)
        return (32.0 * both[:, 0:1] + both[:, 128:129]).astype(jnp.int32)

    condition = table_rows(decode(14), decode(15), count)
    sigmoid = 1.0 / (1.0 + jnp.exp(-condition))
    silu_ref[...] = (condition * sigmoid).astype(BF16)
    reduces[1].gather.finish()
    outs[1].start()
    reduces[0].gather.finish()
    outs[0].start()
    wires.arrived(silu_slot, silu_in, place.column())
    condition_grad_ref[...] = (silu_out[...] + silu_in[...]) * (
        sigmoid * (1.0 + condition * (1.0 - sigmoid))
    )

    @pl.when(mine)
    def _():
        result_ref[...] = res_out[out_half]
        xgrad_ref[...] = xg_out[out_half]

    @pl.when(jnp.logical_not(mine))
    def _():
        wires.copy(res_slot, res_out.at[out_half], res_in, across).wait_send()
        wires.copy(res_slot, res_out.at[out_half], res_in, back_from).wait_recv()
        wires.copy(xg_slot, xg_low.at[out_half], xg_in, across).wait_send()
        wires.copy(xg_slot, xg_low.at[out_half], xg_in, back_from).wait_recv()
        result_ref[...] = res_in[...]
        xgrad_ref[...] = xg_in[...].astype(F32)

    x_spread.sent()
    cot_spread.sent()
    wires.drain()
    for out in outs:
        out.wait()


class Spread:
    def __init__(self, place, wires, source, landing):
        self.place, self.wires, self.landing = place, wires, landing
        r, c, k, latent = place.r, place.c, place.k, place.latent
        self.mine = r == latent
        self.far = 1 - xor(latent, k * latent)
        self.first, _, self.last = [wires.slot() for _ in range(3)]
        self.out = self.copy(
            source, c, self.first, self.first + c, place.at(row=1 - r, col=xor(r, k * (1 - r)))
        )
        self.forwarded = self.copy(
            landing.at[self.far], self.far, self.last, self.last, place.partner()
        )
        self.out.start()

        @pl.when(self.mine)
        def _():
            landing[c] = source[...]

    def copy(self, source, half, send_slot, recv_slot, there):
        return pltpu.make_async_remote_copy(
            src_ref=source,
            dst_ref=self.landing.at[half],
            send_sem=self.wires.send_sems.at[send_slot],
            recv_sem=self.wires.recv_sems.at[recv_slot],
            device_id=there,
            device_id_type=MESH,
        )

    def arrived(self, half, slot):
        self.copy(self.landing.at[half], half, self.last, slot, self.place.partner()).wait_recv()

    def forward(self):
        @pl.when(jnp.logical_not(self.mine))
        def _():
            self.arrived(self.far, self.first + self.far)
            self.forwarded.start()

    def collect(self):
        @pl.when(self.mine)
        def _():
            self.arrived(self.far, self.last)

        @pl.when(jnp.logical_not(self.mine))
        def _():
            self.arrived(1 - self.far, self.first + 1 - self.far)

    def sent(self):
        self.out.wait_send()

        @pl.when(jnp.logical_not(self.mine))
        def _():
            self.forwarded.wait_send()


def whole(shape, dtype):
    return pltpu.VMEM(shape, dtype)


def run_block(n, *operands):
    shards = 2 * n * n
    rows = SEG // shards
    tokens = (2, SEQ, HALF)
    vmem = pl.BlockSpec(memory_space=pltpu.VMEM)
    hbm = pl.BlockSpec(memory_space=pl.ANY)
    smem = pl.BlockSpec(memory_space=pltpu.SMEM)
    scratch = [
        whole((3, 2, SEG, HALF), BF16),
        whole((STEPS, HALF), BF16),
        whole((CLASSES, HALF), BF16),
        whole((6, HALF, HALF), BF16),
        whole((8, 128), jnp.int32),
        whole((8, 128), jnp.int32),
        whole((2, 8, HALF), F32),
        whole((3, 32 * shards, 128), F32),
        whole((2 * shards, HALF), F32),
        whole((2 * shards, HALF), F32),
        whole(tokens, BF16),
        whole(tokens, BF16),
        whole((4, 8, HALF), F32),
        whole((2, 8, HALF), F32),
        whole(tokens, F32),
        whole((SEQ, 1), F32),
        whole(tokens, BF16),
        whole((3, SEQ, HALF), BF16),
        whole((6, SEQ, SEQ), F32),
        whole((SEQ, HALF), BF16),
        whole(tokens, BF16),
        whole(tokens, BF16),
        whole(tokens, F32),
        whole(tokens, F32),
        whole((SEQ, 1), F32),
        whole(tokens, BF16),
        whole((4, SEQ, HALF), BF16),
        whole((4, SEQ, HALF), F32),
        whole(tokens, BF16),
        whole(tokens, BF16),
        whole(tokens, BF16),
        whole((4, SEQ, HALF), BF16),
        whole(tokens, BF16),
        whole(tokens, BF16),
        whole(tokens, F32),
        whole(tokens, BF16),
        whole((SEQ, HALF), BF16),
        whole((3, SEQ, HALF), BF16),
        whole(tokens, BF16),
        whole(tokens, BF16),
        whole(tokens, BF16),
        whole((SEQ, HALF), BF16),
        whole(tokens, F32),
        whole(tokens, BF16),
        whole((SEQ, HALF), BF16),
        whole((2, 16, HALF), BF16),
        whole((2 * shards, 16, HALF), BF16),
        whole((3, 2, SEG, HALF), BF16),
        whole((3, 2, SEG // 2, HALF), BF16),
        whole((3, 6, 2, 2 * rows, HALF), BF16),
        whole((3, 2 * n, rows, HALF), BF16),
        whole((3, SEG, HALF), BF16),
        pltpu.SemaphoreType.DMA((SEMS,)),
        pltpu.SemaphoreType.DMA((SEMS,)),
        pltpu.SemaphoreType.DMA((16,)),
    ]

    def body(*refs):
        kernel(n, *refs)

    return pl.pallas_call(
        body,
        out_shape=(
            jax.ShapeDtypeStruct((SEQ, HALF), BF16),
            jax.ShapeDtypeStruct((SEQ, HALF), F32),
            jax.ShapeDtypeStruct((3, SEG, HALF), BF16),
            jax.ShapeDtypeStruct((16, 2 * shards, HALF), BF16),
            jax.ShapeDtypeStruct((2 * shards, HALF), BF16),
            jax.ShapeDtypeStruct((2 * shards, HALF), F32),
        ),
        in_specs=[vmem, vmem, smem, smem] + [hbm] * 7 + [vmem] * 5,
        out_specs=(vmem, vmem, hbm, vmem, vmem, vmem),
        scratch_shapes=scratch,
        compiler_params=pltpu.CompilerParams(
            collective_id=0, has_side_effects=True, vmem_limit_bytes=60 * 1024 * 1024
        ),
        name="block",
    )(*operands)


def finish_kernel(
    result_in,
    xgrad_in,
    final_hbm,
    rows_ref,
    silu_ref,
    condition_grad_ref,
    result_ref,
    xgrad_ref,
    time_hbm,
    class_hbm,
    modulation_hbm,
    modulation_bias_ref,
    attention_hbm,
    attention_bias_ref,
    projection_hbm,
    projection_bias_ref,
    expansion_hbm,
    widening_ref,
    reduction_hbm,
    narrowing_ref,
    final,
    time_grad,
    class_grad,
    modulation_grad,
    wide,
    sems,
):
    loads = [
        [
            pltpu.make_async_copy(
                final_hbm.at[seg, pl.ds(block * HALF, HALF)],
                final.at[seg, pl.ds(block * HALF, HALF)],
                sems.at[24 + 4 * seg + block],
            )
            for block in range(4)
        ]
        for seg in range(3)
    ]
    for seg in (2, 1, 0):
        for load in loads[seg]:
            load.start()
    stores = []

    def store(source, target):
        copy = pltpu.make_async_copy(source, target, sems.at[3 + len(stores)])
        copy.start()
        stores.append(copy)

    result_ref[...] = result_in[...]
    xgrad_ref[...] = xgrad_in[...]
    silu = silu_ref[...].T
    for kind in range(6):
        modulation_grad[kind] = dot(silu, rows_ref[kind])
        store(modulation_grad.at[kind], modulation_hbm.at[kind])

    def widen(seg, block):
        loads[seg][block].wait()
        at = pl.ds(block * HALF, HALF)
        wide[seg, at] = final[seg, at].astype(F32)
        return wide.at[seg, at]

    for block in range(4):
        store(widen(2, block), reduction_hbm.at[pl.ds(block * HALF, HALF)])
    for block in range(4):
        store(widen(1, block), expansion_hbm.at[:, pl.ds(block * HALF, HALF)])
    for block in range(3):
        store(widen(0, block), attention_hbm.at[block])
    store(widen(0, 3), projection_hbm)

    count = silu_ref.shape[0]
    grad = condition_grad_ref[...]
    high = grad.astype(BF16)
    rest = grad - high.astype(F32)
    middle = rest.astype(BF16)
    low = (rest - middle.astype(F32)).astype(BF16)

    def scatter(kind, size):
        both = rows_ref[kind].astype(F32)
        picked = (32.0 * both[:, 0:1] + both[:, 128:129]).astype(jnp.int32)
        onehot = (lax.broadcasted_iota(jnp.int32, (count, 1024), 1) == picked).astype(BF16)
        onehot = onehot.T
        return (dot(onehot, high) + dot(onehot, middle) + dot(onehot, low))[:size]

    time_grad[...] = scatter(14, STEPS)
    store(time_grad, time_hbm)
    class_grad[...] = scatter(15, CLASSES)
    store(class_grad, class_hbm)

    def total(kind):
        return jnp.sum(rows_ref[kind].astype(F32), axis=0, keepdims=True)

    for kind in range(6):
        modulation_bias_ref[kind : kind + 1, :] = total(kind)
    projection_bias_ref[...] = total(6).reshape(HALF)
    narrowing_ref[...] = total(7).reshape(HALF)
    for kind in range(2):
        attention_bias_ref[kind : kind + 1, :] = total(8 + kind)
    for block in range(4):
        widening_ref[block * HALF : (block + 1) * HALF] = total(10 + block).reshape(HALF)
    for copy in stores:
        copy.wait()


def finish(result, xgrad, final, rows, silu, condition_grad):
    vmem = pl.BlockSpec(memory_space=pltpu.VMEM)
    hbm = pl.BlockSpec(memory_space=pl.ANY)
    shapes = [
        ((SEQ, HALF), vmem),
        ((SEQ, HALF), vmem),
        ((STEPS, HALF), hbm),
        ((CLASSES, HALF), hbm),
        ((6, HALF, HALF), hbm),
        ((6, HALF), vmem),
        ((3, HALF, HALF), hbm),
        ((2, HALF), vmem),
        ((HALF, HALF), hbm),
        ((HALF,), vmem),
        ((HALF, SEG), hbm),
        ((SEG,), vmem),
        ((SEG, HALF), hbm),
        ((HALF,), vmem),
    ]
    return pl.pallas_call(
        finish_kernel,
        out_shape=tuple(
            jax.ShapeDtypeStruct(shape, BF16 if i == 0 else F32)
            for i, (shape, _) in enumerate(shapes)
        ),
        in_specs=[vmem, vmem, hbm, vmem, vmem, vmem],
        out_specs=tuple(spec for _, spec in shapes),
        scratch_shapes=[
            whole((3, SEG, HALF), BF16),
            whole((STEPS, HALF), F32),
            whole((CLASSES, HALF), F32),
            whole((6, HALF, HALF), F32),
            whole((3, SEG, HALF), F32),
            pltpu.SemaphoreType.DMA((40,)),
        ],
        compiler_params=pltpu.CompilerParams(vmem_limit_bytes=60 * 1024 * 1024),
        name="finish",
    )(result, xgrad, final, rows, silu, condition_grad)


def body(
    activations,
    timesteps,
    class_labels,
    time_table,
    class_table,
    modulation,
    modulation_bias,
    attention,
    attention_bias,
    projection,
    projection_bias,
    expansion,
    widening_bias,
    reduction,
    narrowing_bias,
    cotangent,
):
    n = math.isqrt(lax.axis_size("dp") // 2)
    result, activations_grad, final, rows, silu, condition_grad = run_block(
        n,
        activations,
        cotangent,
        timesteps,
        class_labels,
        time_table,
        class_table,
        jnp.swapaxes(modulation, 0, 1),
        jnp.swapaxes(attention, 0, 1),
        projection,
        expansion,
        reduction,
        modulation_bias,
        projection_bias,
        narrowing_bias,
        attention_bias,
        widening_bias,
    )
    (
        result,
        activations_grad,
        time_grad,
        class_grad,
        modulation_grad,
        modulation_bias_grad,
        attention_grad,
        attention_bias_grad,
        projection_grad,
        projection_bias_grad,
        expansion_grad,
        expansion_bias_grad,
        reduction_grad,
        reduction_bias_grad,
    ) = finish(result, activations_grad, final, rows, silu, condition_grad)
    return (
        result,
        activations_grad,
        time_grad,
        class_grad,
        jnp.swapaxes(modulation_grad, 0, 1),
        modulation_bias_grad,
        jnp.swapaxes(attention_grad, 0, 1),
        attention_bias_grad,
        projection_grad,
        projection_bias_grad,
        expansion_grad,
        expansion_bias_grad,
        reduction_grad,
        reduction_bias_grad,
    )


def solution(mesh):
    placed = (
        P(("dp", "row"), "col"),
        P(("dp", "col")),
        P(("dp", "col")),
        P(None, "row"),
        P(None, "row"),
        P("row", None, "col"),
        P(None, "col"),
        P("col", None, "row"),
        P(None, "row"),
        P("row", "col"),
        P("col"),
        P("col", "row"),
        P("row"),
        P("row", "col"),
        P("col"),
        P(("dp", "row"), "col"),
    )
    return jax.shard_map(
        body,
        mesh=mesh,
        in_specs=placed,
        out_specs=(
            P(("dp", "row"), "col"),
            P(("dp", "row"), "col"),
            P(None, "row"),
            P(None, "row"),
            P("row", None, "col"),
            P(None, "col"),
            P("col", None, "row"),
            P(None, "row"),
            P("row", "col"),
            P("col"),
            P("col", "row"),
            P("row"),
            P("row", "col"),
            P("col"),
        ),
        check_vma=False,
    )
```
